32 devices in a mesh: leaf: 8 (over z, y), front: 4 (over x, core).
Axes of the slice: x: 2, y: 2, z: 4, core: 2. Of those that a mesh axis runs over, the one named last changes fastest.
Arguments:
- leaf_fronts: float32 [8, 1024, 1024], P('leaf', 'front')
- coupling_cols: int32 [8, 4, 224, 128], P('leaf', 'front'), may hold values from 0 to 1023, as said below
- coupling_vals: float32 [8, 4, 224, 128], P('leaf', 'front'), may hold values from -0.1 to 0.1
- sep_diag: float32 [8, 4, 224], P('leaf', 'front'), may hold values from 1 to 3
- child_maps: int32 [14, 512], replicated, may hold values from 0 to 1023, as said below
Outputs:
- factors: float32 [8, 4, 480, 512], P('leaf', 'front')
- log_det: float32 [], replicated
The draws below stay inside these ranges and needn't reach their ends.
Inputs may be any that keep to these rules, and one draw needn't show every extreme that they name: `coupling_cols`: each coupling column is at most the index, in its front, of the row that holds it, so every entry lies on or below the diagonal. `child_maps`: the 512 entries of each row are distinct.
All inputs are finite; a program needn't handle non-finite values.
Results may differ from the reference program's by a relative error of at most 0.0001.
Values sent between devices are 32-bit elements; how exact they have to be, the bound alone decides.
No kernel may reach another device: no remote copies, remote signals or barrier semaphores. Data moves between devices by JAX's collectives and lax.ppermute only.
A program may use at most 128 MiB of HBM per device.

```python
import math
import jax
import jax.numpy as jnp
import numpy as np
from jax import lax

SEP = 512
BND = 512
KC = 128
LEVELS = 4
RT = 224
RALL = 480
N_LEAF = 8
N_FRONT = 4


def coupling_rows():
    row_list = []
    for level_no in range(1, LEVELS):
        size_rows = (SEP + BND) // (N_FRONT * 2 ** level_no)
        leaf_ids = np.arange(N_LEAF)[:, None, None]
        front_ids = np.arange(N_FRONT)[None, :, None]
        local_ids = np.arange(size_rows)[None, None, :]
        group_rank = leaf_ids % 2 ** level_no * N_FRONT + front_ids
        row_list.append(np.broadcast_to(group_rank * size_rows + local_ids, (N_LEAF, N_FRONT, size_rows)))
    return np.concatenate(row_list, axis=2).astype(np.int32)


def draw_coupling_cols(key, part):
    upper_ids = jnp.asarray(coupling_rows())[..., None] + 1
    upper_ids = jnp.broadcast_to(upper_ids, (N_LEAF, N_FRONT, RT, KC))
    return jax.random.randint(key, (N_LEAF, N_FRONT, RT, KC), 0, upper_ids, dtype=jnp.int32)


def draw_child_maps(key, part):
    key_list = jax.random.split(jax.random.fold_in(key, 7), 2 * N_LEAF - 2)
    return jax.vmap(lambda one_key: jax.random.permutation(one_key, SEP + BND)[:BND])(key_list).astype(jnp.int32)


def draw_leaf_fronts(key, part):
    width_all = SEP + BND
    key_off, key_diag = jax.random.split(jax.random.fold_in(key, 11))
    shape_all = (N_LEAF, width_all, width_all)
    spread = 0.8 / math.sqrt(width_all)
    entries = jnp.clip(jax.random.normal(key_off, shape_all, jnp.float32), -4.0, 4.0) * spread
    diag_vals = jax.random.uniform(key_diag, (N_LEAF, width_all), jnp.float32, 2.5, 4.0)
    row_grid = lax_iota_rows(width_all)
    identity = row_grid == row_grid.T
    return jnp.where(identity[None], diag_vals[:, :, None], entries)


def lax_iota_rows(width_all):
    return jnp.broadcast_to(jnp.arange(width_all, dtype=jnp.int32)[:, None], (width_all, width_all))


def steps_of(key, dims, cuts, least, top_value):
    factor_of = 1.0
    for axis_at, blocks in cuts:
        draws = jax.random.uniform(jax.random.fold_in(jax.random.fold_in(key, 6), axis_at), (blocks,), jnp.float32, least / len(cuts), top_value / len(cuts))
        factor_of = factor_of * jnp.repeat(jnp.exp(draws), dims[axis_at] // blocks).reshape((-1,) + (1,) * (len(dims) - 1 - axis_at))
    return factor_of


def bell_draw(key, dims, deviation, limit, cuts=(), kind=jnp.bfloat16):
    factor_of = steps_of(key, dims, cuts, -0.22, 0.18) if cuts else 1.0
    values = jax.random.normal(key, dims, jnp.float32) * deviation * factor_of
    return jnp.minimum(jnp.maximum(values, -limit), limit).astype(kind)


def setup_inputs(seed: int = 0) -> dict:
    key_of = jax.random.split(jax.random.key(seed), 6)
    leaf_fronts = draw_leaf_fronts(jax.random.fold_in(key_of[5], 71), 0)
    coupling_cols = draw_coupling_cols(jax.random.fold_in(key_of[5], 71), 0)
    coupling_vals = bell_draw(key_of[2], (N_LEAF, N_FRONT, RT, KC), 0.02, 0.1, ((0, 8), (1, 4)), jnp.float32)
    sep_diag = jnp.clip(jnp.exp(math.log(3.0) - 1.0986123 * jax.random.uniform(key_of[3], (N_LEAF, N_FRONT, RT), jnp.float32) ** steps_of(key_of[3], (N_LEAF, N_FRONT, RT), ((0, 8), (1, 4)), -0.2, 0.2)), 1.0, 3.0)
    child_maps = draw_child_maps(jax.random.fold_in(key_of[5], 71), 0)
    return {"leaf_fronts": leaf_fronts, "coupling_cols": coupling_cols, "coupling_vals": coupling_vals, "sep_diag": sep_diag, "child_maps": child_maps}


highest_precision = lax.Precision.HIGHEST

def symmetric_of(lower_tri):
    return lower_tri + lower_tri.T - jnp.diag(jnp.diag(lower_tri))

def partial_factor(lower_front):
    panel_cols = lower_front[:, :SEP]
    head_block = symmetric_of(panel_cols[:SEP])
    chol_head = jnp.linalg.cholesky(head_block)
    below = jax.scipy.linalg.solve_triangular(chol_head, panel_cols[SEP:].T, lower=True).T
    return (chol_head, below)

def reference(leaf_fronts, coupling_cols, coupling_vals, sep_diag, child_maps):
    width_all = SEP + BND
    factor_out = jnp.zeros((N_LEAF, N_FRONT, RALL, SEP), jnp.float32)
    log_total = jnp.zeros((), jnp.float32)
    updates_now = []
    factor_offset = 0
    list_offset = 0
    map_base = 0
    for level_no in range(LEVELS):
        span_leaf = 2 ** level_no
        size_rows = width_all // (N_FRONT * span_leaf)
        fronts_here = N_LEAF // span_leaf
        updates_next = []
        for front_no in range(fronts_here):
            first_leaf = front_no * span_leaf
            if level_no == 0:
                lower_front = jnp.tril(leaf_fronts[front_no])
            else:
                assembled = jnp.zeros((width_all, width_all), jnp.float32)
                for child_no in range(2):
                    index_map = child_maps[map_base + 2 * front_no + child_no]
                    assembled = assembled.at[index_map[:, None], index_map[None, :]].add(updates_now[2 * front_no + child_no])
                lower_front = jnp.tril(assembled)
                col_block = coupling_cols[first_leaf:first_leaf + span_leaf, :, list_offset:list_offset + size_rows, :].reshape(width_all, KC)
                val_block = coupling_vals[first_leaf:first_leaf + span_leaf, :, list_offset:list_offset + size_rows, :].reshape(width_all, KC)
                row_ids = jnp.arange(width_all, dtype=jnp.int32)
                lower_front = lower_front.at[row_ids[:, None], col_block].add(val_block)
                diag_block = sep_diag[first_leaf:first_leaf + span_leaf, :, list_offset:list_offset + size_rows].reshape(width_all)
                lower_front = lower_front + jnp.diag(diag_block)
            chol_head, below = partial_factor(lower_front)
            log_total = log_total + 2.0 * jnp.sum(jnp.log(jnp.diag(chol_head)))
            factor_cols = jnp.concatenate([chol_head, below], axis=0).reshape(span_leaf, N_FRONT, size_rows, SEP)
            factor_out = factor_out.at[first_leaf:first_leaf + span_leaf, :, factor_offset:factor_offset + size_rows, :].set(factor_cols)
            if level_no < LEVELS - 1:
                product = jnp.dot(below.astype(jnp.float32), below.T.astype(jnp.float32), precision=highest_precision, preferred_element_type=jnp.float32)
                update_low = jnp.tril(lower_front[SEP:, SEP:] - product)
                updates_next.append(symmetric_of(update_low))
        if level_no > 0:
            list_offset = list_offset + size_rows
            map_base = map_base + N_LEAF // 2 ** (level_no - 1)
        factor_offset = factor_offset + size_rows
        updates_now = updates_next
    return (factor_out, log_total)
```

```python
import functools

import jax
import jax.numpy as jnp
from jax import lax
from jax.experimental import pallas as pl
from jax.experimental.pallas import tpu as pltpu
from jax.sharding import Mesh, PartitionSpec as P

SEP = 512
BND = 512
WIDTH = SEP + BND
KC = 128
T = 128
NB = SEP // T
TILE = 256
NPACK = NB * (NB + 1) // 2
F32 = jnp.float32
BF16 = jnp.bfloat16
VMEM_LIMIT = 50 * 1024 * 1024


def pack_index(i, j):
    return i * (i + 1) // 2 + j


def split(x):
    hi = x.astype(BF16)
    return hi, (x - hi.astype(F32)).astype(BF16)


def dot_nt(a, b):
    return lax.dot_general(a, b, (((1,), (1,)), ((), ())), preferred_element_type=F32)


def dot_nn(a, b):
    return lax.dot_general(a, b, (((1,), (0,)), ((), ())), preferred_element_type=F32)


def mm_nt(a, b):
    a_hi, a_lo = split(a)
    b_hi, b_lo = split(b)
    return dot_nt(a_hi, b_hi) + (dot_nt(a_hi, b_lo) + dot_nt(a_lo, b_hi))


def iota2(shape, dim):
    return lax.broadcasted_iota(jnp.int32, shape, dim)


def tri_sym(block):
    n = block.shape[0]
    rows, cols = iota2((n, n), 0), iota2((n, n), 1)
    low = jnp.where(cols <= rows, block, 0.0)
    strict = jnp.where(cols < rows, block, 0.0)
    return low + strict.T


def chol_and_inverse(sym):
    lane, sub = iota2((8, T), 1), iota2((8, T), 0)
    groups = [sym[8 * g : 8 * g + 8] for g in range(T // 8)]
    upper_rows, inv_rows = [], []
    for s in range(T // 8):
        c = 8 * s
        panel = groups[s]
        inside = (lane >= c) & (lane < c + 8)
        cols = [jnp.broadcast_to(panel[:, c + k : c + k + 1], (8, T)) for k in range(8)]
        plain = panel
        aug = jnp.where(inside, jnp.where(lane - c == sub, 1.0, 0.0), panel)
        upper_acc = jnp.zeros((8, T), F32)
        inv_acc = jnp.zeros((8, T), F32)
        for k in range(8):
            at_k = sub == k
            pivot = jnp.broadcast_to(cols[k][k : k + 1], (8, T))
            recip = 1.0 / pivot
            root = lax.rsqrt(pivot)
            plain_row = jnp.broadcast_to(plain[k : k + 1], (8, T))
            aug_row = jnp.broadcast_to(aug[k : k + 1], (8, T))
            upper_acc = jnp.where(at_k, plain_row * root, upper_acc)
            inv_acc = jnp.where(at_k, aug_row * root, inv_acc)
            plain = plain - cols[k] * (plain_row * recip)
            scaled = aug_row * recip
            aug = jnp.where(at_k, scaled, aug - cols[k] * scaled)
            for m in range(k + 1, 8):
                term = jnp.broadcast_to(cols[m][k : k + 1], (8, T)) * recip
                cols[m] = jnp.where(at_k, term, cols[m] - cols[k] * term)
        upper_rows.append(jnp.where(lane >= c + sub, upper_acc, 0.0))
        inv_rows.append(jnp.where(lane <= c + sub, inv_acc, 0.0))
        sol = [jnp.broadcast_to(aug[k : k + 1], (8, T)) for k in range(8)]
        for g in range(s + 1, T // 8):
            old = groups[g]
            terms = [
                jnp.broadcast_to(old[:, c + k : c + k + 1], (8, T)) * sol[k] for k in range(8)
            ]
            total = ((terms[0] + terms[1]) + (terms[2] + terms[3])) + (
                (terms[4] + terms[5]) + (terms[6] + terms[7])
            )
            groups[g] = jnp.where(inside, 0.0, old) - total
    return jnp.concatenate(upper_rows, axis=0), jnp.concatenate(inv_rows, axis=0)


def factor_panel(f_ref, x_ref, log_ref, rows):
    log_ref[...] = jnp.zeros_like(log_ref)

    @pl.loop(0, NB)
    def _(j):
        at = pl.multiple_of(j * T, T)
        upper, inv = chol_and_inverse(tri_sym(f_ref[pl.ds(at, T), pl.ds(at, T)]))
        f_ref[pl.ds(at, T), pl.ds(at, T)] = upper.T
        x_ref[pl.ds(at, T), :] = inv
        eye = iota2((T, T), 0) == iota2((T, T), 1)
        diag = jnp.sum(jnp.where(eye, upper, 0.0), axis=0, keepdims=True)
        log_ref[0:1, :] += jnp.log(diag)
        for k in range(NB):
            first = (k + 1) * T
            if first >= rows:
                continue

            @pl.when(j == k)
            def _():
                below = mm_nt(f_ref[first:rows, k * T : first], inv)
                f_ref[first:rows, k * T : first] = below
                if first < SEP:
                    f_ref[first:rows, first:SEP] -= mm_nt(below, below[: SEP - first])


def zero_above(f_ref):
    for i in range(NB - 1):
        f_ref[i * T : (i + 1) * T, (i + 1) * T : SEP] = jnp.zeros((T, SEP - (i + 1) * T), F32)


def log_total(log_ref):
    return 2.0 * jnp.sum(log_ref[0:1, :], axis=1, keepdims=True)


def write_own(out_ref, f_ref, start):
    size = out_ref.shape[0]
    if size % 8 == 0:
        out_ref[...] = f_ref[pl.ds(pl.multiple_of(start, 8), size), 0:SEP]
    else:
        base = pl.multiple_of(start // 8 * 8, 8)
        block = f_ref[pl.ds(base, 8), 0:SEP]
        offset = start - base
        piece = block[0:size]
        for shift in range(size, 8, size):
            piece = jnp.where(offset == shift, block[shift : shift + size], piece)
        out_ref[...] = piece


def write_update(pk_ref, below, tail_of, log_value):
    hi, lo = split(below)
    rows, cols = iota2((T, T), 0), iota2((T, T), 1)
    for i in range(NB):
        here = slice(i * T, (i + 1) * T)
        upto = slice(0, (i + 1) * T)
        prod = dot_nt(hi[here], hi[upto]) + (dot_nt(hi[here], lo[upto]) + dot_nt(lo[here], hi[upto]))
        for j in range(i + 1):
            block = tail_of(i, j) - prod[:, j * T : (j + 1) * T]
            if i == 0:
                block = jnp.where((rows == 0) & (cols == T - 1), log_value, block)
            pk_ref[pack_index(i, j)] = block


def head_kernel(head_ref, fac_ref, x_ref, log_ref):
    fac_ref[...] = head_ref[...]
    factor_panel(fac_ref, x_ref, log_ref, SEP)
    zero_above(fac_ref)


def leaf_kernel(pos_ref, fac_ref, x_ref, log_ref, panel_ref, tail_ref, own_ref, pk_ref, work, stack):
    work[...] = panel_ref[...]
    for j in range(NB):
        here = slice(j * T, (j + 1) * T)
        solved = mm_nt(work[:, here], x_ref[here, :])
        work[:, here] = solved
        if j + 1 < NB:
            rest = slice((j + 1) * T, SEP)
            work[:, rest] -= mm_nt(solved, fac_ref[rest, here])
    stack[0:SEP, :] = fac_ref[...]
    stack[SEP:, :] = work[...]
    write_own(own_ref, stack, pos_ref[1] * own_ref.shape[0])

    def tail_of(i, j):
        return tail_ref[i * T : (i + 1) * T, j * T : (j + 1) * T]

    write_update(pk_ref, work[...], tail_of, log_total(log_ref))


def assemble(level, n_leaf, pos_ref, kids, maps_ref, dense_ref, diag_ref, f_ref, u_hi, u_lo, hot, y_hi, y_lo, last):
    leaf = pos_ref[0]
    base = 2 * n_leaf - 2 * (n_leaf >> (level - 1))
    own = leaf >> (level - 1)
    rows, cols = iota2((T, T), 0), iota2((T, T), 1)
    for child, pk_ref in enumerate(kids):
        number = base + (own if child == 0 else own ^ 1)
        for i in range(NB):
            for j in range(i + 1):
                block = pk_ref[pack_index(i, j)]
                if i == j:
                    low = jnp.where(cols <= rows, block, 0.0)
                    block = low + jnp.where(cols < rows, block, 0.0).T
                hi, lo = split(block)
                u_hi[i * T : (i + 1) * T, j * T : (j + 1) * T] = hi
                u_lo[i * T : (i + 1) * T, j * T : (j + 1) * T] = lo
                if i != j:
                    hi, lo = split(block.T)
                    u_hi[j * T : (j + 1) * T, i * T : (i + 1) * T] = hi
                    u_lo[j * T : (j + 1) * T, i * T : (i + 1) * T] = lo
        index_row = maps_ref[pl.ds(number, 1), :]

        @pl.loop(0, WIDTH // TILE)
        def _(tile):
            at = pl.multiple_of(tile * TILE, TILE)
            ids = iota2((TILE, BND), 0) + at
            match = jnp.where(ids == index_row, 1.0, 0.0).astype(BF16)
            hot[child, pl.ds(at, TILE), :] = match
            y_hi[child, pl.ds(at, TILE), :] = dot_nn(match, u_hi[...]).astype(BF16)
            y_lo[child, pl.ds(at, TILE), :] = dot_nn(match, u_lo[...]).astype(BF16)

    for a in range(WIDTH // TILE):
        here = slice(a * TILE, (a + 1) * TILE)
        for b in range(a + 1):
            if last and b * TILE >= SEP:
                continue
            there = slice(b * TILE, (b + 1) * TILE)
            parts = [
                dot_nt(y_hi[c, here, :], hot[c, there, :]) + dot_nt(y_lo[c, here, :], hot[c, there, :])
                for c in range(2)
            ]
            total = parts[0] + parts[1]
            for h in range(TILE // T):
                col_block = b * (TILE // T) + h
                piece = total[:, h * T : (h + 1) * T] + dense_ref[col_block, here, :]
                f_ref[here, col_block * T : (col_block + 1) * T] = piece
    for d in range((SEP if last else WIDTH) // T):
        spot = slice(d * T, (d + 1) * T)
        f_ref[spot, spot] += jnp.where(rows == cols, diag_ref[d : d + 1, :], 0.0)


def level_kernel(
    level, n_leaf, n_front, last,
    pos_ref, own_pk, sib_pk, maps_ref, dense_ref, diag_ref,
    own_ref, next_ref,
    f_ref, x_ref, log_ref, u_hi, u_lo, hot, y_hi, y_lo,
):
    assemble(
        level, n_leaf, pos_ref, (own_pk, sib_pk), maps_ref, dense_ref, diag_ref,
        f_ref, u_hi, u_lo, hot, y_hi, y_lo, last,
    )
    factor_panel(f_ref, x_ref, log_ref, WIDTH)
    zero_above(f_ref)
    rank = (pos_ref[0] & ((1 << level) - 1)) * n_front + pos_ref[1]
    write_own(own_ref, f_ref, rank * own_ref.shape[0])
    kids_log = own_pk[0][0:1, T - 1 : T] + sib_pk[0][0:1, T - 1 : T]
    log_value = kids_log + log_total(log_ref)
    if last:
        next_ref[...] = jnp.broadcast_to(log_value, next_ref.shape)
    else:

        def tail_of(i, j):
            return f_ref[SEP + i * T : SEP + (i + 1) * T, SEP + j * T : SEP + (j + 1) * T]

        write_update(next_ref, f_ref[SEP:, 0:SEP], tail_of, log_value)


def densify_kernel(lists_ref, out_ref):
    block_ids = iota2((8, KC), 0).astype(F32)
    column_ids = iota2((T, KC), 0).astype(F32)

    @pl.loop(0, WIDTH // 8)
    def _(group):
        at = pl.multiple_of(group * 8, 8)
        cols = lists_ref[pl.ds(at, 8), 0:KC]
        vals = lists_ref[pl.ds(at, 8), KC:]
        block_no = jnp.floor(cols * (1.0 / T))
        within = cols - block_no * T
        hi = vals.astype(BF16).astype(F32)
        lo = vals - hi
        for r in range(8):
            pick = block_ids == block_no[r : r + 1]
            left = jnp.concatenate(
                [jnp.where(pick, hi[r : r + 1], 0.0), jnp.where(pick, lo[r : r + 1], 0.0)], axis=0
            ).astype(BF16)
            right = jnp.where(column_ids == within[r : r + 1], 1.0, 0.0).astype(BF16)
            both = dot_nt(left, right)
            out_ref[pl.ds(at + r, 8, stride=WIDTH), :] = both[0:8] + both[8:16]


def params():
    return pltpu.CompilerParams(vmem_limit_bytes=VMEM_LIMIT)


def vmem():
    return pl.BlockSpec(memory_space=pltpu.VMEM)


def smem():
    return pl.BlockSpec(memory_space=pltpu.SMEM)


def shape(*dims):
    return jax.ShapeDtypeStruct(dims, F32)


def cost(us):
    return pl.CostEstimate(flops=0, bytes_accessed=int(us * 3.0e6), transcendentals=0)


def densify(lists):
    out = pl.pallas_call(
        densify_kernel,
        out_shape=shape(WIDTH // T * WIDTH, T),
        in_specs=[vmem()],
        out_specs=vmem(),
        compiler_params=params(),
        cost_estimate=cost(12),
        name="densify",
    )(lists)
    return out.reshape(WIDTH // T, WIDTH, T)


def run_head(head):
    return pl.pallas_call(
        head_kernel,
        out_shape=(shape(SEP, SEP), shape(SEP, T), shape(8, T)),
        in_specs=[vmem()],
        out_specs=(vmem(),) * 3,
        compiler_params=params(),
        cost_estimate=cost(25),
        name="head_factor",
    )(head)


def run_leaf(pos, fac, inv, logs, panel, tail, size_rows):
    return pl.pallas_call(
        leaf_kernel,
        out_shape=(shape(size_rows, SEP), shape(NPACK, T, T)),
        in_specs=[smem()] + [vmem()] * 5,
        out_specs=(vmem(),) * 2,
        scratch_shapes=[pltpu.VMEM((BND, SEP), F32), pltpu.VMEM((WIDTH, SEP), F32)],
        compiler_params=params(),
        cost_estimate=cost(5),
        name="leaf_update",
    )(pos, fac, inv, logs, panel, tail)


def run_level(level, n_leaf, n_front, last, pos, own_pk, sib_pk, maps, dense, diag, size_rows):
    return pl.pallas_call(
        functools.partial(level_kernel, level, n_leaf, n_front, last),
        out_shape=(shape(size_rows, SEP), shape(8, T) if last else shape(NPACK, T, T)),
        in_specs=[smem()] + [vmem()] * 5,
        out_specs=(vmem(),) * 2,
        scratch_shapes=[
            pltpu.VMEM((WIDTH, WIDTH), F32),
            pltpu.VMEM((SEP, T), F32),
            pltpu.VMEM((8, T), F32),
            pltpu.VMEM((BND, BND), BF16),
            pltpu.VMEM((BND, BND), BF16),
            pltpu.VMEM((2, WIDTH, BND), BF16),
            pltpu.VMEM((2, WIDTH, BND), BF16),
            pltpu.VMEM((2, WIDTH, BND), BF16),
        ],
        compiler_params=params(),
        cost_estimate=cost(35),
        name="level_front",
    )(pos, own_pk, sib_pk, maps, dense, diag)


def swap_front(x, mask):
    count = lax.axis_size("front")
    return lax.ppermute(x, "front", [(f, f ^ mask) for f in range(count)])


def double_up(x, bits, front):
    for b in range(bits):
        partner = swap_front(x, 1 << b)
        high = (front >> b & 1) == 1
        x = jnp.concatenate([jnp.where(high, partner, x), jnp.where(high, x, partner)], axis=0)
    return x


def body(leaf_bits, leaf_fronts, coupling_cols, coupling_vals, sep_diag, child_maps):
    n_front = lax.axis_size("front")
    bits = len(leaf_bits)
    n_leaf = 1 << bits
    front = lax.axis_index("front")
    leaf = lax.axis_index(leaf_bits) if bits else 0
    pos = jnp.stack([leaf, front]).astype(jnp.int32)
    strip = leaf_fronts[0]
    half = n_front // 2
    half_bits = half.bit_length() - 1
    in_tail = front >= half

    panel_strip = strip[:, :SEP]
    other_strip = swap_front(panel_strip, half)
    own_half = double_up(panel_strip, half_bits, front)
    other_half = double_up(other_strip, half_bits, front)
    head = jnp.where(in_tail, other_half, own_half)
    panel = jnp.where(in_tail, own_half, other_half)
    tail_strip = strip[:, SEP:]
    sent = lax.ppermute(tail_strip, "front", [(f, f - half) for f in range(half, n_front)])
    tail = double_up(jnp.where(in_tail, tail_strip, sent), half_bits, front)

    lists, diags = [], []
    offset = 0
    for level in range(1, bits + 1):
        size_rows = WIDTH // (n_front << level)
        span = slice(offset, offset + size_rows)
        entries = jnp.concatenate(
            [coupling_cols[0, 0, span].astype(F32), coupling_vals[0, 0, span]], axis=1
        )
        diag_row = jnp.pad(sep_diag[0, 0, span], (0, 2 * KC - size_rows))[None]
        packed = jnp.concatenate([entries, jnp.pad(diag_row, ((0, 7), (0, 0)))], axis=0)
        axes = leaf_bits[bits - level :] + ("front",)
        gathered = lax.all_gather(packed, axes, axis=0, tiled=False)
        lists.append(gathered[:, :size_rows].reshape(WIDTH, 2 * KC))
        diags.append(gathered[:, size_rows, :size_rows].reshape(WIDTH // T, T))
        offset += size_rows

    fac, inv, logs = run_head(head)
    piece, pk = run_leaf(pos, fac, inv, logs, panel, tail, WIDTH // n_front)
    pieces = [piece]
    for level in range(1, bits + 1):
        size_rows = WIDTH // (n_front << level)
        last = level == bits
        sib = lax.ppermute(pk, leaf_bits[bits - level], [(0, 1), (1, 0)])
        dense = densify(lists[level - 1])
        piece, pk = run_level(
            level, n_leaf, n_front, last, pos, pk, sib, child_maps, dense, diags[level - 1], size_rows
        )
        pieces.append(piece)
    log_det = pk[0, 0]
    return jnp.concatenate(pieces, axis=0)[None, None], log_det


def solution(mesh):
    bits = mesh.shape["leaf"].bit_length() - 1
    leaf_bits = tuple(f"leaf{b}" for b in reversed(range(bits)))
    fine = Mesh(mesh.devices.reshape((2,) * bits + (mesh.shape["front"],)), leaf_bits + ("front",))
    placed = (
        P(leaf_bits, "front", None),
        P(leaf_bits, "front", None, None),
        P(leaf_bits, "front", None, None),
        P(leaf_bits, "front", None),
        P(),
    )
    return jax.shard_map(
        functools.partial(body, leaf_bits),
        mesh=fine,
        in_specs=placed,
        out_specs=(P(leaf_bits, "front", None, None), P()),
        check_vma=False,
    )
```

```python
import functools

import jax
import jax.numpy as jnp
from jax import lax
from jax.experimental import pallas as pl
from jax.experimental.pallas import tpu as pltpu
from jax.sharding import Mesh, PartitionSpec as P

SEP = 512
BND = 512
WIDTH = SEP + BND
KC = 128
T = 128
NB = SEP // T
TILE = 256
NPACK = NB * (NB + 1) // 2
F32 = jnp.float32
BF16 = jnp.bfloat16
VMEM_LIMIT = 50 * 1024 * 1024


def pack_index(i, j):
    return i * (i + 1) // 2 + j


def split(x):
    hi = x.astype(BF16)
    return hi, (x - hi.astype(F32)).astype(BF16)


def dot_nt(a, b):
    return lax.dot_general(a, b, (((1,), (1,)), ((), ())), preferred_element_type=F32)


def dot_nn(a, b):
    return lax.dot_general(a, b, (((1,), (0,)), ((), ())), preferred_element_type=F32)


def mm_nt(a, b):
    a_hi, a_lo = split(a)
    b_hi, b_lo = split(b)
    return dot_nt(a_hi, b_hi) + (dot_nt(a_hi, b_lo) + dot_nt(a_lo, b_hi))


def iota2(shape, dim):
    return lax.broadcasted_iota(jnp.int32, shape, dim)


def tri_sym(block):
    n = block.shape[0]
    rows, cols = iota2((n, n), 0), iota2((n, n), 1)
    low = jnp.where(cols <= rows, block, 0.0)
    strict = jnp.where(cols < rows, block, 0.0)
    return low + strict.T


def chol_and_inverse(sym):
    lane, sub = iota2((8, T), 1), iota2((8, T), 0)
    groups = [sym[8 * g : 8 * g + 8] for g in range(T // 8)]
    upper_rows, inv_rows = [], []
    for s in range(T // 8):
        c = 8 * s
        panel = groups[s]
        inside = (lane >= c) & (lane < c + 8)
        cols = [jnp.broadcast_to(panel[:, c + k : c + k + 1], (8, T)) for k in range(8)]
        plain = panel
        aug = jnp.where(inside, jnp.where(lane - c == sub, 1.0, 0.0), panel)
        upper_acc = jnp.zeros((8, T), F32)
        inv_acc = jnp.zeros((8, T), F32)
        for k in range(8):
            at_k = sub == k
            pivot = jnp.broadcast_to(cols[k][k : k + 1], (8, T))
            recip = 1.0 / pivot
            root = lax.rsqrt(pivot)
            plain_row = jnp.broadcast_to(plain[k : k + 1], (8, T))
            aug_row = jnp.broadcast_to(aug[k : k + 1], (8, T))
            upper_acc = jnp.where(at_k, plain_row * root, upper_acc)
            inv_acc = jnp.where(at_k, aug_row * root, inv_acc)
            plain = plain - cols[k] * (plain_row * recip)
            scaled = aug_row * recip
            aug = jnp.where(at_k, scaled, aug - cols[k] * scaled)
            for m in range(k + 1, 8):
                term = jnp.broadcast_to(cols[m][k : k + 1], (8, T)) * recip
                cols[m] = jnp.where(at_k, term, cols[m] - cols[k] * term)
        upper_rows.append(jnp.where(lane >= c + sub, upper_acc, 0.0))
        inv_rows.append(jnp.where(lane <= c + sub, inv_acc, 0.0))
        sol = [jnp.broadcast_to(aug[k : k + 1], (8, T)) for k in range(8)]
        for g in range(s + 1, T // 8):
            old = groups[g]
            terms = [
                jnp.broadcast_to(old[:, c + k : c + k + 1], (8, T)) * sol[k] for k in range(8)
            ]
            total = ((terms[0] + terms[1]) + (terms[2] + terms[3])) + (
                (terms[4] + terms[5]) + (terms[6] + terms[7])
            )
            groups[g] = jnp.where(inside, 0.0, old) - total
    return jnp.concatenate(upper_rows, axis=0), jnp.concatenate(inv_rows, axis=0)


def factor_panel(f_ref, x_ref, log_ref, rows, blocks):
    width = blocks * T
    log_ref[...] = jnp.zeros_like(log_ref)

    @pl.loop(0, blocks)
    def _(j):
        at = pl.multiple_of(j * T, T)
        upper, inv = chol_and_inverse(tri_sym(f_ref[pl.ds(at, T), pl.ds(at, T)]))
        f_ref[pl.ds(at, T), pl.ds(at, T)] = upper.T
        x_ref[pl.ds(at, T), :] = inv
        eye = iota2((T, T), 0) == iota2((T, T), 1)
        diag = jnp.sum(jnp.where(eye, upper, 0.0), axis=0, keepdims=True)
        log_ref[0:1, :] += jnp.log(diag)
        for k in range(blocks):
            first = (k + 1) * T
            if first >= rows:
                continue

            @pl.when(j == k)
            def _():
                below = mm_nt(f_ref[first:rows, k * T : first], inv)
                f_ref[first:rows, k * T : first] = below
                if first < width:
                    f_ref[first:rows, first:width] -= mm_nt(below, below[: width - first])


def zero_above(f_ref, blocks):
    for i in range(blocks - 1):
        f_ref[i * T : (i + 1) * T, (i + 1) * T : blocks * T] = jnp.zeros((T, (blocks - 1 - i) * T), F32)


def log_total(log_ref):
    return 2.0 * jnp.sum(log_ref[0:1, :], axis=1, keepdims=True)


def write_own(out_ref, f_ref, start):
    size = out_ref.shape[0]
    if size % 8 == 0:
        out_ref[...] = f_ref[pl.ds(pl.multiple_of(start, 8), size), 0:SEP]
    else:
        base = pl.multiple_of(start // 8 * 8, 8)
        block = f_ref[pl.ds(base, 8), 0:SEP]
        offset = start - base
        piece = block[0:size]
        for shift in range(size, 8, size):
            piece = jnp.where(offset == shift, block[shift : shift + size], piece)
        out_ref[...] = piece


def write_update(pk_ref, below, tail_of, log_value):
    hi, lo = split(below)
    rows, cols = iota2((T, T), 0), iota2((T, T), 1)
    for i in range(NB):
        here = slice(i * T, (i + 1) * T)
        upto = slice(0, (i + 1) * T)
        prod = dot_nt(hi[here], hi[upto]) + (dot_nt(hi[here], lo[upto]) + dot_nt(lo[here], hi[upto]))
        for j in range(i + 1):
            block = tail_of(i, j) - prod[:, j * T : (j + 1) * T]
            if i == 0:
                block = jnp.where((rows == 0) & (cols == T - 1), log_value, block)
            pk_ref[pack_index(i, j)] = block


def place(pieces, work, front, want_tail, skip=0):
    count = len(pieces)
    half = count // 2
    size = pieces[0].shape[0]
    for m, piece in enumerate(pieces):
        source = front ^ m

        @pl.when(((source >= half) == want_tail) & ((source & (half - 1)) * size >= skip))
        def _():
            at = pl.multiple_of((source & (half - 1)) * size - skip, 8)
            work[pl.ds(at, size), :] = piece[...]


def first_kernel(n, pos_ref, *refs):
    pieces, (fac_ref, x_ref, log_ref) = refs[:n], refs[n:]
    place(pieces, fac_ref, pos_ref[1], False)
    factor_panel(fac_ref, x_ref, log_ref, SEP, NB // 2)
    zero_above(fac_ref, NB // 2)


def second_kernel(n, pos_ref, first_ref, *refs):
    pieces, (fac_ref, x_ref, log_ref) = refs[:n], refs[n:]
    place(pieces, fac_ref, pos_ref[1], False, SEP // 2)
    left = first_ref[SEP // 2 :, :]
    fac_ref[...] -= mm_nt(left, left)
    factor_panel(fac_ref, x_ref, log_ref, SEP // 2, NB // 2)
    zero_above(fac_ref, NB // 2)


def leaf_kernel(n, pos_ref, fac1, x1, log1, fac2, x2, log2, *refs):
    pieces1, pieces2, tails = refs[:n], refs[n : 2 * n], refs[2 * n : 2 * n + n // 2]
    own_ref, pk_ref, work, tail_ref, stack = refs[2 * n + n // 2 :]
    front = pos_ref[1]
    half = n // 2
    middle = SEP // 2
    place(pieces1, work.at[:, 0:middle], front, True)
    place(pieces2, work.at[:, middle:SEP], front, True)
    for m, piece in enumerate(tails):
        at = pl.multiple_of(((front ^ m) & (half - 1)) * piece.shape[0], 8)
        tail_ref[pl.ds(at, piece.shape[0]), :] = piece[...]
    stack[0:SEP, 0:middle] = fac1[...]
    stack[0:middle, middle:SEP] = jnp.zeros((middle, middle), F32)
    stack[middle:SEP, middle:SEP] = fac2[...]
    for j in range(NB):
        here = slice(j * T, (j + 1) * T)
        inv = x1[here, :] if j < NB // 2 else x2[j * T - middle : (j + 1) * T - middle, :]
        solved = mm_nt(work[:, here], inv)
        work[:, here] = solved
        if j + 1 < NB:
            rest = slice((j + 1) * T, SEP)
            work[:, rest] -= mm_nt(solved, stack[rest, here])
    stack[SEP:, :] = work[...]
    write_own(own_ref, stack, front * own_ref.shape[0])

    def tail_of(i, j):
        return tail_ref[i * T : (i + 1) * T, j * T : (j + 1) * T]

    write_update(pk_ref, work[...], tail_of, log_total(log1) + log_total(log2))


def expand(pk_ref, u_hi, u_lo):
    rows, cols = iota2((T, T), 0), iota2((T, T), 1)
    for i in range(NB):
        for j in range(i + 1):
            block = pk_ref[pack_index(i, j)]
            if i == j:
                low = jnp.where(cols <= rows, block, 0.0)
                block = low + jnp.where(cols < rows, block, 0.0).T
            hi, lo = split(block)
            u_hi[i * T : (i + 1) * T, j * T : (j + 1) * T] = hi
            u_lo[i * T : (i + 1) * T, j * T : (j + 1) * T] = lo
            if i != j:
                hi, lo = split(block.T)
                u_hi[j * T : (j + 1) * T, i * T : (i + 1) * T] = hi
                u_lo[j * T : (j + 1) * T, i * T : (i + 1) * T] = lo


def extend_add(pk_ref, index_row, base_of, last, f_ref, u_hi, u_lo, hot, y_hi, y_lo):
    expand(pk_ref, u_hi, u_lo)

    @pl.loop(0, WIDTH // TILE)
    def _(tile):
        at = pl.multiple_of(tile * TILE, TILE)
        ids = iota2((TILE, BND), 0) + at
        match = jnp.where(ids == index_row, 1.0, 0.0).astype(BF16)
        hot[pl.ds(at, TILE), :] = match
        y_hi[pl.ds(at, TILE), :] = dot_nn(match, u_hi[...]).astype(BF16)
        y_lo[pl.ds(at, TILE), :] = dot_nn(match, u_lo[...]).astype(BF16)

    for a in range(WIDTH // TILE):
        here = slice(a * TILE, (a + 1) * TILE)
        for b in range(a + 1):
            if last and b * TILE >= SEP:
                continue
            there = slice(b * TILE, (b + 1) * TILE)
            part = dot_nt(y_hi[here, :], hot[there, :]) + dot_nt(y_lo[here, :], hot[there, :])
            f_ref[here, there] = base_of(a, b) + part


def map_row(level, n_leaf, pos_ref, maps_ref, sibling):
    base = 2 * n_leaf - 2 * (n_leaf >> (level - 1))
    own = pos_ref[0] >> (level - 1)
    number = base + (own ^ 1 if sibling else own)
    return maps_ref[pl.ds(number, 1), :]


def own_kernel(level, n_leaf, last, pos_ref, lists_ref, pk_ref, maps_ref, f_ref, dense, u_hi, u_lo, hot, y_hi, y_lo):
    densify(lists_ref, dense)
    index_row = map_row(level, n_leaf, pos_ref, maps_ref, False)

    def base_of(a, b):
        per = TILE // T
        return jnp.concatenate(
            [dense[(b * per + h) * WIDTH + a * TILE : (b * per + h) * WIDTH + (a + 1) * TILE, :] for h in range(per)],
            axis=1,
        )

    extend_add(pk_ref, index_row, base_of, last, f_ref, u_hi, u_lo, hot, y_hi, y_lo)
    size = lists_ref.shape[1] - 8
    rows, cols = iota2((T, T), 0), iota2((T, T), 1)
    for d in range((SEP if last else WIDTH) // T):
        diag = jnp.zeros((1, T), F32)
        for rank in range(d * T // size, (d + 1) * T // size):
            diag = diag + lists_ref[rank, size : size + 1, 0:T]
        spot = slice(d * T, (d + 1) * T)
        f_ref[spot, spot] += jnp.where(rows == cols, diag, 0.0)


def level_kernel(
    level, n_leaf, n_front, last,
    pos_ref, base_ref, own_pk, sib_pk, maps_ref,
    own_ref, next_ref,
    f_ref, x_ref, log_ref, u_hi, u_lo, hot, y_hi, y_lo,
):
    index_row = map_row(level, n_leaf, pos_ref, maps_ref, True)

    def base_of(a, b):
        return base_ref[a * TILE : (a + 1) * TILE, b * TILE : (b + 1) * TILE]

    extend_add(sib_pk, index_row, base_of, last, f_ref, u_hi, u_lo, hot, y_hi, y_lo)
    factor_panel(f_ref, x_ref, log_ref, WIDTH, NB)
    zero_above(f_ref, NB)
    rank = (pos_ref[0] & ((1 << level) - 1)) * n_front + pos_ref[1]
    write_own(own_ref, f_ref, rank * own_ref.shape[0])
    kids_log = own_pk[0][0:1, T - 1 : T] + sib_pk[0][0:1, T - 1 : T]
    log_value = kids_log + log_total(log_ref)
    if last:
        next_ref[...] = jnp.broadcast_to(log_value, next_ref.shape)
    else:

        def tail_of(i, j):
            return f_ref[SEP + i * T : SEP + (i + 1) * T, SEP + j * T : SEP + (j + 1) * T]

        write_update(next_ref, f_ref[SEP:, 0:SEP], tail_of, log_value)


def densify(lists_ref, out_ref):
    block_ids = iota2((8, KC), 0).astype(F32)
    column_ids = iota2((T, KC), 0).astype(F32)
    size = lists_ref.shape[1] - 8
    step = min(size, 32)

    @pl.loop(0, WIDTH // step)
    def _(turn):
        start = turn * step
        rank = start // size
        within_rank = start % size
        for g in range(step // 8):
            at = pl.multiple_of(within_rank + g * 8, 8)
            cols = lists_ref[rank, pl.ds(at, 8), 0:KC]
            vals = lists_ref[rank, pl.ds(at, 8), KC:]
            block_no = jnp.floor(cols * (1.0 / T))
            within = cols - block_no * T
            hi = vals.astype(BF16).astype(F32)
            lo = vals - hi
            for r in range(8):
                pick = block_ids == block_no[r : r + 1]
                left = jnp.concatenate(
                    [jnp.where(pick, hi[r : r + 1], 0.0), jnp.where(pick, lo[r : r + 1], 0.0)], axis=0
                ).astype(BF16)
                right = jnp.where(column_ids == within[r : r + 1], 1.0, 0.0).astype(BF16)
                both = dot_nt(left, right)
                out_ref[pl.ds(start + g * 8 + r, 8, stride=WIDTH), :] = both[0:8] + both[8:16]


def pack_kernel(sizes, cols_ref, vals_ref, diag_ref, *out_refs):
    offset = 0
    for n, (size, out_ref) in enumerate(zip(sizes, out_refs)):
        out_ref[0:size, 0:KC] = cols_ref[offset : offset + size, :].astype(F32)
        out_ref[0:size, KC:] = vals_ref[offset : offset + size, :]
        out_ref[size : size + 8, :] = jnp.broadcast_to(diag_ref[n : n + 1, :], (8, 2 * KC))
        offset += size


def params():
    return pltpu.CompilerParams(vmem_limit_bytes=VMEM_LIMIT)


def vmem():
    return pl.BlockSpec(memory_space=pltpu.VMEM)


def smem():
    return pl.BlockSpec(memory_space=pltpu.SMEM)


def shape(*dims):
    return jax.ShapeDtypeStruct(dims, F32)


def cost(us):
    return pl.CostEstimate(flops=0, bytes_accessed=int(us * 3.0e6), transcendentals=0)


def call(kernel, out_shape, n_args, n_smem, scratch, us, name):
    outs = out_shape if isinstance(out_shape, tuple) else (out_shape,)
    return pl.pallas_call(
        kernel,
        out_shape=out_shape,
        in_specs=[smem()] * n_smem + [vmem()] * (n_args - n_smem),
        out_specs=(vmem(),) * len(outs) if isinstance(out_shape, tuple) else vmem(),
        scratch_shapes=scratch,
        compiler_params=params(),
        cost_estimate=cost(us),
        name=name,
    )


def extend_scratch():
    return [pltpu.VMEM((BND, BND), BF16)] * 2 + [pltpu.VMEM((WIDTH, BND), BF16)] * 3


def swap_front(x, mask):
    count = lax.axis_size("front")
    return lax.ppermute(x, "front", [(f, f ^ mask) for f in range(count)])


def hypercube(strip, masks):
    pieces = {0: strip}
    for mask in masks:
        for m in sorted(pieces):
            pieces[m | mask] = swap_front(pieces[m], mask)
    return [pieces[m] for m in range(len(pieces))]


def after(x, done):
    return lax.optimization_barrier((x, done))[0]


def body(leaf_bits, leaf_fronts, coupling_cols, coupling_vals, sep_diag, child_maps):
    n_front = lax.axis_size("front")
    bits = len(leaf_bits)
    n_leaf = 1 << bits
    front = lax.axis_index("front")
    leaf = lax.axis_index(leaf_bits)
    pos = jnp.stack([leaf, front]).astype(jnp.int32)
    strip = leaf_fronts[0]
    half = n_front // 2
    inner = [1 << b for b in range(half.bit_length() - 1)]
    masks = [half] + inner
    middle = SEP // 2

    first = hypercube(strip[:, :middle], masks)
    held = after(strip[:, middle:], first[-1])
    second = hypercube(held[:, : SEP - middle], masks)
    tail_strip = held[:, SEP - middle :]
    sent = lax.ppermute(tail_strip, "front", [(f, f - half) for f in range(half, n_front)])
    tails = hypercube(jnp.where(front >= half, tail_strip, sent), inner)

    sizes = [WIDTH // (n_front << level) for level in range(1, bits + 1)]
    diag_rows, offset = [], 0
    for n, size in enumerate(sizes):
        rank = (leaf & ((2 << n) - 1)) * n_front + front
        spread = jnp.tile(sep_diag[0, 0, offset : offset + size], T // size)
        mine = jnp.arange(T) // size == rank % (T // size)
        diag_rows.append(jnp.pad(jnp.where(mine, spread, 0.0), (0, 2 * KC - T)))
        offset += size
    diag_rows = jnp.pad(jnp.stack(diag_rows), ((0, -len(sizes) % 8), (0, 0)))
    packed = call(
        functools.partial(pack_kernel, sizes),
        tuple(shape(size + 8, 2 * KC) for size in sizes), 3, 0, [], 1, "pack_lists",
    )(coupling_cols[0, 0], coupling_vals[0, 0], diag_rows)
    lists = []
    for n, size in enumerate(sizes):
        gathered = lax.all_gather(packed[n], leaf_bits[bits - 1 - n :] + ("front",), axis=0, tiled=False)
        if size < 8:
            rows = gathered[:, :size].reshape(WIDTH // 8, 8, 2 * KC)
            diag = gathered[:, size].reshape(WIDTH // 8, 8 // size, 2 * KC).sum(1, keepdims=True)
            gathered = jnp.concatenate([rows, jnp.pad(diag, ((0, 0), (0, 7), (0, 0)))], axis=1)
        lists.append(gathered)

    fac1, x1, log1 = call(
        functools.partial(first_kernel, n_front),
        (shape(SEP, middle), shape(middle, T), shape(8, T)), 1 + n_front, 1, [], 10, "first_half",
    )(pos, *first)
    fac2, x2, log2 = call(
        functools.partial(second_kernel, n_front),
        (shape(middle, middle), shape(middle, T), shape(8, T)), 2 + n_front, 1, [], 10, "second_half",
    )(pos, fac1, *second)
    piece, pk = call(
        functools.partial(leaf_kernel, n_front),
        (shape(WIDTH // n_front, SEP), shape(NPACK, T, T)), 7 + 2 * n_front + half, 1,
        [pltpu.VMEM((BND, SEP), F32), pltpu.VMEM((BND, BND), F32), pltpu.VMEM((WIDTH, SEP), F32)],
        5, "leaf_update",
    )(pos, fac1, x1, log1, fac2, x2, log2, *first, *second, *tails)
    pieces = [piece]
    for level in range(1, bits + 1):
        size = sizes[level - 1]
        last = level == bits
        sib = lax.ppermute(pk, leaf_bits[bits - level], [(0, 1), (1, 0)])
        base = call(
            functools.partial(own_kernel, level, n_leaf, last), shape(WIDTH, WIDTH), 4, 1,
            [pltpu.VMEM((WIDTH // T * WIDTH, T), F32)] + extend_scratch(), 17, "own_child",
        )(pos, lists[level - 1], pk, child_maps)
        piece, pk = call(
            functools.partial(level_kernel, level, n_leaf, n_front, last),
            (shape(size, SEP), shape(8, T) if last else shape(NPACK, T, T)), 5, 1,
            [pltpu.VMEM((WIDTH, WIDTH), F32), pltpu.VMEM((SEP, T), F32), pltpu.VMEM((8, T), F32)] + extend_scratch(),
            27, "level_front",
        )(pos, base, pk, sib, child_maps)
        pieces.append(piece)
    return jnp.concatenate(pieces, axis=0)[None, None], pk[0, 0]


def solution(mesh):
    bits = mesh.shape["leaf"].bit_length() - 1
    leaf_bits = tuple(f"leaf{b}" for b in reversed(range(bits)))
    fine = Mesh(mesh.devices.reshape((2,) * bits + (mesh.shape["front"],)), leaf_bits + ("front",))
    placed = (
        P(leaf_bits, "front", None),
        P(leaf_bits, "front", None, None),
        P(leaf_bits, "front", None, None),
        P(leaf_bits, "front", None),
        P(),
    )
    return jax.shard_map(
        functools.partial(body, leaf_bits),
        mesh=fine,
        in_specs=placed,
        out_specs=(P(leaf_bits, "front", None, None), P()),
        check_vma=False,
    )
```

```python
import functools

import jax
import jax.numpy as jnp
from jax import lax
from jax.experimental import pallas as pl
from jax.experimental.pallas import tpu as pltpu
from jax.sharding import Mesh, PartitionSpec as P

SEP = 512
BND = 512
WIDTH = SEP + BND
KC = 128
T = 128
NB = SEP // T
TILE = 256
NPACK = NB * (NB + 1) // 2
F32 = jnp.float32
BF16 = jnp.bfloat16
VMEM_LIMIT = 50 * 1024 * 1024


def pack_index(i, j):
    return i * (i + 1) // 2 + j


def split(x):
    hi = x.astype(BF16)
    return hi, (x - hi.astype(F32)).astype(BF16)


def dot_nt(a, b):
    return lax.dot_general(a, b, (((1,), (1,)), ((), ())), preferred_element_type=F32)


def dot_nn(a, b):
    return lax.dot_general(a, b, (((1,), (0,)), ((), ())), preferred_element_type=F32)


def mm_nt(a, b):
    a_hi, a_lo = split(a)
    b_hi, b_lo = split(b)
    return dot_nt(a_hi, b_hi) + (dot_nt(a_hi, b_lo) + dot_nt(a_lo, b_hi))


def iota2(shape, dim):
    return lax.broadcasted_iota(jnp.int32, shape, dim)


def tri_sym(block):
    n = block.shape[0]
    rows, cols = iota2((n, n), 0), iota2((n, n), 1)
    low = jnp.where(cols <= rows, block, 0.0)
    strict = jnp.where(cols < rows, block, 0.0)
    return low + strict.T


def row_of(x, k):
    return jnp.broadcast_to(x[k : k + 1], (8, T))


def lane_of(x, k):
    return jnp.broadcast_to(x[:, k : k + 1], (8, T))


def tree_sum(terms):
    while len(terms) > 1:
        terms = [sum(terms[i : i + 2][1:], terms[i]) for i in range(0, len(terms), 2)]
    return terms[0]


def chol_and_inverse(sym):
    lane, sub = iota2((8, T), 1), iota2((8, T), 0)
    groups = [sym[8 * g : 8 * g + 8] for g in range(T // 8)]
    upper_rows, inv_rows = [], []
    for s in range(T // 8):
        c = 8 * s
        panel = groups[s]
        inside = (lane >= c) & (lane < c + 8)
        lanes = [lane_of(panel, c + m) for m in range(8)]
        d = {(i, m): row_of(lanes[m], i) for m in range(8) for i in range(m + 1)}
        aug = jnp.where(inside, jnp.where(lane - c == sub, 1.0, 0.0), panel)
        rows = [row_of(aug, k) for k in range(8)]
        mult, recips = {}, []
        upper_acc = jnp.zeros((8, T), F32)
        inv_acc = jnp.zeros((8, T), F32)
        for k in range(8):
            root = lax.rsqrt(d[k, k])
            recip = root * root
            recips.append(recip)
            for i in range(k + 1, 8):
                for m in range(i, 8):
                    d[i, m] = d[i, m] - (d[k, i] * d[k, m]) * recip
            for i in range(k + 1, 8):
                mult[k, i] = d[k, i] * recip
                rows[i] = rows[i] - mult[k, i] * rows[k]
            line = rows[k]
            inv_acc = jnp.where(sub == k, line * root, inv_acc)
            for m in range(k, 8):
                line = jnp.where(lane == c + m, d[k, m], line)
            upper_acc = jnp.where(sub == k, line * root, upper_acc)
        upper_rows.append(jnp.where(lane >= c + sub, upper_acc, 0.0))
        inv_rows.append(jnp.where(lane <= c + sub, inv_acc, 0.0))
        sol = [None] * 8
        for k in reversed(range(8)):
            x = rows[k] * recips[k]
            for m in reversed(range(k + 1, 8)):
                x = x - mult[k, m] * sol[m]
            sol[k] = x
        for g in range(s + 1, T // 8):
            old = groups[g]
            groups[g] = jnp.where(inside, 0.0, old) - tree_sum([lane_of(old, c + k) * sol[k] for k in range(8)])
    return jnp.concatenate(upper_rows, axis=0), jnp.concatenate(inv_rows, axis=0)


def factor_panel(f_ref, x_ref, log_ref, rows, blocks):
    width = blocks * T
    log_ref[...] = jnp.zeros_like(log_ref)

    @pl.loop(0, blocks)
    def _(j):
        at = pl.multiple_of(j * T, T)
        upper, inv = chol_and_inverse(tri_sym(f_ref[pl.ds(at, T), pl.ds(at, T)]))
        f_ref[pl.ds(at, T), pl.ds(at, T)] = upper.T
        x_ref[pl.ds(at, T), :] = inv
        eye = iota2((T, T), 0) == iota2((T, T), 1)
        diag = jnp.sum(jnp.where(eye, upper, 0.0), axis=0, keepdims=True)
        log_ref[0:1, :] += jnp.log(diag)
        for k in range(blocks):
            first = (k + 1) * T
            if first >= rows:
                continue

            @pl.when(j == k)
            def _():
                below = mm_nt(f_ref[first:rows, k * T : first], inv)
                f_ref[first:rows, k * T : first] = below
                if first < width:
                    f_ref[first:rows, first:width] -= mm_nt(below, below[: width - first])


def zero_above(f_ref, blocks):
    for i in range(blocks - 1):
        f_ref[i * T : (i + 1) * T, (i + 1) * T : blocks * T] = jnp.zeros((T, (blocks - 1 - i) * T), F32)


def log_total(log_ref):
    return 2.0 * jnp.sum(log_ref[0:1, :], axis=1, keepdims=True)


def write_own(out_ref, f_ref, start):
    size = out_ref.shape[0]
    if size % 8 == 0:
        out_ref[...] = f_ref[pl.ds(pl.multiple_of(start, 8), size), 0:SEP]
    else:
        base = pl.multiple_of(start // 8 * 8, 8)
        block = f_ref[pl.ds(base, 8), 0:SEP]
        offset = start - base
        piece = block[0:size]
        for shift in range(size, 8, size):
            piece = jnp.where(offset == shift, block[shift : shift + size], piece)
        out_ref[...] = piece


def write_update(pk_ref, below, tail_of, log_value):
    hi, lo = split(below)
    rows, cols = iota2((T, T), 0), iota2((T, T), 1)
    for i in range(NB):
        here = slice(i * T, (i + 1) * T)
        upto = slice(0, (i + 1) * T)
        prod = dot_nt(hi[here], hi[upto]) + (dot_nt(hi[here], lo[upto]) + dot_nt(lo[here], hi[upto]))
        for j in range(i + 1):
            block = tail_of(i, j) - prod[:, j * T : (j + 1) * T]
            if i == 0:
                block = jnp.where((rows == 0) & (cols == T - 1), log_value, block)
            pk_ref[pack_index(i, j)] = block


def place(pieces, work, front, want_tail, skip=0):
    count = len(pieces)
    half = count // 2
    size = pieces[0].shape[0]
    for m, piece in enumerate(pieces):
        source = front ^ m

        @pl.when(((source >= half) == want_tail) & ((source & (half - 1)) * size >= skip))
        def _():
            at = pl.multiple_of((source & (half - 1)) * size - skip, 8)
            work[pl.ds(at, size), :] = piece[...]


def first_kernel(n, pos_ref, *refs):
    pieces, (fac_ref, x_ref, log_ref) = refs[:n], refs[n:]
    place(pieces, fac_ref, pos_ref[1], False)
    factor_panel(fac_ref, x_ref, log_ref, SEP, NB // 2)
    zero_above(fac_ref, NB // 2)


def second_kernel(n, pos_ref, first_ref, *refs):
    pieces, (fac_ref, x_ref, log_ref) = refs[:n], refs[n:]
    place(pieces, fac_ref, pos_ref[1], False, SEP // 2)
    left = first_ref[SEP // 2 :, :]
    fac_ref[...] -= mm_nt(left, left)
    factor_panel(fac_ref, x_ref, log_ref, SEP // 2, NB // 2)
    zero_above(fac_ref, NB // 2)


def leaf_kernel(n, pos_ref, fac1, x1, log1, fac2, x2, log2, *refs):
    pieces1, pieces2, tails = refs[:n], refs[n : 2 * n], refs[2 * n : 2 * n + n // 2]
    own_ref, pk_ref, work, tail_ref, stack = refs[2 * n + n // 2 :]
    front = pos_ref[1]
    half = n // 2
    middle = SEP // 2
    place(pieces1, work.at[:, 0:middle], front, True)
    place(pieces2, work.at[:, middle:SEP], front, True)
    for m, piece in enumerate(tails):
        at = pl.multiple_of(((front ^ m) & (half - 1)) * piece.shape[0], 8)
        tail_ref[pl.ds(at, piece.shape[0]), :] = piece[...]
    stack[0:SEP, 0:middle] = fac1[...]
    stack[0:middle, middle:SEP] = jnp.zeros((middle, middle), F32)
    stack[middle:SEP, middle:SEP] = fac2[...]
    for j in range(NB):
        here = slice(j * T, (j + 1) * T)
        inv = x1[here, :] if j < NB // 2 else x2[j * T - middle : (j + 1) * T - middle, :]
        solved = mm_nt(work[:, here], inv)
        work[:, here] = solved
        if j + 1 < NB:
            rest = slice((j + 1) * T, SEP)
            work[:, rest] -= mm_nt(solved, stack[rest, here])
    stack[SEP:, :] = work[...]
    write_own(own_ref, stack, front * own_ref.shape[0])

    def tail_of(i, j):
        return tail_ref[i * T : (i + 1) * T, j * T : (j + 1) * T]

    write_update(pk_ref, work[...], tail_of, log_total(log1) + log_total(log2))


def expand(pk_ref, u_hi, u_lo):
    rows, cols = iota2((T, T), 0), iota2((T, T), 1)
    for i in range(NB):
        for j in range(i + 1):
            block = pk_ref[pack_index(i, j)]
            if i == j:
                low = jnp.where(cols <= rows, block, 0.0)
                block = low + jnp.where(cols < rows, block, 0.0).T
            hi, lo = split(block)
            u_hi[i * T : (i + 1) * T, j * T : (j + 1) * T] = hi
            u_lo[i * T : (i + 1) * T, j * T : (j + 1) * T] = lo
            if i != j:
                hi, lo = split(block.T)
                u_hi[j * T : (j + 1) * T, i * T : (i + 1) * T] = hi
                u_lo[j * T : (j + 1) * T, i * T : (i + 1) * T] = lo


def extend_add(pk_ref, index_row, base_of, last, f_ref, u_hi, u_lo, hot, y_hi, y_lo):
    expand(pk_ref, u_hi, u_lo)

    @pl.loop(0, WIDTH // TILE)
    def _(tile):
        at = pl.multiple_of(tile * TILE, TILE)
        ids = iota2((TILE, BND), 0) + at
        match = jnp.where(ids == index_row, 1.0, 0.0).astype(BF16)
        hot[pl.ds(at, TILE), :] = match
        y_hi[pl.ds(at, TILE), :] = dot_nn(match, u_hi[...]).astype(BF16)
        y_lo[pl.ds(at, TILE), :] = dot_nn(match, u_lo[...]).astype(BF16)

    for a in range(WIDTH // TILE):
        here = slice(a * TILE, (a + 1) * TILE)
        for b in range(a + 1):
            if last and b * TILE >= SEP:
                continue
            there = slice(b * TILE, (b + 1) * TILE)
            part = dot_nt(y_hi[here, :], hot[there, :]) + dot_nt(y_lo[here, :], hot[there, :])
            f_ref[here, there] = base_of(a, b) + part


def map_row(level, n_leaf, pos_ref, maps_ref, sibling):
    base = 2 * n_leaf - 2 * (n_leaf >> (level - 1))
    own = pos_ref[0] >> (level - 1)
    number = base + (own ^ 1 if sibling else own)
    return maps_ref[pl.ds(number, 1), :]


def own_kernel(level, n_leaf, last, pos_ref, lists_ref, pk_ref, maps_ref, f_ref, dense, u_hi, u_lo, hot, y_hi, y_lo):
    densify(lists_ref, dense)
    index_row = map_row(level, n_leaf, pos_ref, maps_ref, False)

    def base_of(a, b):
        per = TILE // T
        return jnp.concatenate(
            [dense[(b * per + h) * WIDTH + a * TILE : (b * per + h) * WIDTH + (a + 1) * TILE, :] for h in range(per)],
            axis=1,
        )

    extend_add(pk_ref, index_row, base_of, last, f_ref, u_hi, u_lo, hot, y_hi, y_lo)
    size = lists_ref.shape[1] - 8
    rows, cols = iota2((T, T), 0), iota2((T, T), 1)
    for d in range((SEP if last else WIDTH) // T):
        diag = jnp.zeros((1, T), F32)
        for rank in range(d * T // size, (d + 1) * T // size):
            diag = diag + lists_ref[rank, size : size + 1, 0:T]
        spot = slice(d * T, (d + 1) * T)
        f_ref[spot, spot] += jnp.where(rows == cols, diag, 0.0)


def level_kernel(
    level, n_leaf, n_front, last,
    pos_ref, base_ref, own_pk, sib_pk, maps_ref,
    own_ref, next_ref,
    f_ref, x_ref, log_ref, u_hi, u_lo, hot, y_hi, y_lo,
):
    index_row = map_row(level, n_leaf, pos_ref, maps_ref, True)

    def base_of(a, b):
        return base_ref[a * TILE : (a + 1) * TILE, b * TILE : (b + 1) * TILE]

    extend_add(sib_pk, index_row, base_of, last, f_ref, u_hi, u_lo, hot, y_hi, y_lo)
    factor_panel(f_ref, x_ref, log_ref, WIDTH, NB)
    zero_above(f_ref, NB)
    rank = (pos_ref[0] & ((1 << level) - 1)) * n_front + pos_ref[1]
    write_own(own_ref, f_ref, rank * own_ref.shape[0])
    kids_log = own_pk[0][0:1, T - 1 : T] + sib_pk[0][0:1, T - 1 : T]
    log_value = kids_log + log_total(log_ref)
    if last:
        next_ref[...] = jnp.broadcast_to(log_value, next_ref.shape)
    else:

        def tail_of(i, j):
            return f_ref[SEP + i * T : SEP + (i + 1) * T, SEP + j * T : SEP + (j + 1) * T]

        write_update(next_ref, f_ref[SEP:, 0:SEP], tail_of, log_value)


def densify(lists_ref, out_ref):
    block_ids = iota2((8, KC), 0).astype(F32)
    column_ids = [(iota2((16, KC), 0) + 16 * j).astype(F32).astype(BF16) for j in range(T // 16)]
    one, zero = jnp.ones((16, KC), BF16), jnp.zeros((16, KC), BF16)
    size = lists_ref.shape[1] - 8
    step = min(size, 32)

    @pl.loop(0, WIDTH // step)
    def _(turn):
        start = turn * step
        rank = start // size
        within_rank = start % size
        for g in range(step // 8):
            at = pl.multiple_of(within_rank + g * 8, 8)
            cols = lists_ref[rank, pl.ds(at, 8), 0:KC]
            vals = lists_ref[rank, pl.ds(at, 8), KC:]
            block_no = jnp.floor(cols * (1.0 / T))
            within = cols - block_no * T
            hi = vals.astype(BF16).astype(F32)
            lo = vals - hi
            for r in range(8):
                pick = block_ids == block_no[r : r + 1]
                left = jnp.concatenate(
                    [jnp.where(pick, hi[r : r + 1], 0.0), jnp.where(pick, lo[r : r + 1], 0.0)], axis=0
                ).astype(BF16)
                column = jnp.broadcast_to(within[r : r + 1], (16, KC)).astype(BF16)
                right = jnp.concatenate([jnp.where(ids == column, one, zero) for ids in column_ids], axis=0)
                both = dot_nt(left, right)
                out_ref[pl.ds(start + g * 8 + r, 8, stride=WIDTH), :] = both[0:8] + both[8:16]


def pack_kernel(sizes, cols_ref, vals_ref, diag_ref, *out_refs):
    offset = 0
    for n, (size, out_ref) in enumerate(zip(sizes, out_refs)):
        out_ref[0:size, 0:KC] = cols_ref[offset : offset + size, :].astype(F32)
        out_ref[0:size, KC:] = vals_ref[offset : offset + size, :]
        out_ref[size : size + 8, :] = jnp.broadcast_to(diag_ref[n : n + 1, :], (8, 2 * KC))
        offset += size


def params():
    return pltpu.CompilerParams(vmem_limit_bytes=VMEM_LIMIT)


def vmem():
    return pl.BlockSpec(memory_space=pltpu.VMEM)


def smem():
    return pl.BlockSpec(memory_space=pltpu.SMEM)


def shape(*dims):
    return jax.ShapeDtypeStruct(dims, F32)


def cost(us):
    return pl.CostEstimate(flops=0, bytes_accessed=int(us * 3.0e6), transcendentals=0)


def call(kernel, out_shape, n_args, n_smem, scratch, us, name):
    outs = out_shape if isinstance(out_shape, tuple) else (out_shape,)
    return pl.pallas_call(
        kernel,
        out_shape=out_shape,
        in_specs=[smem()] * n_smem + [vmem()] * (n_args - n_smem),
        out_specs=(vmem(),) * len(outs) if isinstance(out_shape, tuple) else vmem(),
        scratch_shapes=scratch,
        compiler_params=params(),
        cost_estimate=cost(us),
        name=name,
    )


def extend_scratch():
    return [pltpu.VMEM((BND, BND), BF16)] * 2 + [pltpu.VMEM((WIDTH, BND), BF16)] * 3


def swap_front(x, mask):
    count = lax.axis_size("front")
    return lax.ppermute(x, "front", [(f, f ^ mask) for f in range(count)])


def hypercube(strip, masks):
    pieces = {0: strip}
    for mask in masks:
        for m in sorted(pieces):
            pieces[m | mask] = swap_front(pieces[m], mask)
    return [pieces[m] for m in range(len(pieces))]


def after(x, done):
    return lax.optimization_barrier((x, done))[0]


def body(leaf_bits, leaf_fronts, coupling_cols, coupling_vals, sep_diag, child_maps):
    n_front = lax.axis_size("front")
    bits = len(leaf_bits)
    n_leaf = 1 << bits
    front = lax.axis_index("front")
    leaf = lax.axis_index(leaf_bits)
    pos = jnp.stack([leaf, front]).astype(jnp.int32)
    strip = leaf_fronts[0]
    half = n_front // 2
    inner = [1 << b for b in range(half.bit_length() - 1)]
    masks = [half] + inner
    middle = SEP // 2

    first = hypercube(strip[:, :middle], masks)
    held = after(strip[:, middle:], first[-1])
    second_strip = held[:, : SEP - middle]
    second = [second_strip] + [swap_front(second_strip, m) for m in range(1, n_front)]
    tail_strip = held[:, SEP - middle :]
    sent = lax.ppermute(tail_strip, "front", [(f, f - half) for f in range(half, n_front)])

    coupling_cols, coupling_vals, sep_diag, _ = lax.optimization_barrier(
        (coupling_cols, coupling_vals, sep_diag, first[half])
    )
    sizes = [WIDTH // (n_front << level) for level in range(1, bits + 1)]
    diag_rows, offset = [], 0
    for n, size in enumerate(sizes):
        rank = (leaf & ((2 << n) - 1)) * n_front + front
        spread = jnp.tile(sep_diag[0, 0, offset : offset + size], T // size)
        mine = jnp.arange(T) // size == rank % (T // size)
        diag_rows.append(jnp.pad(jnp.where(mine, spread, 0.0), (0, 2 * KC - T)))
        offset += size
    diag_rows = jnp.pad(jnp.stack(diag_rows), ((0, -len(sizes) % 8), (0, 0)))
    packed = call(
        functools.partial(pack_kernel, sizes),
        tuple(shape(size + 8, 2 * KC) for size in sizes), 3, 0, [], 1, "pack_lists",
    )(coupling_cols[0, 0], coupling_vals[0, 0], diag_rows)
    lists = []
    for n, size in enumerate(sizes):
        gathered = lax.all_gather(packed[n], leaf_bits[bits - 1 - n :] + ("front",), axis=0, tiled=False)
        if size < 8:
            rows = gathered[:, :size].reshape(WIDTH // 8, 8, 2 * KC)
            diag = gathered[:, size].reshape(WIDTH // 8, 8 // size, 2 * KC).sum(1, keepdims=True)
            gathered = jnp.concatenate([rows, jnp.pad(diag, ((0, 0), (0, 7), (0, 0)))], axis=1)
        lists.append(gathered)

    fac1, x1, log1 = call(
        functools.partial(first_kernel, n_front),
        (shape(SEP, middle), shape(middle, T), shape(8, T)), 1 + n_front, 1, [], 10, "first_half",
    )(pos, *first)
    tails = hypercube(jnp.where(front >= half, tail_strip, after(sent, fac1)), inner)
    fac2, x2, log2 = call(
        functools.partial(second_kernel, n_front),
        (shape(middle, middle), shape(middle, T), shape(8, T)), 2 + n_front, 1, [], 10, "second_half",
    )(pos, fac1, *second)
    piece, pk = call(
        functools.partial(leaf_kernel, n_front),
        (shape(WIDTH // n_front, SEP), shape(NPACK, T, T)), 7 + 2 * n_front + half, 1,
        [pltpu.VMEM((BND, SEP), F32), pltpu.VMEM((BND, BND), F32), pltpu.VMEM((WIDTH, SEP), F32)],
        5, "leaf_update",
    )(pos, fac1, x1, log1, fac2, x2, log2, *first, *second, *tails)
    pieces = [piece]
    for level in range(1, bits + 1):
        size = sizes[level - 1]
        last = level == bits
        sib = lax.ppermute(pk, leaf_bits[bits - level], [(0, 1), (1, 0)])
        base = call(
            functools.partial(own_kernel, level, n_leaf, last), shape(WIDTH, WIDTH), 4, 1,
            [pltpu.VMEM((WIDTH // T * WIDTH, T), F32)] + extend_scratch(), 17, "own_child",
        )(pos, lists[level - 1], pk, child_maps)
        piece, pk = call(
            functools.partial(level_kernel, level, n_leaf, n_front, last),
            (shape(size, SEP), shape(8, T) if last else shape(NPACK, T, T)), 5, 1,
            [pltpu.VMEM((WIDTH, WIDTH), F32), pltpu.VMEM((SEP, T), F32), pltpu.VMEM((8, T), F32)] + extend_scratch(),
            27, "level_front",
        )(pos, base, pk, sib, child_maps)
        pieces.append(piece)
    return jnp.concatenate(pieces, axis=0)[None, None], pk[0, 0]


def solution(mesh):
    bits = mesh.shape["leaf"].bit_length() - 1
    leaf_bits = tuple(f"leaf{b}" for b in reversed(range(bits)))
    fine = Mesh(mesh.devices.reshape((2,) * bits + (mesh.shape["front"],)), leaf_bits + ("front",))
    placed = (
        P(leaf_bits, "front", None),
        P(leaf_bits, "front", None, None),
        P(leaf_bits, "front", None, None),
        P(leaf_bits, "front", None),
        P(),
    )
    return jax.shard_map(
        functools.partial(body, leaf_bits),
        mesh=fine,
        in_specs=placed,
        out_specs=(P(leaf_bits, "front", None, None), P()),
        check_vma=False,
    )
```

```python
import functools

import jax
import jax.numpy as jnp
from jax import lax
from jax.experimental import pallas as pl
from jax.experimental.pallas import tpu as pltpu
from jax.sharding import Mesh, PartitionSpec as P

SEP = 512
BND = 512
WIDTH = SEP + BND
KC = 128
T = 128
NB = SEP // T
PANEL = 32
TILE = 256
NPACK = NB * (NB + 1) // 2
F32 = jnp.float32
BF16 = jnp.bfloat16
VMEM_LIMIT = 50 * 1024 * 1024


def pack_index(i, j):
    return i * (i + 1) // 2 + j


def split(x):
    hi = x.astype(BF16)
    return hi, (x - hi.astype(F32)).astype(BF16)


def dot_nt(a, b):
    return lax.dot_general(a, b, (((1,), (1,)), ((), ())), preferred_element_type=F32)


def dot_nn(a, b):
    return lax.dot_general(a, b, (((1,), (0,)), ((), ())), preferred_element_type=F32)


def mm_nt(a, b):
    a_hi, a_lo = split(a)
    b_hi, b_lo = split(b)
    return dot_nt(a_hi, b_hi) + (dot_nt(a_hi, b_lo) + dot_nt(a_lo, b_hi))


def iota2(shape, dim):
    return lax.broadcasted_iota(jnp.int32, shape, dim)


def tri_sym(block):
    n = block.shape[0]
    rows, cols = iota2((n, n), 0), iota2((n, n), 1)
    low = jnp.where(cols <= rows, block, 0.0)
    strict = jnp.where(cols < rows, block, 0.0)
    return low + strict.T


def row_of(x, k):
    return jnp.broadcast_to(x[k : k + 1], (8, T))


def lane_of(x, k):
    return jnp.broadcast_to(x[:, k : k + 1], (8, T))


def tree_sum(terms):
    while len(terms) > 1:
        terms = [sum(terms[i : i + 2][1:], terms[i]) for i in range(0, len(terms), 2)]
    return terms[0]


def eliminate_eight(groups, s, c, keep, lane, sub, tmp_ref):
    panel = groups[s]
    inside = (lane >= c) & (lane < c + 8)
    base = c * 9
    for m in range(8):
        tmp_ref[base + 8 * m : base + 8 * m + 8, :] = lane_of(panel, c + m)
    tmp_ref[base + 64 : base + 72, :] = jnp.where(inside, jnp.where(lane - c == sub, 1.0, 0.0), panel)

    def row(n):
        return jnp.broadcast_to(tmp_ref[base + n : base + n + 1, :], (8, T))

    d = {(i, m): row(8 * m + i) for m in range(8) for i in range(m + 1)}
    rows = [row(64 + k) for k in range(8)]
    mult, recips = {}, []
    upper_acc = jnp.zeros((8, T), F32)
    inv_acc = jnp.zeros((8, T), F32)
    for k in range(8):
        root = lax.rsqrt(d[k, k])
        recip = root * root
        recips.append(recip)
        for i in range(k + 1, 8):
            for m in range(i, 8):
                d[i, m] = d[i, m] - (d[k, i] * d[k, m]) * recip
        for i in range(k + 1, 8):
            mult[k, i] = d[k, i] * recip
            rows[i] = rows[i] - mult[k, i] * rows[k]
        line = rows[k]
        inv_acc = jnp.where(sub == k, line * root, inv_acc)
        for m in range(k, 8):
            line = jnp.where(lane == c + m, d[k, m], line)
        upper_acc = jnp.where(sub == k, line * root, upper_acc)
    if s + 1 < keep:
        sol = [None] * 8
        for k in reversed(range(8)):
            x = rows[k] * recips[k]
            for m in reversed(range(k + 1, 8)):
                x = x - mult[k, m] * sol[m]
            sol[k] = x
        for g in range(s + 1, keep):
            old = groups[g]
            groups[g] = jnp.where(inside, 0.0, old) - tree_sum([lane_of(old, c + k) * sol[k] for k in range(8)])
    return jnp.where(lane >= c + sub, upper_acc, 0.0), jnp.where(lane <= c + sub, inv_acc, 0.0)


def chol_and_inverse(sym, tmp_ref):
    lane, sub = iota2((8, T), 1), iota2((8, T), 0)
    per = PANEL // 8
    groups = [sym[8 * g : 8 * g + 8] for g in range(T // 8)]
    upper_rows, inv_rows = [], []
    for p in range(T // PANEL):
        for s in range(p * per, (p + 1) * per):
            upper, inv = eliminate_eight(groups, s, 8 * s, (p + 1) * per, lane, sub, tmp_ref)
            upper_rows.append(upper)
            inv_rows.append(inv)
        end = (p + 1) * PANEL
        if end < T:
            both = jnp.concatenate(
                [jnp.where(lane < end, inv_rows[s], upper_rows[s]) for s in range(p * per, (p + 1) * per)], axis=0
            )
            hi, lo = split(both)
            product = lax.dot_general(
                jnp.concatenate([hi, lo, hi], axis=0), jnp.concatenate([hi, hi, lo], axis=0),
                (((0,), (0,)), ((), ())), preferred_element_type=F32,
            )
            done = (lane >= p * PANEL) & (lane < end)
            for g in range((p + 1) * per, T // 8):
                groups[g] = jnp.where(done, 0.0, groups[g]) - product[8 * g : 8 * g + 8]
    return jnp.concatenate(upper_rows, axis=0), jnp.concatenate(inv_rows, axis=0)


def factor_panel(f_ref, x_ref, log_ref, tmp_ref, rows, blocks):
    width = blocks * T
    log_ref[...] = jnp.zeros_like(log_ref)

    @pl.loop(0, blocks)
    def _(j):
        at = pl.multiple_of(j * T, T)
        upper, inv = chol_and_inverse(tri_sym(f_ref[pl.ds(at, T), pl.ds(at, T)]), tmp_ref)
        f_ref[pl.ds(at, T), pl.ds(at, T)] = upper.T
        x_ref[pl.ds(at, T), :] = inv
        eye = iota2((T, T), 0) == iota2((T, T), 1)
        diag = jnp.sum(jnp.where(eye, upper, 0.0), axis=0, keepdims=True)
        log_ref[0:1, :] += jnp.log(diag)
        for k in range(blocks):
            first = (k + 1) * T
            if first >= rows:
                continue

            @pl.when(j == k)
            def _():
                below = mm_nt(f_ref[first:rows, k * T : first], inv)
                f_ref[first:rows, k * T : first] = below
                if first < width:
                    f_ref[first:rows, first:width] -= mm_nt(below, below[: width - first])


def zero_above(f_ref, blocks):
    for i in range(blocks - 1):
        f_ref[i * T : (i + 1) * T, (i + 1) * T : blocks * T] = jnp.zeros((T, (blocks - 1 - i) * T), F32)


def log_total(log_ref):
    return 2.0 * jnp.sum(log_ref[0:1, :], axis=1, keepdims=True)


def write_own(out_ref, f_ref, start):
    size = out_ref.shape[0]
    if size % 8 == 0:
        out_ref[...] = f_ref[pl.ds(pl.multiple_of(start, 8), size), 0:SEP]
    else:
        base = pl.multiple_of(start // 8 * 8, 8)
        block = f_ref[pl.ds(base, 8), 0:SEP]
        offset = start - base
        piece = block[0:size]
        for shift in range(size, 8, size):
            piece = jnp.where(offset == shift, block[shift : shift + size], piece)
        out_ref[...] = piece


def write_update(pk_ref, below, tail_of, log_value):
    hi, lo = split(below)
    rows, cols = iota2((T, T), 0), iota2((T, T), 1)
    for i in range(NB):
        here = slice(i * T, (i + 1) * T)
        upto = slice(0, (i + 1) * T)
        prod = dot_nt(hi[here], hi[upto]) + (dot_nt(hi[here], lo[upto]) + dot_nt(lo[here], hi[upto]))
        for j in range(i + 1):
            block = tail_of(i, j) - prod[:, j * T : (j + 1) * T]
            if i == 0:
                block = jnp.where((rows == 0) & (cols == T - 1), log_value, block)
            pk_ref[pack_index(i, j)] = block


def place(pieces, work, front, want_tail):
    count = len(pieces)
    half = count // 2
    size = pieces[0].shape[0]
    for m, piece in enumerate(pieces):
        source = front ^ m

        @pl.when((source >= half) == want_tail)
        def _():
            at = pl.multiple_of((source & (half - 1)) * size, 8)
            work[pl.ds(at, size), :] = piece[...]


def head_kernel(n, pos_ref, *refs):
    pieces, (fac_ref, x_ref, log_ref, tmp_ref) = refs[:n], refs[n:]
    place(pieces, fac_ref, pos_ref[1], False)
    factor_panel(fac_ref, x_ref, log_ref, tmp_ref, SEP, NB)
    zero_above(fac_ref, NB)


def below_kernel(n, pos_ref, fac, inv, *refs):
    pieces, (own_ref, below_ref, stack) = refs[:n], refs[n:]
    front = pos_ref[1]
    place(pieces, below_ref, front, True)
    for j in range(NB):
        here = slice(j * T, (j + 1) * T)
        solved = mm_nt(below_ref[:, here], inv[here, :])
        below_ref[:, here] = solved
        if j + 1 < NB:
            rest = slice((j + 1) * T, SEP)
            below_ref[:, rest] -= mm_nt(solved, fac[rest, here])
    stack[0:SEP, :] = fac[...]
    stack[SEP:, :] = below_ref[...]
    write_own(own_ref, stack, front * own_ref.shape[0])


def update_kernel(n, pos_ref, below_ref, log_ref, *refs):
    pieces, (pk_ref, tail_ref) = refs[:n], refs[n:]
    place(pieces, tail_ref, pos_ref[1], True)

    def tail_of(i, j):
        return tail_ref[i * T : (i + 1) * T, j * T : (j + 1) * T]

    write_update(pk_ref, below_ref[...], tail_of, log_total(log_ref))


def expand(pk_ref, u_hi, u_lo):
    rows, cols = iota2((T, T), 0), iota2((T, T), 1)
    for i in range(NB):
        for j in range(i + 1):
            block = pk_ref[pack_index(i, j)]
            if i == j:
                low = jnp.where(cols <= rows, block, 0.0)
                block = low + jnp.where(cols < rows, block, 0.0).T
            hi, lo = split(block)
            u_hi[i * T : (i + 1) * T, j * T : (j + 1) * T] = hi
            u_lo[i * T : (i + 1) * T, j * T : (j + 1) * T] = lo
            if i != j:
                hi, lo = split(block.T)
                u_hi[j * T : (j + 1) * T, i * T : (i + 1) * T] = hi
                u_lo[j * T : (j + 1) * T, i * T : (i + 1) * T] = lo


def extend_add(pk_ref, index_row, base_of, last, f_ref, u_hi, u_lo, hot, y_hi, y_lo):
    expand(pk_ref, u_hi, u_lo)

    @pl.loop(0, WIDTH // TILE)
    def _(tile):
        at = pl.multiple_of(tile * TILE, TILE)
        ids = iota2((TILE, BND), 0) + at
        match = jnp.where(ids == index_row, 1.0, 0.0).astype(BF16)
        hot[pl.ds(at, TILE), :] = match
        y_hi[pl.ds(at, TILE), :] = dot_nn(match, u_hi[...]).astype(BF16)
        y_lo[pl.ds(at, TILE), :] = dot_nn(match, u_lo[...]).astype(BF16)

    for a in range(WIDTH // TILE):
        here = slice(a * TILE, (a + 1) * TILE)
        for b in range(a + 1):
            if last and b * TILE >= SEP:
                continue
            there = slice(b * TILE, (b + 1) * TILE)
            part = dot_nt(y_hi[here, :], hot[there, :]) + dot_nt(y_lo[here, :], hot[there, :])
            f_ref[here, there] = base_of(a, b) + part


def map_row(level, n_leaf, pos_ref, maps_ref, sibling):
    base = 2 * n_leaf - 2 * (n_leaf >> (level - 1))
    own = pos_ref[0] >> (level - 1)
    number = base + (own ^ 1 if sibling else own)
    return maps_ref[pl.ds(number, 1), :]


def own_kernel(level, n_leaf, last, pos_ref, lists_ref, pk_ref, maps_ref, f_ref, dense, u_hi, u_lo, hot, y_hi, y_lo):
    densify(lists_ref, dense)
    index_row = map_row(level, n_leaf, pos_ref, maps_ref, False)

    def base_of(a, b):
        per = TILE // T
        return jnp.concatenate(
            [dense[(b * per + h) * WIDTH + a * TILE : (b * per + h) * WIDTH + (a + 1) * TILE, :] for h in range(per)],
            axis=1,
        )

    extend_add(pk_ref, index_row, base_of, last, f_ref, u_hi, u_lo, hot, y_hi, y_lo)
    size = lists_ref.shape[1] - 8
    rows, cols = iota2((T, T), 0), iota2((T, T), 1)
    for d in range((SEP if last else WIDTH) // T):
        diag = jnp.zeros((1, T), F32)
        for rank in range(d * T // size, (d + 1) * T // size):
            diag = diag + lists_ref[rank, size : size + 1, 0:T]
        spot = slice(d * T, (d + 1) * T)
        f_ref[spot, spot] += jnp.where(rows == cols, diag, 0.0)


def level_kernel(
    level, n_leaf, n_front, last,
    pos_ref, base_ref, own_pk, sib_pk, maps_ref,
    own_ref, next_ref,
    f_ref, x_ref, log_ref, tmp_ref, u_hi, u_lo, hot, y_hi, y_lo,
):
    index_row = map_row(level, n_leaf, pos_ref, maps_ref, True)

    def base_of(a, b):
        return base_ref[a * TILE : (a + 1) * TILE, b * TILE : (b + 1) * TILE]

    extend_add(sib_pk, index_row, base_of, last, f_ref, u_hi, u_lo, hot, y_hi, y_lo)
    factor_panel(f_ref, x_ref, log_ref, tmp_ref, WIDTH, NB)
    zero_above(f_ref, NB)
    rank = (pos_ref[0] & ((1 << level) - 1)) * n_front + pos_ref[1]
    write_own(own_ref, f_ref, rank * own_ref.shape[0])
    kids_log = own_pk[0][0:1, T - 1 : T] + sib_pk[0][0:1, T - 1 : T]
    log_value = kids_log + log_total(log_ref)
    if last:
        next_ref[...] = jnp.broadcast_to(log_value, next_ref.shape)
    else:

        def tail_of(i, j):
            return f_ref[SEP + i * T : SEP + (i + 1) * T, SEP + j * T : SEP + (j + 1) * T]

        write_update(next_ref, f_ref[SEP:, 0:SEP], tail_of, log_value)


def densify(lists_ref, out_ref):
    block_ids = iota2((8, KC), 0).astype(F32)
    column_ids = [(iota2((16, KC), 0) + 16 * j).astype(F32).astype(BF16) for j in range(T // 16)]
    one, zero = jnp.ones((16, KC), BF16), jnp.zeros((16, KC), BF16)
    blank = jnp.zeros((8, KC), F32)
    pair_of = iota2((T, T), 1) % 64 // 16
    size = lists_ref.shape[1] - 8
    step = min(size, 32)

    @pl.loop(0, WIDTH // step)
    def _(turn):
        start = turn * step
        rank = start // size
        within_rank = start % size
        for g in range(step // 8):
            hots, parts = [], ([], [])
            at = pl.multiple_of(within_rank + g * 8, 8)
            cols = lists_ref[rank, pl.ds(at, 8), 0:KC]
            vals = lists_ref[rank, pl.ds(at, 8), KC:]
            block_no = jnp.floor(cols * (1.0 / T))
            within = cols - block_no * T
            for r in range(8):
                column = row_of(within, r)
                column = jnp.concatenate([column, column], axis=0).astype(BF16)
                hots.append(jnp.concatenate([jnp.where(ids == column, one, zero) for ids in column_ids], axis=0))
                val = row_of(vals, r)
                hi = val.astype(BF16).astype(F32)
                pick = block_ids == row_of(block_no, r)
                parts[0].append(jnp.where(pick, hi, 0.0))
                parts[1].append(jnp.where(pick, val - hi, 0.0))
            held = jnp.concatenate(
                [
                    jnp.concatenate(
                        [
                            jnp.concatenate([part[r], blank] if side == 0 else [blank, part[r + 1]], axis=0).astype(BF16)
                            for part in parts
                            for r in range(0, 8, 2)
                        ],
                        axis=0,
                    )
                    for side in range(2)
                ],
                axis=1,
            )
            total = jnp.zeros((T, T), F32)
            for pair in range(4):
                streamed = jnp.concatenate([hots[2 * pair], hots[2 * pair + 1]], axis=1)
                total = jnp.where(pair_of == pair, dot_nt(streamed, held), total)
            flipped = total.T
            dense = flipped[0:64] + flipped[64:128]
            for r in range(8):
                out_ref[pl.ds(start + g * 8 + r, 8, stride=WIDTH), :] = dense[8 * r : 8 * r + 8]


def pack_kernel(sizes, cols_ref, vals_ref, diag_ref, *out_refs):
    offset = 0
    for n, (size, out_ref) in enumerate(zip(sizes, out_refs)):
        out_ref[0:size, 0:KC] = cols_ref[offset : offset + size, :].astype(F32)
        out_ref[0:size, KC:] = vals_ref[offset : offset + size, :]
        out_ref[size : size + 8, :] = jnp.broadcast_to(diag_ref[n : n + 1, :], (8, 2 * KC))
        offset += size


def params():
    return pltpu.CompilerParams(vmem_limit_bytes=VMEM_LIMIT)


def vmem():
    return pl.BlockSpec(memory_space=pltpu.VMEM)


def smem():
    return pl.BlockSpec(memory_space=pltpu.SMEM)


def shape(*dims):
    return jax.ShapeDtypeStruct(dims, F32)


def cost(us):
    return pl.CostEstimate(flops=0, bytes_accessed=int(us * 3.0e6), transcendentals=0)


def call(kernel, out_shape, n_args, n_smem, scratch, us, name):
    outs = out_shape if isinstance(out_shape, tuple) else (out_shape,)
    return pl.pallas_call(
        kernel,
        out_shape=out_shape,
        in_specs=[smem()] * n_smem + [vmem()] * (n_args - n_smem),
        out_specs=(vmem(),) * len(outs) if isinstance(out_shape, tuple) else vmem(),
        scratch_shapes=scratch,
        compiler_params=params(),
        cost_estimate=cost(us),
        name=name,
    )


def row_scratch():
    return pltpu.VMEM((9 * T, T), F32)


def extend_scratch():
    return [pltpu.VMEM((BND, BND), BF16)] * 2 + [pltpu.VMEM((WIDTH, BND), BF16)] * 3


def swap_front(x, mask):
    count = lax.axis_size("front")
    return lax.ppermute(x, "front", [(f, f ^ mask) for f in range(count)])


def hypercube(strip, masks):
    pieces = {0: strip}
    for mask in masks:
        for m in sorted(pieces):
            pieces[m | mask] = swap_front(pieces[m], mask)
    return [pieces[m] for m in range(len(pieces))]


def after(x, done):
    return lax.optimization_barrier((x, done))[0]


def body(leaf_bits, leaf_fronts, coupling_cols, coupling_vals, sep_diag, child_maps):
    n_front = lax.axis_size("front")
    bits = len(leaf_bits)
    n_leaf = 1 << bits
    front = lax.axis_index("front")
    leaf = lax.axis_index(leaf_bits)
    pos = jnp.stack([leaf, front]).astype(jnp.int32)
    strip = leaf_fronts[0]
    half = n_front // 2
    inner = [1 << b for b in range(half.bit_length() - 1)]
    strip_rows = WIDTH // n_front
    panel_strip = strip[:, :SEP]
    cross = swap_front(panel_strip, half)
    panels = hypercube(panel_strip, inner) + hypercube(cross, inner)
    strip3 = after(strip, panels[-1])[:, SEP:]
    cross3 = lax.ppermute(strip3, "front", [(f, f - half) for f in range(half, n_front)])

    coupling_cols, coupling_vals, sep_diag, _ = lax.optimization_barrier(
        (coupling_cols, coupling_vals, sep_diag, cross)
    )
    sizes = [WIDTH // (n_front << level) for level in range(1, bits + 1)]
    diag_rows, offset = [], 0
    for n, size in enumerate(sizes):
        rank = (leaf & ((2 << n) - 1)) * n_front + front
        spread = jnp.tile(sep_diag[0, 0, offset : offset + size], T // size)
        mine = jnp.arange(T) // size == rank % (T // size)
        diag_rows.append(jnp.pad(jnp.where(mine, spread, 0.0), (0, 2 * KC - T)))
        offset += size
    diag_rows = jnp.pad(jnp.stack(diag_rows), ((0, -len(sizes) % 8), (0, 0)))
    packed = call(
        functools.partial(pack_kernel, sizes),
        tuple(shape(size + 8, 2 * KC) for size in sizes), 3, 0, [], 1, "pack_lists",
    )(coupling_cols[0, 0], coupling_vals[0, 0], diag_rows)
    lists = []
    for n, size in enumerate(sizes):
        gathered = lax.all_gather(packed[n], leaf_bits[bits - 1 - n :] + ("front",), axis=0, tiled=False)
        if size < 8:
            rows = gathered[:, :size].reshape(WIDTH // 8, 8, 2 * KC)
            diag = gathered[:, size].reshape(WIDTH // 8, 8 // size, 2 * KC).sum(1, keepdims=True)
            gathered = jnp.concatenate([rows, jnp.pad(diag, ((0, 0), (0, 7), (0, 0)))], axis=1)
        lists.append(gathered)

    fac, inv, logs = call(
        functools.partial(head_kernel, n_front),
        (shape(SEP, SEP), shape(SEP, T), shape(8, T)), 1 + n_front, 1, [row_scratch()], 18, "head_factor",
    )(pos, *panels)
    pieces3 = hypercube(strip3, inner) + hypercube(after(cross3, inv), inner)
    piece, below = call(
        functools.partial(below_kernel, n_front),
        (shape(strip_rows, SEP), shape(BND, SEP)), 3 + n_front, 1, [pltpu.VMEM((WIDTH, SEP), F32)],
        4, "leaf_below",
    )(pos, fac, inv, *panels)
    pk = call(
        functools.partial(update_kernel, n_front), shape(NPACK, T, T), 3 + n_front, 1,
        [pltpu.VMEM((BND, BND), F32)], 3, "leaf_update",
    )(pos, below, logs, *pieces3)
    pieces = [piece]
    for level in range(1, bits + 1):
        size = sizes[level - 1]
        last = level == bits
        sib = lax.ppermute(pk, leaf_bits[bits - level], [(0, 1), (1, 0)])
        base = call(
            functools.partial(own_kernel, level, n_leaf, last), shape(WIDTH, WIDTH), 4, 1,
            [pltpu.VMEM((WIDTH // T * WIDTH, T), F32)] + extend_scratch(), 17, "own_child",
        )(pos, lists[level - 1], pk, child_maps)
        piece, pk = call(
            functools.partial(level_kernel, level, n_leaf, n_front, last),
            (shape(size, SEP), shape(8, T) if last else shape(NPACK, T, T)), 5, 1,
            [pltpu.VMEM((WIDTH, WIDTH), F32), pltpu.VMEM((SEP, T), F32), pltpu.VMEM((8, T), F32), row_scratch()] + extend_scratch(),
            27, "level_front",
        )(pos, base, pk, sib, child_maps)
        pieces.append(piece)
    return jnp.concatenate(pieces, axis=0)[None, None], pk[0, 0]


def solution(mesh):
    bits = mesh.shape["leaf"].bit_length() - 1
    leaf_bits = tuple(f"leaf{b}" for b in reversed(range(bits)))
    fine = Mesh(mesh.devices.reshape((2,) * bits + (mesh.shape["front"],)), leaf_bits + ("front",))
    placed = (
        P(leaf_bits, "front", None),
        P(leaf_bits, "front", None, None),
        P(leaf_bits, "front", None, None),
        P(leaf_bits, "front", None),
        P(),
    )
    return jax.shard_map(
        functools.partial(body, leaf_bits),
        mesh=fine,
        in_specs=placed,
        out_specs=(P(leaf_bits, "front", None, None), P()),
        check_vma=False,
    )
```

```python
import functools

import jax
import jax.numpy as jnp
from jax import lax
from jax.experimental import pallas as pl
from jax.experimental.pallas import tpu as pltpu
from jax.sharding import Mesh, PartitionSpec as P

SEP = 512
BND = 512
WIDTH = SEP + BND
KC = 128
T = 128
NB = SEP // T
PANEL = 32
TILE = 256
NPACK = NB * (NB + 1) // 2
F32 = jnp.float32
BF16 = jnp.bfloat16
VMEM_LIMIT = 50 * 1024 * 1024


def pack_index(i, j):
    return i * (i + 1) // 2 + j


def split(x):
    hi = x.astype(BF16)
    return hi, (x - hi.astype(F32)).astype(BF16)


def dot_nt(a, b):
    return lax.dot_general(a, b, (((1,), (1,)), ((), ())), preferred_element_type=F32)


def dot_nn(a, b):
    return lax.dot_general(a, b, (((1,), (0,)), ((), ())), preferred_element_type=F32)


def mm_nt(a, b):
    a_hi, a_lo = split(a)
    b_hi, b_lo = split(b)
    return dot_nt(a_hi, b_hi) + (dot_nt(a_hi, b_lo) + dot_nt(a_lo, b_hi))


def iota2(shape, dim):
    return lax.broadcasted_iota(jnp.int32, shape, dim)


def tri_sym(block):
    n = block.shape[0]
    rows, cols = iota2((n, n), 0), iota2((n, n), 1)
    low = jnp.where(cols <= rows, block, 0.0)
    strict = jnp.where(cols < rows, block, 0.0)
    return low + strict.T


def row_of(x, k):
    return jnp.broadcast_to(x[k : k + 1], (8, T))


def lane_of(x, k):
    return jnp.broadcast_to(x[:, k : k + 1], (8, T))


def tree_sum(terms):
    while len(terms) > 1:
        terms = [sum(terms[i : i + 2][1:], terms[i]) for i in range(0, len(terms), 2)]
    return terms[0]


def reciprocal(x):
    return pl.reciprocal(x, approx=True)


def eliminate_eight(groups, s, c, keep, lane, sub, tmp_ref):
    panel = groups[s]
    inside = (lane >= c) & (lane < c + 8)
    base = c * 9
    for m in range(8):
        tmp_ref[base + 8 * m : base + 8 * m + 8, :] = lane_of(panel, c + m)
    tmp_ref[base + 64 : base + 72, :] = jnp.where(inside, jnp.where(lane - c == sub, 1.0, 0.0), panel)

    def row(n):
        return jnp.broadcast_to(tmp_ref[base + n : base + n + 1, :], (8, T))

    d = {(i, m): row(8 * m + i) for m in range(8) for i in range(m + 1)}
    rows = [row(64 + k) for k in range(8)]
    upper_acc = jnp.zeros((8, T), F32)
    inv_acc = jnp.zeros((8, T), F32)
    to_p, to_q, first = {}, {}, {}

    def emit(k, line, entries, root):
        inv_row = line * root
        for m in range(k, 8):
            line = jnp.where(lane == c + m, entries[m], line)
        return jnp.where(sub == k, line * root, upper_acc), jnp.where(sub == k, inv_row, inv_acc)

    for p in range(0, 8, 2):
        q = p + 1
        a, b, e = d[p, p], d[p, q], d[q, q]
        det = a * e - b * b
        recip = reciprocal(det)
        rest = range(q + 1, 8)
        w = {i: e * d[p, i] - b * d[q, i] for i in rest}
        z = {i: a * d[q, i] - b * d[p, i] for i in rest}
        root_p = lax.rsqrt(a)
        inv_a = root_p * root_p
        ratio = b * inv_a
        schur = det * inv_a
        upper_acc, inv_acc = emit(p, rows[p], {m: d[p, m] for m in range(p, 8)}, root_p)
        line_q = {m: d[q, m] - ratio * d[p, m] for m in rest}
        line_q[q] = schur
        upper_acc, inv_acc = emit(q, rows[q] - ratio * rows[p], line_q, lax.rsqrt(schur))
        for i in rest:
            for m in range(i, 8):
                d[i, m] = d[i, m] - (w[i] * d[p, m] + z[i] * d[q, m]) * recip
        for i in rest:
            to_p[p, i], to_q[p, i] = w[i] * recip, z[i] * recip
            rows[i] = rows[i] - (to_p[p, i] * rows[p] + to_q[p, i] * rows[q])
        first[p] = (e * rows[p] - b * rows[q]) * recip
        first[q] = (a * rows[q] - b * rows[p]) * recip
    if s + 1 < keep:
        sol = [None] * 8
        for p in (6, 4, 2, 0):
            rest = range(p + 2, 8)
            sol[p], sol[p + 1] = first[p], first[p + 1]
            if p < 6:
                sol[p] = sol[p] - tree_sum([to_p[p, m] * sol[m] for m in rest])
                sol[p + 1] = sol[p + 1] - tree_sum([to_q[p, m] * sol[m] for m in rest])
        for g in range(s + 1, keep):
            old = groups[g]
            groups[g] = jnp.where(inside, 0.0, old) - tree_sum([lane_of(old, c + k) * sol[k] for k in range(8)])
    return jnp.where(lane >= c + sub, upper_acc, 0.0), jnp.where(lane <= c + sub, inv_acc, 0.0)


def chol_and_inverse(sym, tmp_ref):
    lane, sub = iota2((8, T), 1), iota2((8, T), 0)
    per = PANEL // 8
    diag = jnp.sum(jnp.where(iota2((T, T), 0) == iota2((T, T), 1), sym, 0.0), axis=0, keepdims=True)
    scale = jnp.broadcast_to(lax.rsqrt(diag), (T, T))
    sym = (sym * scale) * scale.T
    groups = [sym[8 * g : 8 * g + 8] for g in range(T // 8)]
    upper_rows, inv_rows = [], []
    for p in range(T // PANEL):
        for s in range(p * per, (p + 1) * per):
            upper, inv = eliminate_eight(groups, s, 8 * s, (p + 1) * per, lane, sub, tmp_ref)
            upper_rows.append(upper)
            inv_rows.append(inv)
        end = (p + 1) * PANEL
        if end < T:
            both = jnp.concatenate(
                [jnp.where(lane < end, inv_rows[s], upper_rows[s]) for s in range(p * per, (p + 1) * per)], axis=0
            )
            hi, lo = split(both)
            product = lax.dot_general(
                jnp.concatenate([hi, lo, hi], axis=0), jnp.concatenate([hi, hi, lo], axis=0),
                (((0,), (0,)), ((), ())), preferred_element_type=F32,
            )
            done = (lane >= p * PANEL) & (lane < end)
            for g in range((p + 1) * per, T // 8):
                groups[g] = jnp.where(done, 0.0, groups[g]) - product[8 * g : 8 * g + 8]
    return jnp.concatenate(upper_rows, axis=0) * (diag * scale[0:1]), jnp.concatenate(inv_rows, axis=0) * scale


def factor_panel(f_ref, x_ref, log_ref, tmp_ref, rows, blocks):
    width = blocks * T
    log_ref[...] = jnp.zeros_like(log_ref)

    @pl.loop(0, blocks)
    def _(j):
        at = pl.multiple_of(j * T, T)
        upper, inv = chol_and_inverse(tri_sym(f_ref[pl.ds(at, T), pl.ds(at, T)]), tmp_ref)
        f_ref[pl.ds(at, T), pl.ds(at, T)] = upper.T
        x_ref[pl.ds(at, T), :] = inv
        eye = iota2((T, T), 0) == iota2((T, T), 1)
        diag = jnp.sum(jnp.where(eye, upper, 0.0), axis=0, keepdims=True)
        log_ref[0:1, :] += jnp.log(diag)
        for k in range(blocks):
            first = (k + 1) * T
            if first >= rows:
                continue

            @pl.when(j == k)
            def _():
                below = mm_nt(f_ref[first:rows, k * T : first], inv)
                f_ref[first:rows, k * T : first] = below
                if first < width:
                    f_ref[first:rows, first:width] -= mm_nt(below, below[: width - first])


def zero_above(f_ref, blocks):
    for i in range(blocks - 1):
        f_ref[i * T : (i + 1) * T, (i + 1) * T : blocks * T] = jnp.zeros((T, (blocks - 1 - i) * T), F32)


def log_total(log_ref):
    return 2.0 * jnp.sum(log_ref[0:1, :], axis=1, keepdims=True)


def write_own(out_ref, f_ref, start):
    size = out_ref.shape[0]
    if size % 8 == 0:
        out_ref[...] = f_ref[pl.ds(pl.multiple_of(start, 8), size), 0:SEP]
    else:
        base = pl.multiple_of(start // 8 * 8, 8)
        block = f_ref[pl.ds(base, 8), 0:SEP]
        offset = start - base
        piece = block[0:size]
        for shift in range(size, 8, size):
            piece = jnp.where(offset == shift, block[shift : shift + size], piece)
        out_ref[...] = piece


def write_update(pk_ref, below, tail_of, log_value):
    hi, lo = split(below)
    rows, cols = iota2((T, T), 0), iota2((T, T), 1)
    for i in range(NB):
        here = slice(i * T, (i + 1) * T)
        upto = slice(0, (i + 1) * T)
        prod = dot_nt(hi[here], hi[upto]) + (dot_nt(hi[here], lo[upto]) + dot_nt(lo[here], hi[upto]))
        for j in range(i + 1):
            block = tail_of(i, j) - prod[:, j * T : (j + 1) * T]
            if i == 0:
                block = jnp.where((rows == 0) & (cols == T - 1), log_value, block)
            pk_ref[pack_index(i, j)] = block


def place(pieces, work, front, want_tail):
    count = len(pieces)
    half = count // 2
    size = pieces[0].shape[0]
    for m, piece in enumerate(pieces):
        source = front ^ m

        @pl.when((source >= half) == want_tail)
        def _():
            at = pl.multiple_of((source & (half - 1)) * size, 8)
            work[pl.ds(at, size), :] = piece[...]


def head_kernel(n, pos_ref, *refs):
    pieces1, pieces2, (fac_ref, x_ref, log_ref, tmp_ref) = refs[:n], refs[n : 2 * n], refs[2 * n :]
    place(pieces1, fac_ref.at[:, 0 : SEP // 2], pos_ref[1], False)
    place(pieces2, fac_ref.at[:, SEP // 2 : SEP], pos_ref[1], False)
    factor_panel(fac_ref, x_ref, log_ref, tmp_ref, SEP, NB)
    zero_above(fac_ref, NB)


def below_kernel(n, pos_ref, fac, inv, *refs):
    pieces1, pieces2, (own_ref, below_ref, stack) = refs[:n], refs[n : 2 * n], refs[2 * n :]
    front = pos_ref[1]
    place(pieces1, below_ref.at[:, 0 : SEP // 2], front, True)
    place(pieces2, below_ref.at[:, SEP // 2 : SEP], front, True)
    for j in range(NB):
        here = slice(j * T, (j + 1) * T)
        solved = mm_nt(below_ref[:, here], inv[here, :])
        below_ref[:, here] = solved
        if j + 1 < NB:
            rest = slice((j + 1) * T, SEP)
            below_ref[:, rest] -= mm_nt(solved, fac[rest, here])
    stack[0:SEP, :] = fac[...]
    stack[SEP:, :] = below_ref[...]
    write_own(own_ref, stack, front * own_ref.shape[0])


def update_kernel(n, pos_ref, below_ref, log_ref, *refs):
    pieces, (pk_ref, tail_ref) = refs[:n], refs[n:]
    place(pieces, tail_ref, pos_ref[1], True)

    def tail_of(i, j):
        return tail_ref[i * T : (i + 1) * T, j * T : (j + 1) * T]

    write_update(pk_ref, below_ref[...], tail_of, log_total(log_ref))


def expand(pk_ref, u_hi, u_lo):
    rows, cols = iota2((T, T), 0), iota2((T, T), 1)
    for i in range(NB):
        for j in range(i + 1):
            block = pk_ref[pack_index(i, j)]
            if i == j:
                low = jnp.where(cols <= rows, block, 0.0)
                block = low + jnp.where(cols < rows, block, 0.0).T
            hi, lo = split(block)
            u_hi[i * T : (i + 1) * T, j * T : (j + 1) * T] = hi
            u_lo[i * T : (i + 1) * T, j * T : (j + 1) * T] = lo
            if i != j:
                hi, lo = split(block.T)
                u_hi[j * T : (j + 1) * T, i * T : (i + 1) * T] = hi
                u_lo[j * T : (j + 1) * T, i * T : (i + 1) * T] = lo


def extend_add(pk_ref, index_row, base_of, last, f_ref, u_hi, u_lo, hot, y_hi, y_lo):
    expand(pk_ref, u_hi, u_lo)

    @pl.loop(0, WIDTH // TILE)
    def _(tile):
        at = pl.multiple_of(tile * TILE, TILE)
        ids = iota2((TILE, BND), 0) + at
        match = jnp.where(ids == index_row, 1.0, 0.0).astype(BF16)
        hot[pl.ds(at, TILE), :] = match
        y_hi[pl.ds(at, TILE), :] = dot_nn(match, u_hi[...]).astype(BF16)
        y_lo[pl.ds(at, TILE), :] = dot_nn(match, u_lo[...]).astype(BF16)

    for a in range(WIDTH // TILE):
        here = slice(a * TILE, (a + 1) * TILE)
        for b in range(a + 1):
            if last and b * TILE >= SEP:
                continue
            there = slice(b * TILE, (b + 1) * TILE)
            part = dot_nt(y_hi[here, :], hot[there, :]) + dot_nt(y_lo[here, :], hot[there, :])
            f_ref[here, there] = base_of(a, b) + part


def map_row(level, n_leaf, pos_ref, maps_ref, sibling):
    base = 2 * n_leaf - 2 * (n_leaf >> (level - 1))
    own = pos_ref[0] >> (level - 1)
    number = base + (own ^ 1 if sibling else own)
    return maps_ref[pl.ds(number, 1), :]


def own_kernel(level, n_leaf, last, pos_ref, lists_ref, pk_ref, maps_ref, f_ref, dense, u_hi, u_lo, hot, y_hi, y_lo):
    densify(lists_ref, dense)
    index_row = map_row(level, n_leaf, pos_ref, maps_ref, False)

    def base_of(a, b):
        per = TILE // T
        return jnp.concatenate(
            [dense[(b * per + h) * WIDTH + a * TILE : (b * per + h) * WIDTH + (a + 1) * TILE, :] for h in range(per)],
            axis=1,
        )

    extend_add(pk_ref, index_row, base_of, last, f_ref, u_hi, u_lo, hot, y_hi, y_lo)
    size = lists_ref.shape[1] - 8
    rows, cols = iota2((T, T), 0), iota2((T, T), 1)
    for d in range((SEP if last else WIDTH) // T):
        diag = jnp.zeros((1, T), F32)
        for rank in range(d * T // size, (d + 1) * T // size):
            diag = diag + lists_ref[rank, size : size + 1, 0:T]
        spot = slice(d * T, (d + 1) * T)
        f_ref[spot, spot] += jnp.where(rows == cols, diag, 0.0)


def level_kernel(
    level, n_leaf, n_front, last,
    pos_ref, base_ref, own_pk, sib_pk, maps_ref,
    own_ref, next_ref,
    f_ref, x_ref, log_ref, tmp_ref, u_hi, u_lo, hot, y_hi, y_lo,
):
    index_row = map_row(level, n_leaf, pos_ref, maps_ref, True)

    def base_of(a, b):
        return base_ref[a * TILE : (a + 1) * TILE, b * TILE : (b + 1) * TILE]

    extend_add(sib_pk, index_row, base_of, last, f_ref, u_hi, u_lo, hot, y_hi, y_lo)
    factor_panel(f_ref, x_ref, log_ref, tmp_ref, WIDTH, NB)
    zero_above(f_ref, NB)
    rank = (pos_ref[0] & ((1 << level) - 1)) * n_front + pos_ref[1]
    write_own(own_ref, f_ref, rank * own_ref.shape[0])
    kids_log = own_pk[0][0:1, T - 1 : T] + sib_pk[0][0:1, T - 1 : T]
    log_value = kids_log + log_total(log_ref)
    if last:
        next_ref[...] = jnp.broadcast_to(log_value, next_ref.shape)
    else:

        def tail_of(i, j):
            return f_ref[SEP + i * T : SEP + (i + 1) * T, SEP + j * T : SEP + (j + 1) * T]

        write_update(next_ref, f_ref[SEP:, 0:SEP], tail_of, log_value)


def densify(lists_ref, out_ref):
    block_ids = iota2((8, KC), 0).astype(F32)
    column_ids = [(iota2((16, KC), 0) + 16 * j).astype(F32).astype(BF16) for j in range(T // 16)]
    one, zero = jnp.ones((16, KC), BF16), jnp.zeros((16, KC), BF16)
    blank = jnp.zeros((8, KC), F32)
    pair_of = iota2((T, T), 1) % 64 // 16
    size = lists_ref.shape[1] - 8
    step = 128

    @pl.loop(0, WIDTH // step)
    def _(turn):
        start = turn * step
        for g in range(step // 8):
            hots, parts = [], ([], [])
            rank = (start + g * 8) // size
            at = pl.multiple_of((start + g * 8) % size, 8)
            cols = lists_ref[rank, pl.ds(at, 8), 0:KC]
            vals = lists_ref[rank, pl.ds(at, 8), KC:]
            block_no = jnp.floor(cols * (1.0 / T))
            within = cols - block_no * T
            for r in range(8):
                column = row_of(within, r)
                column = jnp.concatenate([column, column], axis=0).astype(BF16)
                hots.append(jnp.concatenate([jnp.where(ids == column, one, zero) for ids in column_ids], axis=0))
                val = row_of(vals, r)
                hi = val.astype(BF16).astype(F32)
                pick = block_ids == row_of(block_no, r)
                parts[0].append(jnp.where(pick, hi, 0.0))
                parts[1].append(jnp.where(pick, val - hi, 0.0))
            held = jnp.concatenate(
                [
                    jnp.concatenate(
                        [
                            jnp.concatenate([part[r], blank] if side == 0 else [blank, part[r + 1]], axis=0).astype(BF16)
                            for part in parts
                            for r in range(0, 8, 2)
                        ],
                        axis=0,
                    )
                    for side in range(2)
                ],
                axis=1,
            )
            total = jnp.zeros((T, T), F32)
            for pair in range(4):
                streamed = jnp.concatenate([hots[2 * pair], hots[2 * pair + 1]], axis=1)
                total = jnp.where(pair_of == pair, dot_nt(streamed, held), total)
            flipped = total.T
            dense = flipped[0:64] + flipped[64:128]
            for r in range(8):
                out_ref[pl.ds(start + g * 8 + r, 8, stride=WIDTH), :] = dense[8 * r : 8 * r + 8]


def pack_kernel(sizes, cols_ref, vals_ref, diag_ref, *out_refs):
    offset = 0
    for n, (size, out_ref) in enumerate(zip(sizes, out_refs)):
        out_ref[0:size, 0:KC] = cols_ref[offset : offset + size, :].astype(F32)
        out_ref[0:size, KC:] = vals_ref[offset : offset + size, :]
        out_ref[size : size + 8, :] = jnp.broadcast_to(diag_ref[n : n + 1, :], (8, 2 * KC))
        offset += size


def params():
    return pltpu.CompilerParams(vmem_limit_bytes=VMEM_LIMIT)


def vmem():
    return pl.BlockSpec(memory_space=pltpu.VMEM)


def smem():
    return pl.BlockSpec(memory_space=pltpu.SMEM)


def shape(*dims):
    return jax.ShapeDtypeStruct(dims, F32)


def cost(us):
    return pl.CostEstimate(flops=0, bytes_accessed=int(us * 3.0e6), transcendentals=0)


def call(kernel, out_shape, n_args, n_smem, scratch, us, name):
    outs = out_shape if isinstance(out_shape, tuple) else (out_shape,)
    return pl.pallas_call(
        kernel,
        out_shape=out_shape,
        in_specs=[smem()] * n_smem + [vmem()] * (n_args - n_smem),
        out_specs=(vmem(),) * len(outs) if isinstance(out_shape, tuple) else vmem(),
        scratch_shapes=scratch,
        compiler_params=params(),
        cost_estimate=cost(us),
        name=name,
    )


def row_scratch():
    return pltpu.VMEM((9 * T, T), F32)


def extend_scratch():
    return [pltpu.VMEM((BND, BND), BF16)] * 2 + [pltpu.VMEM((WIDTH, BND), BF16)] * 3


def swap_front(x, mask):
    count = lax.axis_size("front")
    return lax.ppermute(x, "front", [(f, f ^ mask) for f in range(count)])


def hypercube(strip, masks):
    pieces = {0: strip}
    for mask in masks:
        for m in sorted(pieces):
            pieces[m | mask] = swap_front(pieces[m], mask)
    return [pieces[m] for m in range(len(pieces))]


def after(x, done):
    return lax.optimization_barrier((x, done))[0]


def body(leaf_bits, leaf_fronts, coupling_cols, coupling_vals, sep_diag, child_maps):
    n_front = lax.axis_size("front")
    bits = len(leaf_bits)
    n_leaf = 1 << bits
    front = lax.axis_index("front")
    leaf = lax.axis_index(leaf_bits)
    pos = jnp.stack([leaf, front]).astype(jnp.int32)
    strip = leaf_fronts[0]
    half = n_front // 2
    inner = [1 << b for b in range(half.bit_length() - 1)]
    strip_rows = WIDTH // n_front
    middle = SEP // 2
    cross_all = [(f, f ^ half) for f in range(n_front)]
    needed = [(f, g) for f, g in cross_all if f >= half or (f + 1) * strip_rows > middle]
    strip1, strip2 = lax.optimization_barrier((strip[:, :middle], strip[:, middle:SEP]))
    cross1 = lax.ppermute(strip1, "front", cross_all)
    cross2 = lax.ppermute(strip2, "front", needed)
    panels1 = hypercube(strip1, inner) + hypercube(cross1, inner)
    panels2 = hypercube(strip2, inner) + hypercube(cross2, inner)
    strip3 = after(strip, panels2[-1])[:, SEP:]
    cross3 = lax.ppermute(strip3, "front", [(f, f - half) for f in range(half, n_front)])

    coupling_cols, coupling_vals, sep_diag, _ = lax.optimization_barrier(
        (coupling_cols, coupling_vals, sep_diag, panels1[-1])
    )
    sizes = [WIDTH // (n_front << level) for level in range(1, bits + 1)]
    diag_rows, offset = [], 0
    for n, size in enumerate(sizes):
        rank = (leaf & ((2 << n) - 1)) * n_front + front
        spread = jnp.tile(sep_diag[0, 0, offset : offset + size], T // size)
        mine = jnp.arange(T) // size == rank % (T // size)
        diag_rows.append(jnp.pad(jnp.where(mine, spread, 0.0), (0, 2 * KC - T)))
        offset += size
    diag_rows = jnp.pad(jnp.stack(diag_rows), ((0, -len(sizes) % 8), (0, 0)))
    packed = call(
        functools.partial(pack_kernel, sizes),
        tuple(shape(size + 8, 2 * KC) for size in sizes), 3, 0, [], 1, "pack_lists",
    )(coupling_cols[0, 0], coupling_vals[0, 0], diag_rows)
    lists = []
    for n, size in enumerate(sizes):
        gathered = lax.all_gather(packed[n], leaf_bits[bits - 1 - n :] + ("front",), axis=0, tiled=False)
        if size < 8:
            rows = gathered[:, :size].reshape(WIDTH // 8, 8, 2 * KC)
            diag = gathered[:, size].reshape(WIDTH // 8, 8 // size, 2 * KC).sum(1, keepdims=True)
            gathered = jnp.concatenate([rows, jnp.pad(diag, ((0, 0), (0, 7), (0, 0)))], axis=1)
        lists.append(gathered)

    fac, inv, logs = call(
        functools.partial(head_kernel, n_front),
        (shape(SEP, SEP), shape(SEP, T), shape(8, T)), 1 + 2 * n_front, 1, [row_scratch()], 18, "head_factor",
    )(pos, *panels1, *panels2)
    pieces3 = hypercube(strip3, inner) + hypercube(after(cross3, inv), inner)
    piece, below = call(
        functools.partial(below_kernel, n_front),
        (shape(strip_rows, SEP), shape(BND, SEP)), 3 + 2 * n_front, 1, [pltpu.VMEM((WIDTH, SEP), F32)],
        4, "leaf_below",
    )(pos, fac, inv, *panels1, *panels2)
    pk = call(
        functools.partial(update_kernel, n_front), shape(NPACK, T, T), 3 + n_front, 1,
        [pltpu.VMEM((BND, BND), F32)], 3, "leaf_update",
    )(pos, below, logs, *pieces3)
    pieces = [piece]
    for level in range(1, bits + 1):
        size = sizes[level - 1]
        last = level == bits
        sib = lax.ppermute(pk, leaf_bits[bits - level], [(0, 1), (1, 0)])
        base = call(
            functools.partial(own_kernel, level, n_leaf, last), shape(WIDTH, WIDTH), 4, 1,
            [pltpu.VMEM((WIDTH // T * WIDTH, T), F32)] + extend_scratch(), 17, "own_child",
        )(pos, lists[level - 1], pk, child_maps)
        piece, pk = call(
            functools.partial(level_kernel, level, n_leaf, n_front, last),
            (shape(size, SEP), shape(8, T) if last else shape(NPACK, T, T)), 5, 1,
            [pltpu.VMEM((WIDTH, WIDTH), F32), pltpu.VMEM((SEP, T), F32), pltpu.VMEM((8, T), F32), row_scratch()] + extend_scratch(),
            27, "level_front",
        )(pos, base, pk, sib, child_maps)
        pieces.append(piece)
    return jnp.concatenate(pieces, axis=0)[None, None], pk[0, 0]


def solution(mesh):
    bits = mesh.shape["leaf"].bit_length() - 1
    leaf_bits = tuple(f"leaf{b}" for b in reversed(range(bits)))
    fine = Mesh(mesh.devices.reshape((2,) * bits + (mesh.shape["front"],)), leaf_bits + ("front",))
    placed = (
        P(leaf_bits, "front", None),
        P(leaf_bits, "front", None, None),
        P(leaf_bits, "front", None, None),
        P(leaf_bits, "front", None),
        P(),
    )
    return jax.shard_map(
        functools.partial(body, leaf_bits),
        mesh=fine,
        in_specs=placed,
        out_specs=(P(leaf_bits, "front", None, None), P()),
        check_vma=False,
    )
```

```python
import functools

import jax
import jax.numpy as jnp
from jax import lax
from jax.experimental import pallas as pl
from jax.experimental.pallas import tpu as pltpu
from jax.sharding import Mesh, PartitionSpec as P

SEP = 512
BND = 512
WIDTH = SEP + BND
KC = 128
T = 128
NB = SEP // T
PANEL = 32
PIECES = 3
TILE = 256
NPACK = NB * (NB + 1) // 2
F32 = jnp.float32
BF16 = jnp.bfloat16
VMEM_LIMIT = 50 * 1024 * 1024


def pack_index(i, j):
    return i * (i + 1) // 2 + j


def split(x):
    hi = x.astype(BF16)
    return hi, (x - hi.astype(F32)).astype(BF16)


def dot_nt(a, b):
    return lax.dot_general(a, b, (((1,), (1,)), ((), ())), preferred_element_type=F32)


def dot_nn(a, b):
    return lax.dot_general(a, b, (((1,), (0,)), ((), ())), preferred_element_type=F32)


def mm_nt(a, b):
    a_hi, a_lo = split(a)
    b_hi, b_lo = split(b)
    return dot_nt(a_hi, b_hi) + (dot_nt(a_hi, b_lo) + dot_nt(a_lo, b_hi))


def iota2(shape, dim):
    return lax.broadcasted_iota(jnp.int32, shape, dim)


def tri_sym(block):
    n = block.shape[0]
    rows, cols = iota2((n, n), 0), iota2((n, n), 1)
    low = jnp.where(cols <= rows, block, 0.0)
    strict = jnp.where(cols < rows, block, 0.0)
    return low + strict.T


def row_of(x, k):
    return jnp.broadcast_to(x[k : k + 1], (8, T))


def lane_of(x, k):
    return jnp.broadcast_to(x[:, k : k + 1], (8, T))


def tree_sum(terms):
    while len(terms) > 1:
        terms = [sum(terms[i : i + 2][1:], terms[i]) for i in range(0, len(terms), 2)]
    return terms[0]


def reciprocal(x):
    return pl.reciprocal(x, approx=True)


def eliminate_eight(groups, s, c, keep, lane, sub, tmp_ref):
    panel = groups[s]
    inside = (lane >= c) & (lane < c + 8)
    base = c * 9
    for m in range(8):
        tmp_ref[base + 8 * m : base + 8 * m + 8, :] = lane_of(panel, c + m)
    tmp_ref[base + 64 : base + 72, :] = jnp.where(inside, jnp.where(lane - c == sub, 1.0, 0.0), panel)

    def row(n):
        return jnp.broadcast_to(tmp_ref[base + n : base + n + 1, :], (8, T))

    d = {(i, m): row(8 * m + i) for m in range(8) for i in range(m + 1)}
    rows = [row(64 + k) for k in range(8)]
    upper_acc = jnp.zeros((8, T), F32)
    inv_acc = jnp.zeros((8, T), F32)
    to_p, to_q, first = {}, {}, {}

    def emit(k, line, entries, root):
        inv_row = line * root
        for m in range(k, 8):
            line = jnp.where(lane == c + m, entries[m], line)
        return jnp.where(sub == k, line * root, upper_acc), jnp.where(sub == k, inv_row, inv_acc)

    for p in range(0, 8, 2):
        q = p + 1
        a, b, e = d[p, p], d[p, q], d[q, q]
        det = a * e - b * b
        recip = reciprocal(det)
        rest = range(q + 1, 8)
        w = {i: e * d[p, i] - b * d[q, i] for i in rest}
        z = {i: a * d[q, i] - b * d[p, i] for i in rest}
        root_p = lax.rsqrt(a)
        inv_a = root_p * root_p
        ratio = b * inv_a
        schur = det * inv_a
        upper_acc, inv_acc = emit(p, rows[p], {m: d[p, m] for m in range(p, 8)}, root_p)
        line_q = {m: d[q, m] - ratio * d[p, m] for m in rest}
        line_q[q] = schur
        upper_acc, inv_acc = emit(q, rows[q] - ratio * rows[p], line_q, lax.rsqrt(schur))
        for i in rest:
            for m in range(i, 8):
                d[i, m] = d[i, m] - (w[i] * d[p, m] + z[i] * d[q, m]) * recip
        for i in rest:
            to_p[p, i], to_q[p, i] = w[i] * recip, z[i] * recip
            rows[i] = rows[i] - (to_p[p, i] * rows[p] + to_q[p, i] * rows[q])
        first[p] = (e * rows[p] - b * rows[q]) * recip
        first[q] = (a * rows[q] - b * rows[p]) * recip
    if s + 1 < keep:
        sol = [None] * 8
        for p in (6, 4, 2, 0):
            rest = range(p + 2, 8)
            sol[p], sol[p + 1] = first[p], first[p + 1]
            if p < 6:
                sol[p] = sol[p] - tree_sum([to_p[p, m] * sol[m] for m in rest])
                sol[p + 1] = sol[p + 1] - tree_sum([to_q[p, m] * sol[m] for m in rest])
        for g in range(s + 1, keep):
            old = groups[g]
            groups[g] = jnp.where(inside, 0.0, old) - tree_sum([lane_of(old, c + k) * sol[k] for k in range(8)])
    return jnp.where(lane >= c + sub, upper_acc, 0.0), jnp.where(lane <= c + sub, inv_acc, 0.0)


def chol_and_inverse(sym, tmp_ref):
    lane, sub = iota2((8, T), 1), iota2((8, T), 0)
    per = PANEL // 8
    diag = jnp.sum(jnp.where(iota2((T, T), 0) == iota2((T, T), 1), sym, 0.0), axis=0, keepdims=True)
    scale = jnp.broadcast_to(lax.rsqrt(diag), (T, T))
    sym = (sym * scale) * scale.T
    groups = [sym[8 * g : 8 * g + 8] for g in range(T // 8)]
    upper_rows, inv_rows = [], []
    for p in range(T // PANEL):
        for s in range(p * per, (p + 1) * per):
            upper, inv = eliminate_eight(groups, s, 8 * s, (p + 1) * per, lane, sub, tmp_ref)
            upper_rows.append(upper)
            inv_rows.append(inv)
        end = (p + 1) * PANEL
        if end < T:
            both = jnp.concatenate(
                [jnp.where(lane < end, inv_rows[s], upper_rows[s]) for s in range(p * per, (p + 1) * per)], axis=0
            )
            hi, lo = split(both)
            product = lax.dot_general(
                jnp.concatenate([hi, lo, hi], axis=0), jnp.concatenate([hi, hi, lo], axis=0),
                (((0,), (0,)), ((), ())), preferred_element_type=F32,
            )
            done = (lane >= p * PANEL) & (lane < end)
            for g in range((p + 1) * per, T // 8):
                groups[g] = jnp.where(done, 0.0, groups[g]) - product[8 * g : 8 * g + 8]
    return jnp.concatenate(upper_rows, axis=0) * (diag * scale[0:1]), jnp.concatenate(inv_rows, axis=0) * scale


def factor_panel(f_ref, x_ref, log_ref, tmp_ref, rows, blocks):
    width = blocks * T
    log_ref[...] = jnp.zeros_like(log_ref)

    @pl.loop(0, blocks)
    def _(j):
        at = pl.multiple_of(j * T, T)
        upper, inv = chol_and_inverse(tri_sym(f_ref[pl.ds(at, T), pl.ds(at, T)]), tmp_ref)
        f_ref[pl.ds(at, T), pl.ds(at, T)] = upper.T
        x_ref[pl.ds(at, T), :] = inv
        eye = iota2((T, T), 0) == iota2((T, T), 1)
        diag = jnp.sum(jnp.where(eye, upper, 0.0), axis=0, keepdims=True)
        log_ref[0:1, :] += jnp.log(diag)
        for k in range(blocks):
            first = (k + 1) * T
            if first >= rows:
                continue

            @pl.when(j == k)
            def _():
                below = mm_nt(f_ref[first:rows, k * T : first], inv)
                f_ref[first:rows, k * T : first] = below
                if first < width:
                    f_ref[first:rows, first:width] -= mm_nt(below, below[: width - first])


def zero_above(f_ref, blocks):
    for i in range(blocks - 1):
        f_ref[i * T : (i + 1) * T, (i + 1) * T : blocks * T] = jnp.zeros((T, (blocks - 1 - i) * T), F32)


def log_total(log_ref):
    return 2.0 * jnp.sum(log_ref[0:1, :], axis=1, keepdims=True)


def write_own(out_ref, f_ref, start):
    size = out_ref.shape[0]
    if size % 8 == 0:
        out_ref[...] = f_ref[pl.ds(pl.multiple_of(start, 8), size), 0:SEP]
    else:
        base = pl.multiple_of(start // 8 * 8, 8)
        block = f_ref[pl.ds(base, 8), 0:SEP]
        offset = start - base
        piece = block[0:size]
        for shift in range(size, 8, size):
            piece = jnp.where(offset == shift, block[shift : shift + size], piece)
        out_ref[...] = piece


def write_update(pk_ref, below, tail_of, log_value):
    hi, lo = split(below)
    rows, cols = iota2((T, T), 0), iota2((T, T), 1)
    for i in range(NB):
        here = slice(i * T, (i + 1) * T)
        upto = slice(0, (i + 1) * T)
        prod = dot_nt(hi[here], hi[upto]) + (dot_nt(hi[here], lo[upto]) + dot_nt(lo[here], hi[upto]))
        for j in range(i + 1):
            block = tail_of(i, j) - prod[:, j * T : (j + 1) * T]
            if i == 0:
                block = jnp.where((rows == 0) & (cols == T - 1), log_value, block)
            pk_ref[pack_index(i, j)] = block


def place(pieces, work, front, want_tail):
    count = len(pieces)
    half = count // 2
    size = pieces[0].shape[0]
    for m, piece in enumerate(pieces):
        source = front ^ m

        @pl.when((source >= half) == want_tail)
        def _():
            at = pl.multiple_of((source & (half - 1)) * size, 8)
            work[pl.ds(at, size), :] = piece[...]


def head_kernel(n, pos_ref, *refs):
    pieces, (fac_ref, x_ref, log_ref, tmp_ref) = refs[:n], refs[n:]
    place(pieces, fac_ref, pos_ref[1], False)
    factor_panel(fac_ref, x_ref, log_ref, tmp_ref, SEP, NB)
    zero_above(fac_ref, NB)


def below_kernel(n, pos_ref, fac, inv, *refs):
    pieces, (own_ref, below_ref, stack) = refs[:n], refs[n:]
    front = pos_ref[1]
    place(pieces, below_ref, front, True)
    for j in range(NB):
        here = slice(j * T, (j + 1) * T)
        solved = mm_nt(below_ref[:, here], inv[here, :])
        below_ref[:, here] = solved
        if j + 1 < NB:
            rest = slice((j + 1) * T, SEP)
            below_ref[:, rest] -= mm_nt(solved, fac[rest, here])
    stack[0:SEP, :] = fac[...]
    stack[SEP:, :] = below_ref[...]
    write_own(own_ref, stack, front * own_ref.shape[0])


def update_kernel(n, pos_ref, below_ref, log_ref, *refs):
    pieces, (pk_ref, tail_ref) = refs[:n], refs[n:]
    place(pieces, tail_ref, pos_ref[1], True)

    def tail_of(i, j):
        return tail_ref[i * T : (i + 1) * T, j * T : (j + 1) * T]

    write_update(pk_ref, below_ref[...], tail_of, log_total(log_ref))


def expand(pk_ref, u_hi, u_lo):
    rows, cols = iota2((T, T), 0), iota2((T, T), 1)
    for i in range(NB):
        for j in range(i + 1):
            block = pk_ref[pack_index(i, j)]
            if i == j:
                low = jnp.where(cols <= rows, block, 0.0)
                block = low + jnp.where(cols < rows, block, 0.0).T
            hi, lo = split(block)
            u_hi[i * T : (i + 1) * T, j * T : (j + 1) * T] = hi
            u_lo[i * T : (i + 1) * T, j * T : (j + 1) * T] = lo
            if i != j:
                hi, lo = split(block.T)
                u_hi[j * T : (j + 1) * T, i * T : (i + 1) * T] = hi
                u_lo[j * T : (j + 1) * T, i * T : (i + 1) * T] = lo


def extend_add(pk_ref, index_row, emit, last, u_hi, u_lo, hot, y_hi, y_lo):
    expand(pk_ref, u_hi, u_lo)

    @pl.loop(0, WIDTH // TILE)
    def _(tile):
        at = pl.multiple_of(tile * TILE, TILE)
        ids = iota2((TILE, BND), 0) + at
        match = jnp.where(ids == index_row, 1.0, 0.0).astype(BF16)
        hot[pl.ds(at, TILE), :] = match
        y_hi[pl.ds(at, TILE), :] = dot_nn(match, u_hi[...]).astype(BF16)
        y_lo[pl.ds(at, TILE), :] = dot_nn(match, u_lo[...]).astype(BF16)

    for a in range(WIDTH // TILE):
        here = slice(a * TILE, (a + 1) * TILE)
        for b in range(a + 1):
            if last and b * TILE >= SEP:
                continue
            there = slice(b * TILE, (b + 1) * TILE)
            part = dot_nt(y_hi[here, :], hot[there, :]) + dot_nt(y_lo[here, :], hot[there, :])
            emit(a, b, part)


def map_row(level, n_leaf, pos_ref, maps_ref, sibling):
    base = 2 * n_leaf - 2 * (n_leaf >> (level - 1))
    own = pos_ref[0] >> (level - 1)
    number = base + (own ^ 1 if sibling else own)
    return maps_ref[pl.ds(number, 1), :]


def owned_blocks(core, last):
    rows = [2 * turn + (turn + core) % 2 for turn in range(WIDTH // T // 2)]
    return [(i, j) for i in rows for j in range(min(i + 1, NB if last else 2 * NB))]


def piece_bounds(last):
    total = len(owned_blocks(0, last))
    return [total * n // PIECES for n in range(PIECES + 1)]


def coupling_kernel(last, pos_ref, lists_ref, *refs):
    out_refs, dense = refs[:-1], refs[-1]
    bounds = piece_bounds(last)
    core = pos_ref[1] & 1
    size = lists_ref.shape[1] - 8
    eye = iota2((T, T), 0) == iota2((T, T), 1)
    limit = NB if last else 2 * NB

    def turn_of(turn, offset):
        i = 2 * turn + ((turn + core) & 1)
        densify(lists_ref, i * T, dense)
        diag = jnp.zeros((1, T), F32)
        for n in range(max(1, T // size)):
            diag = diag + lists_ref[i * T // size + n, size : size + 1, 0:T]
        for j in range(limit):

            for first, end, out_ref in zip(bounds, bounds[1:], out_refs):

                @pl.when((j <= i) & (offset + j >= first) & (offset + j < end))
                def _():
                    block = dense[j * T : (j + 1) * T, :]
                    out_ref[offset + j - first] = block + jnp.where(eye & (j == i), diag, 0.0)

        return offset + jnp.minimum(i + 1, limit)

    lax.fori_loop(0, WIDTH // T // 2, turn_of, 0)


def own_kernel(level, n_leaf, last, pos_ref, pk_ref, maps_ref, f_ref, u_hi, u_lo, hot, y_hi, y_lo):
    index_row = map_row(level, n_leaf, pos_ref, maps_ref, False)

    def emit(a, b, part):
        f_ref[a * TILE : (a + 1) * TILE, b * TILE : (b + 1) * TILE] = part

    extend_add(pk_ref, index_row, emit, last, u_hi, u_lo, hot, y_hi, y_lo)


def level_kernel(
    level, n_leaf, n_front, last, n_sib,
    pos_ref, base_ref, own_pk, maps_ref, *refs,
):
    mine_refs, theirs_refs, refs = refs[:PIECES], refs[PIECES : 2 * PIECES], refs[2 * PIECES :]
    sibs, (own_ref, next_ref, f_ref, x_ref, log_ref, tmp_ref, u_hi, u_lo, hot, y_hi, y_lo, *gathered) = (
        refs[:n_sib], refs[n_sib:],
    )
    core = pos_ref[1] & 1
    if n_sib == 1:
        sib_pk = sibs[0]
    else:
        sib_pk = gathered[0]
        sib_pk[pl.ds(core * (NPACK // 2), NPACK // 2)] = sibs[0][...]
        sib_pk[pl.ds((1 - core) * (NPACK // 2), NPACK // 2)] = sibs[1][...]
    index_row = map_row(level, n_leaf, pos_ref, maps_ref, True)
    where_is = {}
    bounds = piece_bounds(last)
    for owner in range(2):
        for n, block in enumerate(owned_blocks(owner, last)):
            p = max(m for m in range(PIECES) if bounds[m] <= n)
            where_is[block] = owner, p, n - bounds[p]

    def emit(a, b, part):
        per = TILE // T
        for r in range(per):
            for h in range(per):
                i, j = a * per + r, b * per + h
                if j > i:
                    continue
                owner, p, n = where_is[i, j]
                here, there = slice(i * T, (i + 1) * T), slice(j * T, (j + 1) * T)
                dense = jnp.where(core == owner, mine_refs[p][n], theirs_refs[p][n])
                f_ref[here, there] = (base_ref[here, there] + part[r * T : (r + 1) * T, h * T : (h + 1) * T]) + dense

    extend_add(sib_pk, index_row, emit, last, u_hi, u_lo, hot, y_hi, y_lo)
    factor_panel(f_ref, x_ref, log_ref, tmp_ref, WIDTH, NB)
    zero_above(f_ref, NB)
    rank = (pos_ref[0] & ((1 << level) - 1)) * n_front + pos_ref[1]
    write_own(own_ref, f_ref, rank * own_ref.shape[0])
    kids_log = own_pk[0][0:1, T - 1 : T] + sib_pk[0][0:1, T - 1 : T]
    log_value = kids_log + log_total(log_ref)
    if last:
        next_ref[...] = jnp.broadcast_to(log_value, next_ref.shape)
    else:

        def tail_of(i, j):
            return f_ref[SEP + i * T : SEP + (i + 1) * T, SEP + j * T : SEP + (j + 1) * T]

        write_update(next_ref, f_ref[SEP:, 0:SEP], tail_of, log_value)


def densify(lists_ref, start, out_ref):
    block_ids = iota2((8, KC), 0).astype(F32)
    column_ids = [(iota2((16, KC), 0) + 16 * j).astype(F32).astype(BF16) for j in range(T // 16)]
    one, zero = jnp.ones((16, KC), BF16), jnp.zeros((16, KC), BF16)
    blank = jnp.zeros((8, KC), F32)
    pair_of = iota2((T, T), 1) % 64 // 16
    size = lists_ref.shape[1] - 8
    for g in range(T // 8):
        hots, parts = [], ([], [])
        rank = (start + g * 8) // size
        at = pl.multiple_of((start + g * 8) % size, 8)
        cols = lists_ref[rank, pl.ds(at, 8), 0:KC]
        vals = lists_ref[rank, pl.ds(at, 8), KC:]
        block_no = jnp.floor(cols * (1.0 / T))
        within = cols - block_no * T
        for r in range(8):
            column = row_of(within, r)
            column = jnp.concatenate([column, column], axis=0).astype(BF16)
            hots.append(jnp.concatenate([jnp.where(ids == column, one, zero) for ids in column_ids], axis=0))
            val = row_of(vals, r)
            hi = val.astype(BF16).astype(F32)
            pick = block_ids == row_of(block_no, r)
            parts[0].append(jnp.where(pick, hi, 0.0))
            parts[1].append(jnp.where(pick, val - hi, 0.0))
        held = jnp.concatenate(
            [
                jnp.concatenate(
                    [
                        jnp.concatenate([part[r], blank] if side == 0 else [blank, part[r + 1]], axis=0).astype(BF16)
                        for part in parts
                        for r in range(0, 8, 2)
                    ],
                    axis=0,
                )
                for side in range(2)
            ],
            axis=1,
        )
        total = jnp.zeros((T, T), F32)
        for pair in range(4):
            streamed = jnp.concatenate([hots[2 * pair], hots[2 * pair + 1]], axis=1)
            total = jnp.where(pair_of == pair, dot_nt(streamed, held), total)
        flipped = total.T
        dense = flipped[0:64] + flipped[64:128]
        for r in range(8):
            out_ref[pl.ds(g * 8 + r, 8, stride=T), :] = dense[8 * r : 8 * r + 8]


def pack_kernel(n_front, sizes, pos_ref, cols_ref, vals_ref, diag_ref, *refs):
    out_refs, line_ref = refs[:-1], refs[-1]
    line_ref[...] = jnp.zeros_like(line_ref)
    line_ref[0:1, 0 : diag_ref.shape[1]] = diag_ref[...]
    lane = iota2((8, 2 * KC), 1)
    offset = 0
    for n, (size, out_ref) in enumerate(zip(sizes, out_refs)):
        out_ref[0:size, 0:KC] = cols_ref[offset : offset + size, :].astype(F32)
        out_ref[0:size, KC:] = vals_ref[offset : offset + size, :]
        rank = (pos_ref[0] & ((2 << n) - 1)) * n_front + pos_ref[1]
        first = rank * size % T
        line = pltpu.roll(line_ref[...], (first - offset) & (2 * KC - 1), 1)
        line = jnp.broadcast_to(jnp.where((lane >= first) & (lane < first + size), line, 0.0)[0:1], (8, 2 * KC))
        out_ref[size : size + 8, :] = line
        offset += size


def params():
    return pltpu.CompilerParams(vmem_limit_bytes=VMEM_LIMIT)


def vmem():
    return pl.BlockSpec(memory_space=pltpu.VMEM)


def smem():
    return pl.BlockSpec(memory_space=pltpu.SMEM)


def shape(*dims):
    return jax.ShapeDtypeStruct(dims, F32)


def cost(us):
    return pl.CostEstimate(flops=0, bytes_accessed=int(us * 3.0e6), transcendentals=0)


def call(kernel, out_shape, n_args, n_smem, scratch, us, name):
    outs = out_shape if isinstance(out_shape, tuple) else (out_shape,)
    return pl.pallas_call(
        kernel,
        out_shape=out_shape,
        in_specs=[smem()] * n_smem + [vmem()] * (n_args - n_smem),
        out_specs=(vmem(),) * len(outs) if isinstance(out_shape, tuple) else vmem(),
        scratch_shapes=scratch,
        compiler_params=params(),
        cost_estimate=cost(us),
        name=name,
    )


def row_scratch():
    return pltpu.VMEM((9 * T, T), F32)


def extend_scratch():
    return [pltpu.VMEM((BND, BND), BF16)] * 2 + [pltpu.VMEM((WIDTH, BND), BF16)] * 3


def swap_front(x, mask):
    count = lax.axis_size("front")
    return lax.ppermute(x, "front", [(f, f ^ mask) for f in range(count)])


def hypercube(strip, masks):
    pieces = {0: strip}
    for mask in masks:
        for m in sorted(pieces):
            pieces[m | mask] = swap_front(pieces[m], mask)
    return [pieces[m] for m in range(len(pieces))]


def after(x, done):
    return lax.optimization_barrier((x, done))[0]


def body(leaf_bits, leaf_fronts, coupling_cols, coupling_vals, sep_diag, child_maps):
    n_front = lax.axis_size("front")
    bits = len(leaf_bits)
    n_leaf = 1 << bits
    front = lax.axis_index("front")
    leaf = lax.axis_index(leaf_bits)
    pos = jnp.stack([leaf, front]).astype(jnp.int32)
    strip = leaf_fronts[0]
    half = n_front // 2
    inner = [1 << b for b in range(half.bit_length() - 1)]
    strip_rows = WIDTH // n_front
    panel_strip = strip[:, :SEP]
    cross = swap_front(panel_strip, half)
    sizes = [WIDTH // (n_front << level) for level in range(1, bits + 1)]
    packed = call(
        functools.partial(pack_kernel, n_front, sizes),
        tuple(shape(size + 8, 2 * KC) for size in sizes), 4, 1, [pltpu.VMEM((8, 2 * KC), F32)], 1, "pack_lists",
    )(pos, coupling_cols[0, 0], coupling_vals[0, 0], sep_diag[0])
    panels = hypercube(panel_strip, inner) + hypercube(after(cross, packed[0]), inner)
    strip3 = after(strip, panels[-1])[:, SEP:]
    cross3 = lax.ppermute(strip3, "front", [(f, f - half) for f in range(half, n_front)])

    lists = []
    for n, size in enumerate(sizes):
        gathered = lax.all_gather(packed[n], leaf_bits[bits - 1 - n :] + ("front",), axis=0, tiled=False)
        if size < 8:
            rows = gathered[:, :size].reshape(WIDTH // 8, 8, 2 * KC)
            diag = gathered[:, size].reshape(WIDTH // 8, 8 // size, 2 * KC).sum(1, keepdims=True)
            gathered = jnp.concatenate([rows, jnp.pad(diag, ((0, 0), (0, 7), (0, 0)))], axis=1)
        lists.append(gathered)

    fac, inv, logs = call(
        functools.partial(head_kernel, n_front),
        (shape(SEP, SEP), shape(SEP, T), shape(8, T)), 1 + n_front, 1, [row_scratch()], 300, "head_factor",
    )(pos, *panels)
    pieces3 = hypercube(strip3, inner) + hypercube(after(cross3, inv), inner)
    piece, below = call(
        functools.partial(below_kernel, n_front),
        (shape(strip_rows, SEP), shape(BND, SEP)), 3 + n_front, 1, [pltpu.VMEM((WIDTH, SEP), F32)],
        4, "leaf_below",
    )(pos, fac, inv, *panels)
    pk = call(
        functools.partial(update_kernel, n_front), shape(NPACK, T, T), 3 + n_front, 1,
        [pltpu.VMEM((BND, BND), F32)], 3, "leaf_update",
    )(pos, below, logs, *pieces3)
    pieces = [piece]
    for level in range(1, bits + 1):
        size = sizes[level - 1]
        last = level == bits
        axis = leaf_bits[bits - level]
        if level < 3:
            sibs = [lax.ppermute(pk, axis, [(0, 1), (1, 0)])]
        else:
            part = lax.dynamic_slice_in_dim(pk, (front & 1) * (NPACK // 2), NPACK // 2, 0)
            received = lax.ppermute(part, axis, [(0, 1), (1, 0)])
            sibs = [received, swap_front(received, 1)]
        bounds = piece_bounds(last)
        mine = call(
            functools.partial(coupling_kernel, last),
            tuple(shape(end - first, T, T) for first, end in zip(bounds, bounds[1:])), 2, 1,
            [pltpu.VMEM((WIDTH // T * T, T), F32)], 0.2, "coupling",
        )(pos, after(lists[level - 1], pk))
        theirs = [swap_front(block, 1) for block in mine]
        base = call(
            functools.partial(own_kernel, level, n_leaf, last), shape(WIDTH, WIDTH), 3, 1, extend_scratch(), 0.2, "own_child",
        )(pos, pk, child_maps)
        gathered = [pltpu.VMEM((NPACK, T, T), F32)] if len(sibs) == 2 else []
        piece, pk = call(
            functools.partial(level_kernel, level, n_leaf, n_front, last, len(sibs)),
            (shape(size, SEP), shape(8, T) if last else shape(NPACK, T, T)), 4 + 2 * PIECES + len(sibs), 1,
            [pltpu.VMEM((WIDTH, WIDTH), F32), pltpu.VMEM((SEP, T), F32), pltpu.VMEM((8, T), F32), row_scratch()]
            + extend_scratch() + gathered,
            300, "level_front",
        )(pos, base, pk, child_maps, *mine, *theirs, *sibs)
        pieces.append(piece)
    return jnp.concatenate(pieces, axis=0)[None, None], pk[0, 0]


def solution(mesh):
    bits = mesh.shape["leaf"].bit_length() - 1
    leaf_bits = tuple(f"leaf{b}" for b in reversed(range(bits)))
    fine = Mesh(mesh.devices.reshape((2,) * bits + (mesh.shape["front"],)), leaf_bits + ("front",))
    placed = (
        P(leaf_bits, "front", None),
        P(leaf_bits, "front", None, None),
        P(leaf_bits, "front", None, None),
        P(leaf_bits, "front", None),
        P(),
    )
    return jax.shard_map(
        functools.partial(body, leaf_bits),
        mesh=fine,
        in_specs=placed,
        out_specs=(P(leaf_bits, "front", None, None), P()),
        check_vma=False,
    )
```

```python
import functools

import jax
import jax.numpy as jnp
from jax import lax
from jax.experimental import pallas as pl
from jax.experimental.pallas import tpu as pltpu
from jax.sharding import Mesh, PartitionSpec as P

SEP = 512
BND = 512
WIDTH = SEP + BND
KC = 128
T = 128
NB = SEP // T
PANEL = 32
PIECES = 3
STEP = 32
TILE = 256
NPACK = NB * (NB + 1) // 2
F32 = jnp.float32
BF16 = jnp.bfloat16
VMEM_LIMIT = 28 * 1024 * 1024


def pack_index(i, j):
    return i * (i + 1) // 2 + j


def split(x):
    hi = x.astype(BF16)
    return hi, (x - hi.astype(F32)).astype(BF16)


def dot_nt(a, b):
    return lax.dot_general(a, b, (((1,), (1,)), ((), ())), preferred_element_type=F32)


def dot_nn(a, b):
    return lax.dot_general(a, b, (((1,), (0,)), ((), ())), preferred_element_type=F32)


def mm_nt(a, b):
    a_hi, a_lo = split(a)
    b_hi, b_lo = split(b)
    return dot_nt(a_hi, b_hi) + (dot_nt(a_hi, b_lo) + dot_nt(a_lo, b_hi))


def iota2(shape, dim):
    return lax.broadcasted_iota(jnp.int32, shape, dim)


def tri_sym(block):
    n = block.shape[0]
    rows, cols = iota2((n, n), 0), iota2((n, n), 1)
    low = jnp.where(cols <= rows, block, 0.0)
    strict = jnp.where(cols < rows, block, 0.0)
    return low + strict.T


def row_of(x, k):
    return jnp.broadcast_to(x[k : k + 1], (8, T))


def lane_of(x, k):
    return jnp.broadcast_to(x[:, k : k + 1], (8, T))


def tree_sum(terms):
    while len(terms) > 1:
        terms = [sum(terms[i : i + 2][1:], terms[i]) for i in range(0, len(terms), 2)]
    return terms[0]


def reciprocal(x):
    return pl.reciprocal(x, approx=True)


def eliminate_eight(groups, s, c, keep, lane, sub, tmp_ref):
    panel = groups[s]
    inside = (lane >= c) & (lane < c + 8)
    base = c * 9
    for m in range(8):
        tmp_ref[base + 8 * m : base + 8 * m + 8, :] = lane_of(panel, c + m)
    tmp_ref[base + 64 : base + 72, :] = jnp.where(inside, jnp.where(lane - c == sub, 1.0, 0.0), panel)

    def row(n):
        return jnp.broadcast_to(tmp_ref[base + n : base + n + 1, :], (8, T))

    d = {(i, m): row(8 * m + i) for m in range(8) for i in range(m + 1)}
    rows = [row(64 + k) for k in range(8)]
    upper_acc = jnp.zeros((8, T), F32)
    inv_acc = jnp.zeros((8, T), F32)
    to_p, to_q, first = {}, {}, {}

    def emit(k, line, entries, root):
        inv_row = line * root
        for m in range(k, 8):
            line = jnp.where(lane == c + m, entries[m], line)
        return jnp.where(sub == k, line * root, upper_acc), jnp.where(sub == k, inv_row, inv_acc)

    for p in range(0, 8, 2):
        q = p + 1
        a, b, e = d[p, p], d[p, q], d[q, q]
        det = a * e - b * b
        recip = reciprocal(det)
        rest = range(q + 1, 8)
        w = {i: e * d[p, i] - b * d[q, i] for i in rest}
        z = {i: a * d[q, i] - b * d[p, i] for i in rest}
        root_p = lax.rsqrt(a)
        inv_a = root_p * root_p
        ratio = b * inv_a
        schur = det * inv_a
        upper_acc, inv_acc = emit(p, rows[p], {m: d[p, m] for m in range(p, 8)}, root_p)
        line_q = {m: d[q, m] - ratio * d[p, m] for m in rest}
        line_q[q] = schur
        upper_acc, inv_acc = emit(q, rows[q] - ratio * rows[p], line_q, lax.rsqrt(schur))
        for i in rest:
            for m in range(i, 8):
                d[i, m] = d[i, m] - (w[i] * d[p, m] + z[i] * d[q, m]) * recip
        for i in rest:
            to_p[p, i], to_q[p, i] = w[i] * recip, z[i] * recip
            rows[i] = rows[i] - (to_p[p, i] * rows[p] + to_q[p, i] * rows[q])
        first[p] = (e * rows[p] - b * rows[q]) * recip
        first[q] = (a * rows[q] - b * rows[p]) * recip
    if s + 1 < keep:
        sol = [None] * 8
        for p in (6, 4, 2, 0):
            rest = range(p + 2, 8)
            sol[p], sol[p + 1] = first[p], first[p + 1]
            if p < 6:
                sol[p] = sol[p] - tree_sum([to_p[p, m] * sol[m] for m in rest])
                sol[p + 1] = sol[p + 1] - tree_sum([to_q[p, m] * sol[m] for m in rest])
        for g in range(s + 1, keep):
            old = groups[g]
            groups[g] = jnp.where(inside, 0.0, old) - tree_sum([lane_of(old, c + k) * sol[k] for k in range(8)])
    return jnp.where(lane >= c + sub, upper_acc, 0.0), jnp.where(lane <= c + sub, inv_acc, 0.0)


def chol_and_inverse(sym, tmp_ref):
    lane, sub = iota2((8, T), 1), iota2((8, T), 0)
    per = PANEL // 8
    diag = jnp.sum(jnp.where(iota2((T, T), 0) == iota2((T, T), 1), sym, 0.0), axis=0, keepdims=True)
    scale = jnp.broadcast_to(lax.rsqrt(diag), (T, T))
    sym = (sym * scale) * scale.T
    groups = [sym[8 * g : 8 * g + 8] for g in range(T // 8)]
    upper_rows, inv_rows = [], []
    for p in range(T // PANEL):
        for s in range(p * per, (p + 1) * per):
            upper, inv = eliminate_eight(groups, s, 8 * s, (p + 1) * per, lane, sub, tmp_ref)
            upper_rows.append(upper)
            inv_rows.append(inv)
        end = (p + 1) * PANEL
        if end < T:
            both = jnp.concatenate(
                [jnp.where(lane < end, inv_rows[s], upper_rows[s]) for s in range(p * per, (p + 1) * per)], axis=0
            )
            hi, lo = split(both)
            product = lax.dot_general(
                jnp.concatenate([hi, lo, hi], axis=0), jnp.concatenate([hi, hi, lo], axis=0),
                (((0,), (0,)), ((), ())), preferred_element_type=F32,
            )
            done = (lane >= p * PANEL) & (lane < end)
            for g in range((p + 1) * per, T // 8):
                groups[g] = jnp.where(done, 0.0, groups[g]) - product[8 * g : 8 * g + 8]
    return jnp.concatenate(upper_rows, axis=0) * (diag * scale[0:1]), jnp.concatenate(inv_rows, axis=0) * scale


def factor_panel(f_ref, x_ref, log_ref, tmp_ref, rows, blocks):
    width = blocks * T
    log_ref[...] = jnp.zeros_like(log_ref)

    @pl.loop(0, blocks)
    def _(j):
        at = pl.multiple_of(j * T, T)
        upper, inv = chol_and_inverse(tri_sym(f_ref[pl.ds(at, T), pl.ds(at, T)]), tmp_ref)
        f_ref[pl.ds(at, T), pl.ds(at, T)] = upper.T
        x_ref[pl.ds(at, T), :] = inv
        eye = iota2((T, T), 0) == iota2((T, T), 1)
        diag = jnp.sum(jnp.where(eye, upper, 0.0), axis=0, keepdims=True)
        log_ref[0:1, :] += jnp.log(diag)
        for k in range(blocks):
            first = (k + 1) * T
            if first >= rows:
                continue

            @pl.when(j == k)
            def _():
                below = mm_nt(f_ref[first:rows, k * T : first], inv)
                f_ref[first:rows, k * T : first] = below
                if first < width:
                    f_ref[first:rows, first:width] -= mm_nt(below, below[: width - first])


def zero_above(f_ref, blocks):
    for i in range(blocks - 1):
        f_ref[i * T : (i + 1) * T, (i + 1) * T : blocks * T] = jnp.zeros((T, (blocks - 1 - i) * T), F32)


def log_total(log_ref):
    return 2.0 * jnp.sum(log_ref[0:1, :], axis=1, keepdims=True)


def write_own(out_ref, f_ref, start):
    size = out_ref.shape[0]
    if size % 8 == 0:
        out_ref[...] = f_ref[pl.ds(pl.multiple_of(start, 8), size), 0:SEP]
    else:
        base = pl.multiple_of(start // 8 * 8, 8)
        block = f_ref[pl.ds(base, 8), 0:SEP]
        offset = start - base
        piece = block[0:size]
        for shift in range(size, 8, size):
            piece = jnp.where(offset == shift, block[shift : shift + size], piece)
        out_ref[...] = piece


def write_update(pk_ref, below, tail_of, log_value):
    hi, lo = split(below)
    rows, cols = iota2((T, T), 0), iota2((T, T), 1)
    for i in range(NB):
        here = slice(i * T, (i + 1) * T)
        upto = slice(0, (i + 1) * T)
        prod = dot_nt(hi[here], hi[upto]) + (dot_nt(hi[here], lo[upto]) + dot_nt(lo[here], hi[upto]))
        for j in range(i + 1):
            block = tail_of(i, j) - prod[:, j * T : (j + 1) * T]
            if i == 0:
                block = jnp.where((rows == 0) & (cols == T - 1), log_value, block)
            pk_ref[pack_index(i, j)] = block


def place(pieces, work, front, want_tail):
    count = len(pieces)
    half = count // 2
    size = pieces[0].shape[0]
    for m, piece in enumerate(pieces):
        source = front ^ m

        @pl.when((source >= half) == want_tail)
        def _():
            at = pl.multiple_of((source & (half - 1)) * size, 8)
            work[pl.ds(at, size), :] = piece[...]


def head_kernel(n, pos_ref, *refs):
    pieces, (fac_ref, x_ref, log_ref, tmp_ref) = refs[:n], refs[n:]
    place(pieces, fac_ref, pos_ref[1], False)
    factor_panel(fac_ref, x_ref, log_ref, tmp_ref, SEP, NB)
    zero_above(fac_ref, NB)


def below_kernel(n, pos_ref, fac, inv, *refs):
    pieces, (own_ref, below_ref, stack) = refs[:n], refs[n:]
    front = pos_ref[1]
    place(pieces, below_ref, front, True)
    for j in range(NB):
        here = slice(j * T, (j + 1) * T)
        solved = mm_nt(below_ref[:, here], inv[here, :])
        below_ref[:, here] = solved
        if j + 1 < NB:
            rest = slice((j + 1) * T, SEP)
            below_ref[:, rest] -= mm_nt(solved, fac[rest, here])
    stack[0:SEP, :] = fac[...]
    stack[SEP:, :] = below_ref[...]
    write_own(own_ref, stack, front * own_ref.shape[0])


def update_kernel(n, pos_ref, below_ref, log_ref, *refs):
    pieces, (pk_ref, tail_ref) = refs[:n], refs[n:]
    place(pieces, tail_ref, pos_ref[1], True)

    def tail_of(i, j):
        return tail_ref[i * T : (i + 1) * T, j * T : (j + 1) * T]

    write_update(pk_ref, below_ref[...], tail_of, log_total(log_ref))


def expand(pk_ref, u_hi, u_lo):
    rows, cols = iota2((T, T), 0), iota2((T, T), 1)
    for i in range(NB):
        for j in range(i + 1):
            block = pk_ref[pack_index(i, j)]
            if i == j:
                low = jnp.where(cols <= rows, block, 0.0)
                block = low + jnp.where(cols < rows, block, 0.0).T
            hi, lo = split(block)
            u_hi[i * T : (i + 1) * T, j * T : (j + 1) * T] = hi
            u_lo[i * T : (i + 1) * T, j * T : (j + 1) * T] = lo
            if i != j:
                hi, lo = split(block.T)
                u_hi[j * T : (j + 1) * T, i * T : (i + 1) * T] = hi
                u_lo[j * T : (j + 1) * T, i * T : (i + 1) * T] = lo


def extend_add(pk_ref, index_row, emit, last, u_hi, u_lo, hot, y_hi, y_lo):
    expand(pk_ref, u_hi, u_lo)

    @pl.loop(0, WIDTH // TILE)
    def _(tile):
        at = pl.multiple_of(tile * TILE, TILE)
        ids = iota2((TILE, BND), 0) + at
        match = jnp.where(ids == index_row, 1.0, 0.0).astype(BF16)
        hot[pl.ds(at, TILE), :] = match
        y_hi[pl.ds(at, TILE), :] = dot_nn(match, u_hi[...]).astype(BF16)
        y_lo[pl.ds(at, TILE), :] = dot_nn(match, u_lo[...]).astype(BF16)

    for a in range(WIDTH // TILE):
        here = slice(a * TILE, (a + 1) * TILE)
        for b in range(a + 1):
            if last and b * TILE >= SEP:
                continue
            there = slice(b * TILE, (b + 1) * TILE)
            part = dot_nt(y_hi[here, :], hot[there, :]) + dot_nt(y_lo[here, :], hot[there, :])
            emit(a, b, part)


def map_row(level, n_leaf, pos_ref, maps_ref, sibling):
    base = 2 * n_leaf - 2 * (n_leaf >> (level - 1))
    own = pos_ref[0] >> (level - 1)
    number = base + (own ^ 1 if sibling else own)
    return maps_ref[pl.ds(number, 1), :]


def owned_blocks(core, last):
    rows = [2 * turn + (turn + core) % 2 for turn in range(WIDTH // T // 2)]
    return [(i, j) for i in rows for j in range(min(i + 1, NB if last else 2 * NB))]


def piece_bounds(last):
    total = len(owned_blocks(0, last))
    return [total * n // PIECES for n in range(PIECES + 1)]


def coupling_kernel(last, pos_ref, lists_ref, *refs):
    out_refs, (dense, totals) = refs[:-2], refs[-2:]
    bounds = piece_bounds(last)
    core = pos_ref[1] & 1
    size = lists_ref.shape[1] - 8
    eye = iota2((T, T), 0) == iota2((T, T), 1)
    limit = NB if last else 2 * NB
    steps = WIDTH // 2 // STEP

    @pl.loop(0, steps + 1)
    def _(step):
        spread_rows(totals, dense, jnp.maximum(step - 1, 0) * STEP)
        gather_rows(lists_ref, totals, jnp.minimum(step, steps - 1) * STEP, core)

    def turn_of(turn, offset):
        i = 2 * turn + ((turn + core) & 1)
        diag = jnp.zeros((1, T), F32)
        for n in range(max(1, T // size)):
            diag = diag + lists_ref[i * T // size + n, size : size + 1, 0:T]
        for j in range(limit):
            for first, end, out_ref in zip(bounds, bounds[1:], out_refs):

                @pl.when((j <= i) & (offset + j >= first) & (offset + j < end))
                def _():
                    block = dense[pl.ds(pl.multiple_of(turn * WIDTH + j * T, T), T), :]
                    out_ref[offset + j - first] = block + jnp.where(eye & (j == i), diag, 0.0)

        return offset + jnp.minimum(i + 1, limit)

    lax.fori_loop(0, WIDTH // T // 2, turn_of, 0)


def own_kernel(level, n_leaf, last, pos_ref, pk_ref, maps_ref, f_ref, u_hi, u_lo, hot, y_hi, y_lo):
    index_row = map_row(level, n_leaf, pos_ref, maps_ref, False)

    def emit(a, b, part):
        f_ref[pack_index(a, b)] = part

    extend_add(pk_ref, index_row, emit, last, u_hi, u_lo, hot, y_hi, y_lo)


def level_kernel(
    level, n_leaf, n_front, last, n_sib,
    pos_ref, base_ref, own_pk, maps_ref, *refs,
):
    mine_refs, theirs_refs, refs = refs[:PIECES], refs[PIECES : 2 * PIECES], refs[2 * PIECES :]
    sibs, (own_ref, next_ref, f_ref, x_ref, log_ref, tmp_ref, u_hi, u_lo, hot, y_hi, y_lo, *gathered) = (
        refs[:n_sib], refs[n_sib:],
    )
    core = pos_ref[1] & 1
    if n_sib == 1:
        sib_pk = sibs[0]
    else:
        sib_pk = gathered[0]
        sib_pk[pl.ds(core * (NPACK // 2), NPACK // 2)] = sibs[0][...]
        sib_pk[pl.ds((1 - core) * (NPACK // 2), NPACK // 2)] = sibs[1][...]
    index_row = map_row(level, n_leaf, pos_ref, maps_ref, True)
    where_is = {}
    bounds = piece_bounds(last)
    for owner in range(2):
        for n, block in enumerate(owned_blocks(owner, last)):
            p = max(m for m in range(PIECES) if bounds[m] <= n)
            where_is[block] = owner, p, n - bounds[p]

    def emit(a, b, part):
        per = TILE // T
        for r in range(per):
            for h in range(per):
                i, j = a * per + r, b * per + h
                if j > i:
                    continue
                owner, p, n = where_is[i, j]
                here, there = slice(i * T, (i + 1) * T), slice(j * T, (j + 1) * T)
                dense = jnp.where(core == owner, mine_refs[p][n], theirs_refs[p][n])
                mine, its = slice(r * T, (r + 1) * T), slice(h * T, (h + 1) * T)
                f_ref[here, there] = (base_ref[pack_index(a, b), mine, its] + part[mine, its]) + dense

    extend_add(sib_pk, index_row, emit, last, u_hi, u_lo, hot, y_hi, y_lo)
    factor_panel(f_ref, x_ref, log_ref, tmp_ref, WIDTH, NB)
    zero_above(f_ref, NB)
    rank = (pos_ref[0] & ((1 << level) - 1)) * n_front + pos_ref[1]
    write_own(own_ref, f_ref, rank * own_ref.shape[0])
    kids_log = own_pk[0][0:1, T - 1 : T] + sib_pk[0][0:1, T - 1 : T]
    log_value = kids_log + log_total(log_ref)
    if last:
        next_ref[...] = jnp.broadcast_to(log_value, next_ref.shape)
    else:

        def tail_of(i, j):
            return f_ref[SEP + i * T : SEP + (i + 1) * T, SEP + j * T : SEP + (j + 1) * T]

        write_update(next_ref, f_ref[SEP:, 0:SEP], tail_of, log_value)


def gather_rows(lists_ref, totals, local, core):
    block_ids = iota2((8, KC), 0).astype(F32)
    column_ids = [(iota2((16, KC), 0) + 16 * j).astype(F32).astype(BF16) for j in range(T // 16)]
    one, zero = jnp.ones((16, KC), BF16), jnp.zeros((16, KC), BF16)
    blank = jnp.zeros((8, KC), F32)
    pair_of = iota2((T, T), 1) % 64 // 16
    size = lists_ref.shape[1] - 8
    turn = local // T
    start = (2 * turn + ((turn + core) & 1)) * T + local % T
    for g in range(STEP // 8):
        hots, parts = [], ([], [])
        rank = (start + g * 8) // size
        at = pl.multiple_of((start + g * 8) % size, 8)
        cols = lists_ref[rank, pl.ds(at, 8), 0:KC]
        vals = lists_ref[rank, pl.ds(at, 8), KC:]
        block_no = jnp.floor(cols * (1.0 / T))
        within = cols - block_no * T
        for r in range(8):
            column = row_of(within, r)
            column = jnp.concatenate([column, column], axis=0).astype(BF16)
            hots.append(jnp.concatenate([jnp.where(ids == column, one, zero) for ids in column_ids], axis=0))
            val = row_of(vals, r)
            hi = val.astype(BF16).astype(F32)
            pick = block_ids == row_of(block_no, r)
            parts[0].append(jnp.where(pick, hi, 0.0))
            parts[1].append(jnp.where(pick, val - hi, 0.0))
        held = [
            jnp.concatenate(
                [
                    jnp.concatenate([part[r], blank] if side == 0 else [blank, part[r + 1]], axis=0).astype(BF16)
                    for part in parts
                    for r in range(0, 8, 2)
                ],
                axis=0,
            )
            for side in range(2)
        ]
        held = jnp.concatenate(held, axis=1)
        total = jnp.zeros((T, T), F32)
        for pair in range(4):
            streamed = jnp.concatenate([hots[2 * pair], hots[2 * pair + 1]], axis=1)
            total = jnp.where(pair_of == pair, dot_nt(streamed, held), total)
        totals[g] = total


def spread_rows(totals, dense, local):
    base = local // T * WIDTH + local % T
    for g in range(STEP // 8):
        flipped = totals[g].T
        both = flipped[0:64] + flipped[64:128]
        for r in range(8):
            dense[pl.ds(base + g * 8 + r, 8, stride=T), :] = both[8 * r : 8 * r + 8]


def pack_kernel(n_front, sizes, pos_ref, cols_ref, vals_ref, diag_ref, *refs):
    out_refs, line_ref = refs[:-1], refs[-1]
    line_ref[...] = jnp.zeros_like(line_ref)
    line_ref[0:1, 0 : diag_ref.shape[1]] = diag_ref[...]
    lane = iota2((8, 2 * KC), 1)
    offset = 0
    for n, (size, out_ref) in enumerate(zip(sizes, out_refs)):
        out_ref[0:size, 0:KC] = cols_ref[offset : offset + size, :].astype(F32)
        out_ref[0:size, KC:] = vals_ref[offset : offset + size, :]
        rank = (pos_ref[0] & ((2 << n) - 1)) * n_front + pos_ref[1]
        first = rank * size % T
        line = pltpu.roll(line_ref[...], (first - offset) & (2 * KC - 1), 1)
        line = jnp.broadcast_to(jnp.where((lane >= first) & (lane < first + size), line, 0.0)[0:1], (8, 2 * KC))
        out_ref[size : size + 8, :] = line
        offset += size


def params():
    return pltpu.CompilerParams(vmem_limit_bytes=VMEM_LIMIT)


def vmem():
    return pl.BlockSpec(memory_space=pltpu.VMEM)


def smem():
    return pl.BlockSpec(memory_space=pltpu.SMEM)


def shape(*dims):
    return jax.ShapeDtypeStruct(dims, F32)


def cost(us):
    return pl.CostEstimate(flops=0, bytes_accessed=int(us * 3.0e6), transcendentals=0)


def call(kernel, out_shape, n_args, n_smem, scratch, us, name):
    outs = out_shape if isinstance(out_shape, tuple) else (out_shape,)
    return pl.pallas_call(
        kernel,
        out_shape=out_shape,
        in_specs=[smem()] * n_smem + [vmem()] * (n_args - n_smem),
        out_specs=(vmem(),) * len(outs) if isinstance(out_shape, tuple) else vmem(),
        scratch_shapes=scratch,
        compiler_params=params(),
        cost_estimate=cost(us),
        name=name,
    )


def row_scratch():
    return pltpu.VMEM((9 * T, T), F32)


def extend_scratch():
    return [pltpu.VMEM((BND, BND), BF16)] * 2 + [pltpu.VMEM((WIDTH, BND), BF16)] * 3


def swap_front(x, mask):
    count = lax.axis_size("front")
    return lax.ppermute(x, "front", [(f, f ^ mask) for f in range(count)])


def hypercube(strip, masks):
    pieces = {0: strip}
    for mask in masks:
        for m in sorted(pieces):
            pieces[m | mask] = swap_front(pieces[m], mask)
    return [pieces[m] for m in range(len(pieces))]


def after(x, done):
    return lax.optimization_barrier((x, done))[0]


def body(leaf_bits, leaf_fronts, coupling_cols, coupling_vals, sep_diag, child_maps):
    n_front = lax.axis_size("front")
    bits = len(leaf_bits)
    n_leaf = 1 << bits
    front = lax.axis_index("front")
    leaf = lax.axis_index(leaf_bits)
    pos = jnp.stack([leaf, front]).astype(jnp.int32)
    strip = leaf_fronts[0]
    half = n_front // 2
    inner = [1 << b for b in range(half.bit_length() - 1)]
    strip_rows = WIDTH // n_front
    panel_strip = strip[:, :SEP]
    cross = swap_front(panel_strip, half)
    sizes = [WIDTH // (n_front << level) for level in range(1, bits + 1)]
    packed = call(
        functools.partial(pack_kernel, n_front, sizes),
        tuple(shape(size + 8, 2 * KC) for size in sizes), 4, 1, [pltpu.VMEM((8, 2 * KC), F32)], 1, "pack_lists",
    )(pos, coupling_cols[0, 0], coupling_vals[0, 0], sep_diag[0])
    panels = hypercube(panel_strip, inner) + hypercube(cross, inner)
    strip3 = after(strip, panels[-1])[:, SEP:]
    cross3 = lax.ppermute(strip3, "front", [(f, f - half) for f in range(half, n_front)])

    lists = []
    for n, size in enumerate(sizes):
        gathered = lax.all_gather(after(packed[n], cross), leaf_bits[bits - 1 - n :] + ("front",), axis=0, tiled=False)
        if size < 8:
            rows = gathered[:, :size].reshape(WIDTH // 8, 8, 2 * KC)
            diag = gathered[:, size].reshape(WIDTH // 8, 8 // size, 2 * KC).sum(1, keepdims=True)
            gathered = jnp.concatenate([rows, jnp.pad(diag, ((0, 0), (0, 7), (0, 0)))], axis=1)
        lists.append(gathered)

    fac, inv, logs = call(
        functools.partial(head_kernel, n_front),
        (shape(SEP, SEP), shape(SEP, T), shape(8, T)), 1 + n_front, 1, [row_scratch()], 300, "head_factor",
    )(pos, *panels)
    pieces3 = hypercube(strip3, inner) + hypercube(after(cross3, inv), inner)
    piece, below = call(
        functools.partial(below_kernel, n_front),
        (shape(strip_rows, SEP), shape(BND, SEP)), 3 + n_front, 1, [pltpu.VMEM((WIDTH, SEP), F32)],
        4, "leaf_below",
    )(pos, fac, inv, *panels)
    pk = call(
        functools.partial(update_kernel, n_front), shape(NPACK, T, T), 3 + n_front, 1,
        [pltpu.VMEM((BND, BND), F32)], 3, "leaf_update",
    )(pos, below, logs, *pieces3)
    pieces = [piece]
    for level in range(1, bits + 1):
        size = sizes[level - 1]
        last = level == bits
        axis = leaf_bits[bits - level]
        if level < 3:
            sibs = [lax.ppermute(pk, axis, [(0, 1), (1, 0)])]
        else:
            part = lax.dynamic_slice_in_dim(pk, (front & 1) * (NPACK // 2), NPACK // 2, 0)
            sibs = [lax.ppermute(part, axis, [(0, 1), (1, 0)])]
        bounds = piece_bounds(last)
        mine = call(
            functools.partial(coupling_kernel, last),
            tuple(shape(end - first, T, T) for first, end in zip(bounds, bounds[1:])), 2, 1,
            [pltpu.VMEM((NB * WIDTH, T), F32), pltpu.VMEM((STEP // 8, T, T), F32)], 0.2, "coupling",
        )(pos, after(lists[level - 1], pk))
        theirs = [swap_front(block, 1) for block in mine]
        base = call(
            functools.partial(own_kernel, level, n_leaf, last), shape(pack_index(WIDTH // TILE, 0), TILE, TILE), 3, 1, extend_scratch(), 0.2, "own_child",
        )(pos, pk, child_maps)
        if level >= 3:
            sibs.append(swap_front(after(sibs[0], base), 1))
        gathered = [pltpu.VMEM((NPACK, T, T), F32)] if len(sibs) == 2 else []
        piece, pk = call(
            functools.partial(level_kernel, level, n_leaf, n_front, last, len(sibs)),
            (shape(size, SEP), shape(8, T) if last else shape(NPACK, T, T)), 4 + 2 * PIECES + len(sibs), 1,
            [pltpu.VMEM((WIDTH, WIDTH), F32), pltpu.VMEM((SEP, T), F32), pltpu.VMEM((8, T), F32), row_scratch()]
            + extend_scratch() + gathered,
            300, "level_front",
        )(pos, base, pk, child_maps, *mine, *theirs, *sibs)
        pieces.append(piece)
    return jnp.concatenate(pieces, axis=0)[None, None], pk[0, 0]


def solution(mesh):
    bits = mesh.shape["leaf"].bit_length() - 1
    leaf_bits = tuple(f"leaf{b}" for b in reversed(range(bits)))
    fine = Mesh(mesh.devices.reshape((2,) * bits + (mesh.shape["front"],)), leaf_bits + ("front",))
    placed = (
        P(leaf_bits, "front", None),
        P(leaf_bits, "front", None, None),
        P(leaf_bits, "front", None, None),
        P(leaf_bits, "front", None),
        P(),
    )
    return jax.shard_map(
        functools.partial(body, leaf_bits),
        mesh=fine,
        in_specs=placed,
        out_specs=(P(leaf_bits, "front", None, None), P()),
        check_vma=False,
    )
```

```python
import functools

import jax
import jax.numpy as jnp
from jax import lax
from jax.experimental import pallas as pl
from jax.experimental.pallas import tpu as pltpu
from jax.sharding import Mesh, PartitionSpec as P

SEP = 512
BND = 512
WIDTH = SEP + BND
KC = 128
T = 128
NB = SEP // T
PANEL = 32
PIECES = 3
STEP = 64
TILE = 256
NPACK = NB * (NB + 1) // 2
F32 = jnp.float32
BF16 = jnp.bfloat16
VMEM_LIMIT = 16 * 1024 * 1024


def pack_index(i, j):
    return i * (i + 1) // 2 + j


def split(x):
    hi = x.astype(BF16)
    return hi, (x - hi.astype(F32)).astype(BF16)


def dot_nt(a, b):
    return lax.dot_general(a, b, (((1,), (1,)), ((), ())), preferred_element_type=F32)


def dot_nn(a, b):
    return lax.dot_general(a, b, (((1,), (0,)), ((), ())), preferred_element_type=F32)


def mm_nt(a, b):
    a_hi, a_lo = split(a)
    b_hi, b_lo = split(b)
    return dot_nt(a_hi, b_hi) + (dot_nt(a_hi, b_lo) + dot_nt(a_lo, b_hi))


def iota2(shape, dim):
    return lax.broadcasted_iota(jnp.int32, shape, dim)


def tri_sym(block):
    n = block.shape[0]
    rows, cols = iota2((n, n), 0), iota2((n, n), 1)
    low = jnp.where(cols <= rows, block, 0.0)
    strict = jnp.where(cols < rows, block, 0.0)
    return low + strict.T


def row_of(x, k):
    return jnp.broadcast_to(x[k : k + 1], (8, T))


def lane_of(x, k):
    return jnp.broadcast_to(x[:, k : k + 1], (8, T))


def tree_sum(terms):
    while len(terms) > 1:
        terms = [sum(terms[i : i + 2][1:], terms[i]) for i in range(0, len(terms), 2)]
    return terms[0]


def reciprocal(x):
    return pl.reciprocal(x, approx=True)


def eliminate_eight(groups, s, c, keep, lane, sub, tmp_ref):
    panel = groups[s]
    inside = (lane >= c) & (lane < c + 8)
    base = c * 9
    for m in range(8):
        tmp_ref[base + 8 * m : base + 8 * m + 8, :] = lane_of(panel, c + m)
    tmp_ref[base + 64 : base + 72, :] = jnp.where(inside, jnp.where(lane - c == sub, 1.0, 0.0), panel)

    def row(n):
        return jnp.broadcast_to(tmp_ref[base + n : base + n + 1, :], (8, T))

    d = {(i, m): row(8 * m + i) for m in range(8) for i in range(m + 1)}
    rows = [row(64 + k) for k in range(8)]
    upper_acc = jnp.zeros((8, T), F32)
    inv_acc = jnp.zeros((8, T), F32)
    to_p, to_q, first = {}, {}, {}
    if s + 1 < keep:
        near = [lane_of(groups[s + 1], c + k) for k in range(8)]
        following = jnp.where(inside, 0.0, groups[s + 1])

    def emit(k, line, entries, root):
        inv_row = line * root
        for m in range(k, 8):
            line = jnp.where(lane == c + m, entries[m], line)
        return jnp.where(sub == k, line * root, upper_acc), jnp.where(sub == k, inv_row, inv_acc)

    for p in range(0, 8, 2):
        q = p + 1
        a, b, e = d[p, p], d[p, q], d[q, q]
        det = a * e - b * b
        recip = reciprocal(det)
        rest = range(q + 1, 8)
        w = {i: e * d[p, i] - b * d[q, i] for i in rest}
        z = {i: a * d[q, i] - b * d[p, i] for i in rest}
        root_p = lax.rsqrt(a)
        inv_a = root_p * root_p
        ratio = b * inv_a
        schur = det * inv_a
        upper_acc, inv_acc = emit(p, rows[p], {m: d[p, m] for m in range(p, 8)}, root_p)
        line_q = {m: d[q, m] - ratio * d[p, m] for m in rest}
        line_q[q] = schur
        upper_acc, inv_acc = emit(q, rows[q] - ratio * rows[p], line_q, lax.rsqrt(schur))
        for i in rest:
            for m in range(i, 8):
                d[i, m] = d[i, m] - (w[i] * d[p, m] + z[i] * d[q, m]) * recip
        for i in rest:
            to_p[p, i], to_q[p, i] = w[i] * recip, z[i] * recip
            rows[i] = rows[i] - (to_p[p, i] * rows[p] + to_q[p, i] * rows[q])
        if s + 1 < keep:
            near_p, near_q = (e * near[p] - b * near[q]) * recip, (a * near[q] - b * near[p]) * recip
            following = following - (near_p * rows[p] + near_q * rows[q])
            for m in rest:
                near[m] = near[m] - (near_p * d[p, m] + near_q * d[q, m])
        first[p] = (e * rows[p] - b * rows[q]) * recip
        first[q] = (a * rows[q] - b * rows[p]) * recip
    if s + 1 < keep:
        groups[s + 1] = following
    if s + 2 < keep:
        sol = [None] * 8
        for p in (6, 4, 2, 0):
            rest = range(p + 2, 8)
            sol[p], sol[p + 1] = first[p], first[p + 1]
            if p < 6:
                sol[p] = sol[p] - tree_sum([to_p[p, m] * sol[m] for m in rest])
                sol[p + 1] = sol[p + 1] - tree_sum([to_q[p, m] * sol[m] for m in rest])
        for g in range(s + 2, keep):
            old = groups[g]
            groups[g] = jnp.where(inside, 0.0, old) - tree_sum([lane_of(old, c + k) * sol[k] for k in range(8)])
    return jnp.where(lane >= c + sub, upper_acc, 0.0), jnp.where(lane <= c + sub, inv_acc, 0.0)


def chol_and_inverse(sym, tmp_ref):
    lane, sub = iota2((8, T), 1), iota2((8, T), 0)
    per = PANEL // 8
    diag = jnp.sum(jnp.where(iota2((T, T), 0) == iota2((T, T), 1), sym, 0.0), axis=0, keepdims=True)
    scale = jnp.broadcast_to(lax.rsqrt(diag), (T, T))
    sym = (sym * scale) * scale.T
    groups = [sym[8 * g : 8 * g + 8] for g in range(T // 8)]
    upper_rows, inv_rows = [], []
    for p in range(T // PANEL):
        for s in range(p * per, (p + 1) * per):
            upper, inv = eliminate_eight(groups, s, 8 * s, (p + 1) * per, lane, sub, tmp_ref)
            upper_rows.append(upper)
            inv_rows.append(inv)
        end = (p + 1) * PANEL
        if end < T:
            both = jnp.concatenate(
                [jnp.where(lane < end, inv_rows[s], upper_rows[s]) for s in range(p * per, (p + 1) * per)], axis=0
            )
            hi, lo = split(both)
            product = lax.dot_general(
                jnp.concatenate([hi, lo, hi], axis=0), jnp.concatenate([hi, hi, lo], axis=0),
                (((0,), (0,)), ((), ())), preferred_element_type=F32,
            )
            done = (lane >= p * PANEL) & (lane < end)
            for g in range((p + 1) * per, T // 8):
                groups[g] = jnp.where(done, 0.0, groups[g]) - product[8 * g : 8 * g + 8]
    return jnp.concatenate(upper_rows, axis=0) * (diag * scale[0:1]), jnp.concatenate(inv_rows, axis=0) * scale


def factor_panel(f_ref, x_ref, log_ref, tmp_ref, rows, blocks):
    width = blocks * T
    log_ref[...] = jnp.zeros_like(log_ref)

    @pl.loop(0, blocks)
    def _(j):
        at = pl.multiple_of(j * T, T)
        upper, inv = chol_and_inverse(tri_sym(f_ref[pl.ds(at, T), pl.ds(at, T)]), tmp_ref)
        f_ref[pl.ds(at, T), pl.ds(at, T)] = upper.T
        x_ref[pl.ds(at, T), :] = inv
        eye = iota2((T, T), 0) == iota2((T, T), 1)
        diag = jnp.sum(jnp.where(eye, upper, 0.0), axis=0, keepdims=True)
        log_ref[0:1, :] += jnp.log(diag)
        for k in range(blocks):
            first = (k + 1) * T
            if first >= rows:
                continue

            @pl.when(j == k)
            def _():
                below = mm_nt(f_ref[first:rows, k * T : first], inv)
                f_ref[first:rows, k * T : first] = below
                if first < width:
                    f_ref[first:rows, first:width] -= mm_nt(below, below[: width - first])


def zero_above(f_ref, blocks):
    for i in range(blocks - 1):
        f_ref[i * T : (i + 1) * T, (i + 1) * T : blocks * T] = jnp.zeros((T, (blocks - 1 - i) * T), F32)


def log_total(log_ref):
    return 2.0 * jnp.sum(log_ref[0:1, :], axis=1, keepdims=True)


def write_own(out_ref, f_ref, start):
    size = out_ref.shape[0]
    if size % 8 == 0:
        out_ref[...] = f_ref[pl.ds(pl.multiple_of(start, 8), size), 0:SEP]
    else:
        base = pl.multiple_of(start // 8 * 8, 8)
        block = f_ref[pl.ds(base, 8), 0:SEP]
        offset = start - base
        piece = block[0:size]
        for shift in range(size, 8, size):
            piece = jnp.where(offset == shift, block[shift : shift + size], piece)
        out_ref[...] = piece


def write_update(pk_ref, below, tail_of, log_value):
    hi, lo = split(below)
    rows, cols = iota2((T, T), 0), iota2((T, T), 1)
    for i in range(NB):
        here = slice(i * T, (i + 1) * T)
        upto = slice(0, (i + 1) * T)
        prod = dot_nt(hi[here], hi[upto]) + (dot_nt(hi[here], lo[upto]) + dot_nt(lo[here], hi[upto]))
        for j in range(i + 1):
            block = tail_of(i, j) - prod[:, j * T : (j + 1) * T]
            if i == 0:
                block = jnp.where((rows == 0) & (cols == T - 1), log_value, block)
            pk_ref[pack_index(i, j)] = block


def place(pieces, work, front, want_tail):
    count = len(pieces)
    half = count // 2
    size = pieces[0].shape[0]
    for m, piece in enumerate(pieces):
        source = front ^ m

        @pl.when((source >= half) == want_tail)
        def _():
            at = pl.multiple_of((source & (half - 1)) * size, 8)
            work[pl.ds(at, size), :] = piece[...]


def head_kernel(n, pos_ref, *refs):
    pieces, (fac_ref, x_ref, log_ref, tmp_ref) = refs[:n], refs[n:]
    place(pieces, fac_ref, pos_ref[1], False)
    factor_panel(fac_ref, x_ref, log_ref, tmp_ref, SEP, NB)
    zero_above(fac_ref, NB)


def below_kernel(n, pos_ref, fac, inv, *refs):
    pieces, (own_ref, below_ref, stack) = refs[:n], refs[n:]
    front = pos_ref[1]
    place(pieces, below_ref, front, True)
    for j in range(NB):
        here = slice(j * T, (j + 1) * T)
        solved = mm_nt(below_ref[:, here], inv[here, :])
        below_ref[:, here] = solved
        if j + 1 < NB:
            rest = slice((j + 1) * T, SEP)
            below_ref[:, rest] -= mm_nt(solved, fac[rest, here])
    stack[0:SEP, :] = fac[...]
    stack[SEP:, :] = below_ref[...]
    write_own(own_ref, stack, front * own_ref.shape[0])


def update_kernel(n, pos_ref, below_ref, log_ref, *refs):
    pieces, (pk_ref, tail_ref) = refs[:n], refs[n:]
    place(pieces, tail_ref, pos_ref[1], True)

    def tail_of(i, j):
        return tail_ref[i * T : (i + 1) * T, j * T : (j + 1) * T]

    write_update(pk_ref, below_ref[...], tail_of, log_total(log_ref))


def expand(pk_ref, u_hi, u_lo):
    rows, cols = iota2((T, T), 0), iota2((T, T), 1)
    for i in range(NB):
        for j in range(i + 1):
            block = pk_ref[pack_index(i, j)]
            if i == j:
                low = jnp.where(cols <= rows, block, 0.0)
                block = low + jnp.where(cols < rows, block, 0.0).T
            hi, lo = split(block)
            u_hi[i * T : (i + 1) * T, j * T : (j + 1) * T] = hi
            u_lo[i * T : (i + 1) * T, j * T : (j + 1) * T] = lo
            if i != j:
                hi, lo = split(block.T)
                u_hi[j * T : (j + 1) * T, i * T : (i + 1) * T] = hi
                u_lo[j * T : (j + 1) * T, i * T : (i + 1) * T] = lo


def extend_add(pk_ref, index_row, emit, last, u_hi, u_lo, hot, y_hi, y_lo):
    expand(pk_ref, u_hi, u_lo)

    @pl.loop(0, WIDTH // TILE)
    def _(tile):
        at = pl.multiple_of(tile * TILE, TILE)
        ids = iota2((TILE, BND), 0) + at
        match = jnp.where(ids == index_row, 1.0, 0.0).astype(BF16)
        hot[pl.ds(at, TILE), :] = match
        y_hi[pl.ds(at, TILE), :] = dot_nn(match, u_hi[...]).astype(BF16)
        y_lo[pl.ds(at, TILE), :] = dot_nn(match, u_lo[...]).astype(BF16)

    for a in range(WIDTH // TILE):
        here = slice(a * TILE, (a + 1) * TILE)
        for b in range(a + 1):
            if last and b * TILE >= SEP:
                continue
            there = slice(b * TILE, (b + 1) * TILE)
            part = dot_nt(y_hi[here, :], hot[there, :]) + dot_nt(y_lo[here, :], hot[there, :])
            emit(a, b, part)


def map_row(level, n_leaf, pos_ref, maps_ref, sibling):
    base = 2 * n_leaf - 2 * (n_leaf >> (level - 1))
    own = pos_ref[0] >> (level - 1)
    number = base + (own ^ 1 if sibling else own)
    return maps_ref[pl.ds(number, 1), :]


def owned_blocks(core, last):
    rows = [2 * turn + (turn + core) % 2 for turn in range(WIDTH // T // 2)]
    return [(i, j) for i in rows for j in range(min(i + 1, NB if last else 2 * NB))]


def piece_bounds(last):
    total = len(owned_blocks(0, last))
    return [total * n // PIECES for n in range(PIECES + 1)]


def coupling_kernel(last, pos_ref, lists_ref, *refs):
    out_refs, (dense, held_ref, sems) = refs[:-3], refs[-3:]
    bounds = piece_bounds(last)
    core = pos_ref[1] & 1
    size = lists_ref.shape[1] - 8
    ranks = T // size
    eye = iota2((T, T), 0) == iota2((T, T), 1)
    limit = NB if last else 2 * NB

    def fetch(turn):
        i = 2 * turn + ((turn + core) & 1)
        return pltpu.make_async_copy(lists_ref.at[pl.ds(i * ranks, ranks)], held_ref.at[turn], sems.at[turn])

    for turn in range(NB):
        fetch(turn).start()

    @pl.loop(0, NB * T // STEP)
    def _(step):
        turn = step // (T // STEP)

        @pl.when(step % (T // STEP) == 0)
        def _():
            fetch(turn).wait()

        spread_rows(held_ref, dense, turn, step % (T // STEP) * STEP)

    def turn_of(turn, offset):
        i = 2 * turn + ((turn + core) & 1)
        diag = jnp.zeros((1, T), F32)
        for n in range(ranks):
            diag = diag + held_ref[turn, n, size : size + 1, 0:T]
        for j in range(limit):
            for first, end, out_ref in zip(bounds, bounds[1:], out_refs):

                @pl.when((j <= i) & (offset + j >= first) & (offset + j < end))
                def _():
                    block = dense[pl.ds(pl.multiple_of(turn * WIDTH + j * T, T), T), :]
                    out_ref[offset + j - first] = block + jnp.where(eye & (j == i), diag, 0.0)

        return offset + jnp.minimum(i + 1, limit)

    lax.fori_loop(0, NB, turn_of, 0)


def own_kernel(level, n_leaf, last, pos_ref, pk_ref, maps_ref, f_ref, u_hi, u_lo, hot, y_hi, y_lo):
    index_row = map_row(level, n_leaf, pos_ref, maps_ref, False)

    def emit(a, b, part):
        f_ref[pack_index(a, b)] = part

    extend_add(pk_ref, index_row, emit, last, u_hi, u_lo, hot, y_hi, y_lo)


def level_kernel(
    level, n_leaf, n_front, last, n_sib,
    pos_ref, base_ref, own_pk, maps_ref, *refs,
):
    mine_refs, theirs_refs, refs = refs[:PIECES], refs[PIECES : 2 * PIECES], refs[2 * PIECES :]
    sibs, (own_ref, next_ref, f_ref, x_ref, log_ref, tmp_ref, u_hi, u_lo, hot, y_hi, y_lo, *gathered) = (
        refs[:n_sib], refs[n_sib:],
    )
    core = pos_ref[1] & 1
    if n_sib == 1:
        sib_pk = sibs[0]
    else:
        sib_pk = gathered[0]
        sib_pk[pl.ds(core * (NPACK // 2), NPACK // 2)] = sibs[0][...]
        sib_pk[pl.ds((1 - core) * (NPACK // 2), NPACK // 2)] = sibs[1][...]
    index_row = map_row(level, n_leaf, pos_ref, maps_ref, True)
    where_is = {}
    bounds = piece_bounds(last)
    for owner in range(2):
        for n, block in enumerate(owned_blocks(owner, last)):
            p = max(m for m in range(PIECES) if bounds[m] <= n)
            where_is[block] = owner, p, n - bounds[p]

    def emit(a, b, part):
        per = TILE // T
        for r in range(per):
            for h in range(per):
                i, j = a * per + r, b * per + h
                if j > i:
                    continue
                owner, p, n = where_is[i, j]
                here, there = slice(i * T, (i + 1) * T), slice(j * T, (j + 1) * T)
                dense = jnp.where(core == owner, mine_refs[p][n], theirs_refs[p][n])
                mine, its = slice(r * T, (r + 1) * T), slice(h * T, (h + 1) * T)
                f_ref[here, there] = (base_ref[pack_index(a, b), mine, its] + part[mine, its]) + dense

    extend_add(sib_pk, index_row, emit, last, u_hi, u_lo, hot, y_hi, y_lo)
    factor_panel(f_ref, x_ref, log_ref, tmp_ref, WIDTH, NB)
    zero_above(f_ref, NB)
    rank = (pos_ref[0] & ((1 << level) - 1)) * n_front + pos_ref[1]
    write_own(own_ref, f_ref, rank * own_ref.shape[0])
    kids_log = own_pk[0][0:1, T - 1 : T] + sib_pk[0][0:1, T - 1 : T]
    log_value = kids_log + log_total(log_ref)
    if last:
        next_ref[...] = jnp.broadcast_to(log_value, next_ref.shape)
    else:

        def tail_of(i, j):
            return f_ref[SEP + i * T : SEP + (i + 1) * T, SEP + j * T : SEP + (j + 1) * T]

        write_update(next_ref, f_ref[SEP:, 0:SEP], tail_of, log_value)


def spread_rows(lists_ref, dense, turn, first):
    block_ids = iota2((8, KC), 0).astype(F32)
    column_ids = [(iota2((16, KC), 0) + 16 * j).astype(F32).astype(BF16) for j in range(T // 16)]
    one, zero = jnp.ones((16, KC), BF16), jnp.zeros((16, KC), BF16)
    blank = jnp.zeros((8, KC), F32)
    pair_of = iota2((T, T), 1) % 64 // 16
    size = lists_ref.shape[2] - 8
    for g in range(STEP // 8):
        hots, parts = [], ([], [])
        rank = (first + g * 8) // size
        at = pl.multiple_of((first + g * 8) % size, 8)
        cols = lists_ref[turn, rank, pl.ds(at, 8), 0:KC]
        vals = lists_ref[turn, rank, pl.ds(at, 8), KC:]
        block_no = jnp.floor(cols * (1.0 / T))
        within = cols - block_no * T
        for r in range(8):
            column = row_of(within, r)
            column = jnp.concatenate([column, column], axis=0).astype(BF16)
            hots.append(jnp.concatenate([jnp.where(ids == column, one, zero) for ids in column_ids], axis=0))
            val = row_of(vals, r)
            hi = val.astype(BF16).astype(F32)
            pick = block_ids == row_of(block_no, r)
            parts[0].append(jnp.where(pick, hi, 0.0))
            parts[1].append(jnp.where(pick, val - hi, 0.0))
        held = [
            jnp.concatenate(
                [
                    jnp.concatenate([part[r], blank] if side == 0 else [blank, part[r + 1]], axis=0).astype(BF16)
                    for part in parts
                    for r in range(0, 8, 2)
                ],
                axis=0,
            )
            for side in range(2)
        ]
        held = jnp.concatenate(held, axis=1)
        total = jnp.zeros((T, T), F32)
        for pair in range(4):
            streamed = jnp.concatenate([hots[2 * pair], hots[2 * pair + 1]], axis=1)
            total = jnp.where(pair_of == pair, dot_nt(streamed, held), total)
        flipped = total.T
        both = flipped[0:64] + flipped[64:128]
        for r in range(8):
            dense[pl.ds(turn * WIDTH + first + g * 8 + r, 8, stride=T), :] = both[8 * r : 8 * r + 8]


def pack_kernel(n_front, sizes, pos_ref, cols_ref, vals_ref, diag_ref, *refs):
    out_refs, line_ref = refs[:-1], refs[-1]
    line_ref[...] = jnp.zeros_like(line_ref)
    line_ref[0:1, 0 : diag_ref.shape[1]] = diag_ref[...]
    lane = iota2((8, 2 * KC), 1)
    offset = 0
    for n, (size, out_ref) in enumerate(zip(sizes, out_refs)):
        out_ref[0:size, 0:KC] = cols_ref[offset : offset + size, :].astype(F32)
        out_ref[0:size, KC:] = vals_ref[offset : offset + size, :]
        rank = (pos_ref[0] & ((2 << n) - 1)) * n_front + pos_ref[1]
        first = rank * size % T
        line = pltpu.roll(line_ref[...], (first - offset) & (2 * KC - 1), 1)
        line = jnp.broadcast_to(jnp.where((lane >= first) & (lane < first + size), line, 0.0)[0:1], (8, 2 * KC))
        out_ref[size : size + 8, :] = line
        offset += size


def params():
    return pltpu.CompilerParams(vmem_limit_bytes=VMEM_LIMIT)


def vmem():
    return pl.BlockSpec(memory_space=pltpu.VMEM)


def smem():
    return pl.BlockSpec(memory_space=pltpu.SMEM)


def shape(*dims):
    return jax.ShapeDtypeStruct(dims, F32)


def cost(us):
    return pl.CostEstimate(flops=0, bytes_accessed=int(us * 3.0e6), transcendentals=0)


def call(kernel, out_shape, n_args, n_smem, scratch, us, name):
    outs = out_shape if isinstance(out_shape, tuple) else (out_shape,)
    return pl.pallas_call(
        kernel,
        out_shape=out_shape,
        in_specs=[smem()] * n_smem + [vmem()] * (n_args - n_smem),
        out_specs=(vmem(),) * len(outs) if isinstance(out_shape, tuple) else vmem(),
        scratch_shapes=scratch,
        compiler_params=params(),
        cost_estimate=cost(us),
        name=name,
    )


def row_scratch():
    return pltpu.VMEM((9 * T, T), F32)


def extend_scratch():
    return [pltpu.VMEM((BND, BND), BF16)] * 2 + [pltpu.VMEM((WIDTH, BND), BF16)] * 3


def swap_front(x, mask):
    count = lax.axis_size("front")
    return lax.ppermute(x, "front", [(f, f ^ mask) for f in range(count)])


def hypercube(strip, masks):
    pieces = {0: strip}
    for mask in masks:
        for m in sorted(pieces):
            pieces[m | mask] = swap_front(pieces[m], mask)
    return [pieces[m] for m in range(len(pieces))]


def after(x, done):
    return lax.optimization_barrier((x, done))[0]


def body(leaf_bits, leaf_fronts, coupling_cols, coupling_vals, sep_diag, child_maps):
    n_front = lax.axis_size("front")
    bits = len(leaf_bits)
    n_leaf = 1 << bits
    front = lax.axis_index("front")
    leaf = lax.axis_index(leaf_bits)
    pos = jnp.stack([leaf, front]).astype(jnp.int32)
    strip = leaf_fronts[0]
    half = n_front // 2
    inner = [1 << b for b in range(half.bit_length() - 1)]
    strip_rows = WIDTH // n_front
    panel_strip = strip[:, :SEP]
    cross = swap_front(panel_strip, half)
    sizes = [WIDTH // (n_front << level) for level in range(1, bits + 1)]
    packed = call(
        functools.partial(pack_kernel, n_front, sizes),
        tuple(shape(size + 8, 2 * KC) for size in sizes), 4, 1, [pltpu.VMEM((8, 2 * KC), F32)], 1, "pack_lists",
    )(pos, coupling_cols[0, 0], coupling_vals[0, 0], sep_diag[0])
    panels = hypercube(panel_strip, inner) + hypercube(cross, inner)
    strip3 = after(strip, panels[-1])[:, SEP:]
    cross3 = lax.ppermute(strip3, "front", [(f, f - half) for f in range(half, n_front)])

    lists = []
    for n, size in enumerate(sizes):
        gathered = lax.all_gather(after(packed[n], cross), leaf_bits[bits - 1 - n :] + ("front",), axis=0, tiled=False)
        if size < 8:
            rows = gathered[:, :size].reshape(WIDTH // 8, 8, 2 * KC)
            diag = gathered[:, size].reshape(WIDTH // 8, 8 // size, 2 * KC).sum(1, keepdims=True)
            gathered = jnp.concatenate([rows, jnp.pad(diag, ((0, 0), (0, 7), (0, 0)))], axis=1)
        lists.append(gathered)

    fac, inv, logs = call(
        functools.partial(head_kernel, n_front),
        (shape(SEP, SEP), shape(SEP, T), shape(8, T)), 1 + n_front, 1, [row_scratch()], 300, "head_factor",
    )(pos, *panels)
    pieces3 = hypercube(strip3, inner) + hypercube(after(cross3, inv), inner)
    piece, below = call(
        functools.partial(below_kernel, n_front),
        (shape(strip_rows, SEP), shape(BND, SEP)), 3 + n_front, 1, [pltpu.VMEM((WIDTH, SEP), F32)],
        4, "leaf_below",
    )(pos, fac, inv, *panels)
    pk = call(
        functools.partial(update_kernel, n_front), shape(NPACK, T, T), 3 + n_front, 1,
        [pltpu.VMEM((BND, BND), F32)], 3, "leaf_update",
    )(pos, below, logs, *pieces3)
    pieces = [piece]
    for level in range(1, bits + 1):
        size = sizes[level - 1]
        last = level == bits
        axis = leaf_bits[bits - level]
        if level < 3:
            sibs = [lax.ppermute(pk, axis, [(0, 1), (1, 0)])]
        else:
            part = lax.dynamic_slice_in_dim(pk, (front & 1) * (NPACK // 2), NPACK // 2, 0)
            sibs = [lax.ppermute(part, axis, [(0, 1), (1, 0)])]
        bounds = piece_bounds(last)
        ranks = T // (lists[level - 1].shape[1] - 8)
        mine = pl.pallas_call(
            functools.partial(coupling_kernel, last),
            out_shape=tuple(shape(end - first, T, T) for first, end in zip(bounds, bounds[1:])),
            in_specs=[smem(), pl.BlockSpec(memory_space=pltpu.HBM)],
            out_specs=(vmem(),) * PIECES,
            scratch_shapes=[
                pltpu.VMEM((NB * WIDTH, T), F32),
                pltpu.VMEM((NB, ranks) + lists[level - 1].shape[1:], F32),
                pltpu.SemaphoreType.DMA((NB,)),
            ],
            compiler_params=params(),
            cost_estimate=cost(0.2),
            name="coupling",
        )(pos, after(lists[level - 1], pk))
        theirs = [swap_front(block, 1) for block in mine]
        base = call(
            functools.partial(own_kernel, level, n_leaf, last), shape(pack_index(WIDTH // TILE, 0), TILE, TILE), 3, 1, extend_scratch(), 0.2, "own_child",
        )(pos, pk, child_maps)
        if level >= 3:
            sibs.append(swap_front(after(sibs[0], base), 1))
        gathered = [pltpu.VMEM((NPACK, T, T), F32)] if len(sibs) == 2 else []
        piece, pk = call(
            functools.partial(level_kernel, level, n_leaf, n_front, last, len(sibs)),
            (shape(size, SEP), shape(8, T) if last else shape(NPACK, T, T)), 4 + 2 * PIECES + len(sibs), 1,
            [pltpu.VMEM((WIDTH, WIDTH), F32), pltpu.VMEM((SEP, T), F32), pltpu.VMEM((8, T), F32), row_scratch()]
            + extend_scratch() + gathered,
            300, "level_front",
        )(pos, base, pk, child_maps, *mine, *theirs, *sibs)
        pieces.append(piece)
    return jnp.concatenate(pieces, axis=0)[None, None], pk[0, 0]


def solution(mesh):
    bits = mesh.shape["leaf"].bit_length() - 1
    leaf_bits = tuple(f"leaf{b}" for b in reversed(range(bits)))
    fine = Mesh(mesh.devices.reshape((2,) * bits + (mesh.shape["front"],)), leaf_bits + ("front",))
    placed = (
        P(leaf_bits, "front", None),
        P(leaf_bits, "front", None, None),
        P(leaf_bits, "front", None, None),
        P(leaf_bits, "front", None),
        P(),
    )
    return jax.shard_map(
        functools.partial(body, leaf_bits),
        mesh=fine,
        in_specs=placed,
        out_specs=(P(leaf_bits, "front", None, None), P()),
        check_vma=False,
    )
```

```python
import functools

import jax
import jax.numpy as jnp
from jax import lax
from jax.experimental import pallas as pl
from jax.experimental.pallas import tpu as pltpu
from jax.sharding import Mesh, PartitionSpec as P

SEP = 512
BND = 512
WIDTH = SEP + BND
KC = 128
T = 128
NB = SEP // T
PANEL = 32
PIECES = 3
STEP = 128
TILE = 256
NPACK = NB * (NB + 1) // 2
F32 = jnp.float32
BF16 = jnp.bfloat16
MIB = 1024 * 1024


def pack_index(i, j):
    return i * (i + 1) // 2 + j


def split(x):
    hi = x.astype(BF16)
    return hi, (x - hi.astype(F32)).astype(BF16)


def dot_nt(a, b):
    return lax.dot_general(a, b, (((1,), (1,)), ((), ())), preferred_element_type=F32)


def dot_nn(a, b):
    return lax.dot_general(a, b, (((1,), (0,)), ((), ())), preferred_element_type=F32)


def mm_nt(a, b):
    a_hi, a_lo = split(a)
    b_hi, b_lo = split(b)
    return dot_nt(a_hi, b_hi) + (dot_nt(a_hi, b_lo) + dot_nt(a_lo, b_hi))


def iota2(shape, dim):
    return lax.broadcasted_iota(jnp.int32, shape, dim)


def tri_sym(block):
    n = block.shape[0]
    rows, cols = iota2((n, n), 0), iota2((n, n), 1)
    low = jnp.where(cols <= rows, block, 0.0)
    strict = jnp.where(cols < rows, block, 0.0)
    return low + strict.T


def row_of(x, k):
    return jnp.broadcast_to(x[k : k + 1], (8, T))


def lane_of(x, k):
    return jnp.broadcast_to(x[:, k : k + 1], (8, T))


def tree_sum(terms):
    while len(terms) > 1:
        terms = [sum(terms[i : i + 2][1:], terms[i]) for i in range(0, len(terms), 2)]
    return terms[0]


def reciprocal(x):
    return pl.reciprocal(x, approx=True)


def eliminate_eight(groups, s, c, keep, lane, sub, tmp_ref):
    panel = groups[s]
    inside = (lane >= c) & (lane < c + 8)
    base = c * 9
    for m in range(8):
        tmp_ref[base + 8 * m : base + 8 * m + 8, :] = lane_of(panel, c + m)
    tmp_ref[base + 64 : base + 72, :] = jnp.where(inside, jnp.where(lane - c == sub, 1.0, 0.0), panel)

    def row(n):
        return jnp.broadcast_to(tmp_ref[base + n : base + n + 1, :], (8, T))

    d = {(i, m): row(8 * m + i) for m in range(8) for i in range(m + 1)}
    rows = [row(64 + k) for k in range(8)]
    upper_acc = jnp.zeros((8, T), F32)
    inv_acc = jnp.zeros((8, T), F32)
    to_p, to_q, first = {}, {}, {}
    if s + 1 < keep:
        near = [lane_of(groups[s + 1], c + k) for k in range(8)]
        following = jnp.where(inside, 0.0, groups[s + 1])

    def emit(k, line, entries, root):
        inv_row = line * root
        for m in range(k, 8):
            line = jnp.where(lane == c + m, entries[m], line)
        return jnp.where(sub == k, line * root, upper_acc), jnp.where(sub == k, inv_row, inv_acc)

    for p in range(0, 8, 2):
        q = p + 1
        a, b, e = d[p, p], d[p, q], d[q, q]
        det = a * e - b * b
        recip = reciprocal(det)
        rest = range(q + 1, 8)
        w = {i: e * d[p, i] - b * d[q, i] for i in rest}
        z = {i: a * d[q, i] - b * d[p, i] for i in rest}
        root_p = lax.rsqrt(a)
        inv_a = root_p * root_p
        ratio = b * inv_a
        schur = det * inv_a
        upper_acc, inv_acc = emit(p, rows[p], {m: d[p, m] for m in range(p, 8)}, root_p)
        line_q = {m: d[q, m] - ratio * d[p, m] for m in rest}
        line_q[q] = schur
        upper_acc, inv_acc = emit(q, rows[q] - ratio * rows[p], line_q, lax.rsqrt(schur))
        for i in rest:
            for m in range(i, 8):
                d[i, m] = d[i, m] - (w[i] * d[p, m] + z[i] * d[q, m]) * recip
        for i in rest:
            to_p[p, i], to_q[p, i] = w[i] * recip, z[i] * recip
            rows[i] = rows[i] - (to_p[p, i] * rows[p] + to_q[p, i] * rows[q])
        if s + 1 < keep:
            near_p, near_q = (e * near[p] - b * near[q]) * recip, (a * near[q] - b * near[p]) * recip
            following = following - (near_p * rows[p] + near_q * rows[q])
            for m in rest:
                near[m] = near[m] - (near_p * d[p, m] + near_q * d[q, m])
        first[p] = (e * rows[p] - b * rows[q]) * recip
        first[q] = (a * rows[q] - b * rows[p]) * recip
    if s + 1 < keep:
        groups[s + 1] = following
    if s + 2 < keep:
        sol = [None] * 8
        for p in (6, 4, 2, 0):
            rest = range(p + 2, 8)
            sol[p], sol[p + 1] = first[p], first[p + 1]
            if p < 6:
                sol[p] = sol[p] - tree_sum([to_p[p, m] * sol[m] for m in rest])
                sol[p + 1] = sol[p + 1] - tree_sum([to_q[p, m] * sol[m] for m in rest])
        for g in range(s + 2, keep):
            old = groups[g]
            groups[g] = jnp.where(inside, 0.0, old) - tree_sum([lane_of(old, c + k) * sol[k] for k in range(8)])
    return jnp.where(lane >= c + sub, upper_acc, 0.0), jnp.where(lane <= c + sub, inv_acc, 0.0)


def chol_and_inverse(sym, tmp_ref):
    lane, sub = iota2((8, T), 1), iota2((8, T), 0)
    per = PANEL // 8
    diag = jnp.sum(jnp.where(iota2((T, T), 0) == iota2((T, T), 1), sym, 0.0), axis=0, keepdims=True)
    scale = jnp.broadcast_to(lax.rsqrt(diag), (T, T))
    sym = (sym * scale) * scale.T
    groups = [sym[8 * g : 8 * g + 8] for g in range(T // 8)]
    upper_rows, inv_rows = [], []
    for p in range(T // PANEL):
        for s in range(p * per, (p + 1) * per):
            upper, inv = eliminate_eight(groups, s, 8 * s, (p + 1) * per, lane, sub, tmp_ref)
            upper_rows.append(upper)
            inv_rows.append(inv)
        end = (p + 1) * PANEL
        if end < T:
            both = jnp.concatenate(
                [jnp.where(lane < end, inv_rows[s], upper_rows[s]) for s in range(p * per, (p + 1) * per)], axis=0
            )
            hi, lo = split(both)
            product = lax.dot_general(
                jnp.concatenate([hi, lo, hi], axis=0), jnp.concatenate([hi, hi, lo], axis=0),
                (((0,), (0,)), ((), ())), preferred_element_type=F32,
            )
            done = (lane >= p * PANEL) & (lane < end)
            for g in range((p + 1) * per, T // 8):
                groups[g] = jnp.where(done, 0.0, groups[g]) - product[8 * g : 8 * g + 8]
    return jnp.concatenate(upper_rows, axis=0) * (diag * scale[0:1]), jnp.concatenate(inv_rows, axis=0) * scale


def factor_panel(f_ref, x_ref, log_ref, tmp_ref, rows, blocks):
    width = blocks * T
    log_ref[...] = jnp.zeros_like(log_ref)

    @pl.loop(0, blocks)
    def _(j):
        at = pl.multiple_of(j * T, T)
        upper, inv = chol_and_inverse(tri_sym(f_ref[pl.ds(at, T), pl.ds(at, T)]), tmp_ref)
        f_ref[pl.ds(at, T), pl.ds(at, T)] = upper.T
        x_ref[pl.ds(at, T), :] = inv
        eye = iota2((T, T), 0) == iota2((T, T), 1)
        diag = jnp.sum(jnp.where(eye, upper, 0.0), axis=0, keepdims=True)
        log_ref[0:1, :] += jnp.log(diag)
        for k in range(blocks):
            first = (k + 1) * T
            if first >= rows:
                continue

            @pl.when(j == k)
            def _():
                below = mm_nt(f_ref[first:rows, k * T : first], inv)
                f_ref[first:rows, k * T : first] = below
                if first < width:
                    f_ref[first:rows, first:width] -= mm_nt(below, below[: width - first])


def zero_above(f_ref, blocks):
    for i in range(blocks - 1):
        f_ref[i * T : (i + 1) * T, (i + 1) * T : blocks * T] = jnp.zeros((T, (blocks - 1 - i) * T), F32)


def log_total(log_ref):
    return 2.0 * jnp.sum(log_ref[0:1, :], axis=1, keepdims=True)


def write_own(out_ref, f_ref, start):
    size = out_ref.shape[0]
    if size % 8 == 0:
        out_ref[...] = f_ref[pl.ds(pl.multiple_of(start, 8), size), 0:SEP]
    else:
        base = pl.multiple_of(start // 8 * 8, 8)
        block = f_ref[pl.ds(base, 8), 0:SEP]
        offset = start - base
        piece = block[0:size]
        for shift in range(size, 8, size):
            piece = jnp.where(offset == shift, block[shift : shift + size], piece)
        out_ref[...] = piece


def write_update(pk_ref, below, tail_of, log_value):
    hi, lo = split(below)
    rows, cols = iota2((T, T), 0), iota2((T, T), 1)
    for i in range(NB):
        here = slice(i * T, (i + 1) * T)
        upto = slice(0, (i + 1) * T)
        prod = dot_nt(hi[here], hi[upto]) + (dot_nt(hi[here], lo[upto]) + dot_nt(lo[here], hi[upto]))
        for j in range(i + 1):
            block = tail_of(i, j) - prod[:, j * T : (j + 1) * T]
            if i == 0:
                block = jnp.where((rows == 0) & (cols == T - 1), log_value, block)
            pk_ref[pack_index(i, j)] = block


def place(pieces, work, front, want_tail):
    count = len(pieces)
    half = count // 2
    size = pieces[0].shape[0]
    for m, piece in enumerate(pieces):
        source = front ^ m

        @pl.when((source >= half) == want_tail)
        def _():
            at = pl.multiple_of((source & (half - 1)) * size, 8)
            work[pl.ds(at, size), :] = piece[...]


def head_kernel(n, pos_ref, *refs):
    pieces, (fac_ref, x_ref, log_ref, tmp_ref) = refs[:n], refs[n:]
    place(pieces, fac_ref, pos_ref[1], False)
    factor_panel(fac_ref, x_ref, log_ref, tmp_ref, SEP, NB)
    zero_above(fac_ref, NB)


def below_kernel(n, pos_ref, fac, inv, *refs):
    pieces, (own_ref, below_ref, stack) = refs[:n], refs[n:]
    front = pos_ref[1]
    place(pieces, below_ref, front, True)
    for j in range(NB):
        here = slice(j * T, (j + 1) * T)
        solved = mm_nt(below_ref[:, here], inv[here, :])
        below_ref[:, here] = solved
        if j + 1 < NB:
            rest = slice((j + 1) * T, SEP)
            below_ref[:, rest] -= mm_nt(solved, fac[rest, here])
    stack[0:SEP, :] = fac[...]
    stack[SEP:, :] = below_ref[...]
    write_own(own_ref, stack, front * own_ref.shape[0])


def update_kernel(n, pos_ref, below_ref, log_ref, *refs):
    pieces, (pk_ref, tail_ref) = refs[:n], refs[n:]
    place(pieces, tail_ref, pos_ref[1], True)

    def tail_of(i, j):
        return tail_ref[i * T : (i + 1) * T, j * T : (j + 1) * T]

    write_update(pk_ref, below_ref[...], tail_of, log_total(log_ref))


def expand(pk_ref, u_hi, u_lo):
    rows, cols = iota2((T, T), 0), iota2((T, T), 1)
    for i in range(NB):
        for j in range(i + 1):
            block = pk_ref[pack_index(i, j)]
            if i == j:
                low = jnp.where(cols <= rows, block, 0.0)
                block = low + jnp.where(cols < rows, block, 0.0).T
            hi, lo = split(block)
            u_hi[i * T : (i + 1) * T, j * T : (j + 1) * T] = hi
            u_lo[i * T : (i + 1) * T, j * T : (j + 1) * T] = lo
            if i != j:
                hi, lo = split(block.T)
                u_hi[j * T : (j + 1) * T, i * T : (i + 1) * T] = hi
                u_lo[j * T : (j + 1) * T, i * T : (i + 1) * T] = lo


def extend_add(pk_ref, index_row, emit, last, u_hi, u_lo, hot, y_hi, y_lo):
    expand(pk_ref, u_hi, u_lo)

    @pl.loop(0, WIDTH // TILE)
    def _(tile):
        at = pl.multiple_of(tile * TILE, TILE)
        ids = iota2((TILE, BND), 0) + at
        match = jnp.where(ids == index_row, 1.0, 0.0).astype(BF16)
        hot[pl.ds(at, TILE), :] = match
        y_hi[pl.ds(at, TILE), :] = dot_nn(match, u_hi[...]).astype(BF16)
        y_lo[pl.ds(at, TILE), :] = dot_nn(match, u_lo[...]).astype(BF16)

    for a in range(WIDTH // TILE):
        here = slice(a * TILE, (a + 1) * TILE)
        for b in range(a + 1):
            if last and b * TILE >= SEP:
                continue
            there = slice(b * TILE, (b + 1) * TILE)
            part = dot_nt(y_hi[here, :], hot[there, :]) + dot_nt(y_lo[here, :], hot[there, :])
            emit(a, b, part)


def map_row(level, n_leaf, pos_ref, maps_ref, sibling):
    base = 2 * n_leaf - 2 * (n_leaf >> (level - 1))
    own = pos_ref[0] >> (level - 1)
    number = base + (own ^ 1 if sibling else own)
    return maps_ref[pl.ds(number, 1), :]


def owned_blocks(core, last):
    rows = [2 * turn + (turn + core) % 2 for turn in range(WIDTH // T // 2)]
    return [(i, j) for i in rows for j in range(min(i + 1, NB if last else 2 * NB))]


def piece_bounds(last):
    total = len(owned_blocks(0, last))
    return [total * n // PIECES for n in range(PIECES + 1)]


def coupling_kernel(last, pos_ref, lists_ref, *refs):
    out_refs, (dense, held_ref, sems) = refs[:-3], refs[-3:]
    bounds = piece_bounds(last)
    core = pos_ref[1] & 1
    size = lists_ref.shape[1] - 8
    ranks = T // size
    eye = iota2((T, T), 0) == iota2((T, T), 1)
    def fetch(turn):
        i = 2 * turn + ((turn + core) & 1)
        return pltpu.make_async_copy(lists_ref.at[pl.ds(i * ranks, ranks)], held_ref.at[turn], sems.at[turn])

    for turn in range(NB):
        fetch(turn).start()

    @pl.loop(0, NB * T // STEP)
    def _(step):
        turn = step // (T // STEP)

        @pl.when(step % (T // STEP) == 0)
        def _():
            fetch(turn).wait()

        spread_rows(held_ref, dense, turn, step % (T // STEP) * STEP)

    for owner in range(2):

        @pl.when(core == owner)
        def _():
            for n, (i, j) in enumerate(owned_blocks(owner, last)):
                turn = i // 2
                block = dense[turn * WIDTH + j * T : turn * WIDTH + (j + 1) * T, :]
                if i == j:
                    diag = held_ref[turn, 0, size : size + 1, 0:T]
                    for m in range(1, ranks):
                        diag = diag + held_ref[turn, m, size : size + 1, 0:T]
                    block = block + jnp.where(eye, diag, 0.0)
                p = max(m for m in range(PIECES) if bounds[m] <= n)
                out_refs[p][n - bounds[p]] = block


def own_kernel(level, n_leaf, last, pos_ref, pk_ref, maps_ref, f_ref, u_hi, u_lo, hot, y_hi, y_lo):
    index_row = map_row(level, n_leaf, pos_ref, maps_ref, False)

    def emit(a, b, part):
        f_ref[pack_index(a, b)] = part

    extend_add(pk_ref, index_row, emit, last, u_hi, u_lo, hot, y_hi, y_lo)


def level_kernel(
    level, n_leaf, n_front, last, n_sib,
    pos_ref, base_ref, own_pk, maps_ref, *refs,
):
    mine_refs, theirs_refs, refs = refs[:PIECES], refs[PIECES : 2 * PIECES], refs[2 * PIECES :]
    sibs, (own_ref, next_ref, f_ref, x_ref, log_ref, tmp_ref, u_hi, u_lo, hot, y_hi, y_lo, *gathered) = (
        refs[:n_sib], refs[n_sib:],
    )
    core = pos_ref[1] & 1
    if n_sib == 1:
        sib_pk = sibs[0]
    else:
        sib_pk = gathered[0]
        sib_pk[pl.ds(core * (NPACK // 2), NPACK // 2)] = sibs[0][...]
        sib_pk[pl.ds((1 - core) * (NPACK // 2), NPACK // 2)] = sibs[1][...]
    index_row = map_row(level, n_leaf, pos_ref, maps_ref, True)
    where_is = {}
    bounds = piece_bounds(last)
    for owner in range(2):
        for n, block in enumerate(owned_blocks(owner, last)):
            p = max(m for m in range(PIECES) if bounds[m] <= n)
            where_is[block] = owner, p, n - bounds[p]

    def emit(a, b, part):
        per = TILE // T
        for r in range(per):
            for h in range(per):
                i, j = a * per + r, b * per + h
                if j > i:
                    continue
                owner, p, n = where_is[i, j]
                here, there = slice(i * T, (i + 1) * T), slice(j * T, (j + 1) * T)
                dense = jnp.where(core == owner, mine_refs[p][n], theirs_refs[p][n])
                mine, its = slice(r * T, (r + 1) * T), slice(h * T, (h + 1) * T)
                f_ref[here, there] = (base_ref[pack_index(a, b), mine, its] + part[mine, its]) + dense

    extend_add(sib_pk, index_row, emit, last, u_hi, u_lo, hot, y_hi, y_lo)
    factor_panel(f_ref, x_ref, log_ref, tmp_ref, WIDTH, NB)
    zero_above(f_ref, NB)
    rank = (pos_ref[0] & ((1 << level) - 1)) * n_front + pos_ref[1]
    write_own(own_ref, f_ref, rank * own_ref.shape[0])
    kids_log = own_pk[0][0:1, T - 1 : T] + sib_pk[0][0:1, T - 1 : T]
    log_value = kids_log + log_total(log_ref)
    if last:
        next_ref[...] = jnp.broadcast_to(log_value, next_ref.shape)
    else:

        def tail_of(i, j):
            return f_ref[SEP + i * T : SEP + (i + 1) * T, SEP + j * T : SEP + (j + 1) * T]

        write_update(next_ref, f_ref[SEP:, 0:SEP], tail_of, log_value)


def spread_rows(lists_ref, dense, turn, first):
    block_ids = iota2((8, KC), 0).astype(F32)
    column_ids = [(iota2((16, KC), 0) + 16 * j).astype(F32).astype(BF16) for j in range(T // 16)]
    one, zero = jnp.ones((16, KC), BF16), jnp.zeros((16, KC), BF16)
    blank = jnp.zeros((8, KC), F32)
    pair_of = iota2((T, T), 1) % 64 // 16
    size = lists_ref.shape[2] - 8
    for g in range(STEP // 8):
        hots, parts = [], ([], [])
        rank = (first + g * 8) // size
        at = pl.multiple_of((first + g * 8) % size, 8)
        cols = lists_ref[turn, rank, pl.ds(at, 8), 0:KC]
        vals = lists_ref[turn, rank, pl.ds(at, 8), KC:]
        block_no = jnp.floor(cols * (1.0 / T))
        within = cols - block_no * T
        for r in range(8):
            column = row_of(within, r)
            column = jnp.concatenate([column, column], axis=0).astype(BF16)
            hots.append(jnp.concatenate([jnp.where(ids == column, one, zero) for ids in column_ids], axis=0))
            val = row_of(vals, r)
            hi = val.astype(BF16).astype(F32)
            pick = block_ids == row_of(block_no, r)
            parts[0].append(jnp.where(pick, hi, 0.0))
            parts[1].append(jnp.where(pick, val - hi, 0.0))
        held = [
            jnp.concatenate(
                [
                    jnp.concatenate([part[r], blank] if side == 0 else [blank, part[r + 1]], axis=0).astype(BF16)
                    for part in parts
                    for r in range(0, 8, 2)
                ],
                axis=0,
            )
            for side in range(2)
        ]
        held = jnp.concatenate(held, axis=1)
        total = jnp.zeros((T, T), F32)
        for pair in range(4):
            streamed = jnp.concatenate([hots[2 * pair], hots[2 * pair + 1]], axis=1)
            total = jnp.where(pair_of == pair, dot_nt(streamed, held), total)
        flipped = total.T
        both = flipped[0:64] + flipped[64:128]
        for r in range(8):
            dense[pl.ds(turn * WIDTH + first + g * 8 + r, 8, stride=T), :] = both[8 * r : 8 * r + 8]


def pack_kernel(n_front, sizes, pos_ref, cols_ref, vals_ref, diag_ref, *refs):
    out_refs, line_ref = refs[:-1], refs[-1]
    line_ref[...] = jnp.zeros_like(line_ref)
    line_ref[0:1, 0 : diag_ref.shape[1]] = diag_ref[...]
    lane = iota2((8, 2 * KC), 1)
    offset = 0
    for n, (size, out_ref) in enumerate(zip(sizes, out_refs)):
        out_ref[0:size, 0:KC] = cols_ref[offset : offset + size, :].astype(F32)
        out_ref[0:size, KC:] = vals_ref[offset : offset + size, :]
        rank = (pos_ref[0] & ((2 << n) - 1)) * n_front + pos_ref[1]
        first = rank * size % T
        line = pltpu.roll(line_ref[...], (first - offset) & (2 * KC - 1), 1)
        line = jnp.broadcast_to(jnp.where((lane >= first) & (lane < first + size), line, 0.0)[0:1], (8, 2 * KC))
        out_ref[size : size + 8, :] = line
        offset += size


def params(mib):
    return pltpu.CompilerParams(vmem_limit_bytes=mib * MIB)


def vmem():
    return pl.BlockSpec(memory_space=pltpu.VMEM)


def smem():
    return pl.BlockSpec(memory_space=pltpu.SMEM)


def shape(*dims):
    return jax.ShapeDtypeStruct(dims, F32)


def cost(us):
    return pl.CostEstimate(flops=0, bytes_accessed=int(us * 3.0e6), transcendentals=0)


def call(kernel, out_shape, n_args, n_smem, scratch, us, name, mib=10):
    outs = out_shape if isinstance(out_shape, tuple) else (out_shape,)
    return pl.pallas_call(
        kernel,
        out_shape=out_shape,
        in_specs=[smem()] * n_smem + [vmem()] * (n_args - n_smem),
        out_specs=(vmem(),) * len(outs) if isinstance(out_shape, tuple) else vmem(),
        scratch_shapes=scratch,
        compiler_params=params(mib),
        cost_estimate=cost(us),
        name=name,
    )


def row_scratch():
    return pltpu.VMEM((9 * T, T), F32)


def extend_scratch():
    return [pltpu.VMEM((BND, BND), BF16)] * 2 + [pltpu.VMEM((WIDTH, BND), BF16)] * 3


def swap_front(x, mask):
    count = lax.axis_size("front")
    return lax.ppermute(x, "front", [(f, f ^ mask) for f in range(count)])


def hypercube(strip, masks):
    pieces = {0: strip}
    for mask in masks:
        for m in sorted(pieces):
            pieces[m | mask] = swap_front(pieces[m], mask)
    return [pieces[m] for m in range(len(pieces))]


def after(x, done):
    return lax.optimization_barrier((x, done))[0]


def body(leaf_bits, leaf_fronts, coupling_cols, coupling_vals, sep_diag, child_maps):
    n_front = lax.axis_size("front")
    bits = len(leaf_bits)
    n_leaf = 1 << bits
    front = lax.axis_index("front")
    leaf = lax.axis_index(leaf_bits)
    pos = jnp.stack([leaf, front]).astype(jnp.int32)
    strip = leaf_fronts[0]
    half = n_front // 2
    inner = [1 << b for b in range(half.bit_length() - 1)]
    strip_rows = WIDTH // n_front
    panel_strip = strip[:, :SEP]
    cross = swap_front(panel_strip, half)
    sizes = [WIDTH // (n_front << level) for level in range(1, bits + 1)]
    packed = call(
        functools.partial(pack_kernel, n_front, sizes),
        tuple(shape(size + 8, 2 * KC) for size in sizes), 4, 1, [pltpu.VMEM((8, 2 * KC), F32)], 1, "pack_lists",
    )(pos, coupling_cols[0, 0], coupling_vals[0, 0], sep_diag[0])
    panels = hypercube(panel_strip, inner) + hypercube(cross, inner)
    strip3 = after(strip[:, SEP:], panels[-1])
    cross3 = lax.ppermute(strip3, "front", [(f, f - half) for f in range(half, n_front)])

    lists = []
    for n, size in enumerate(sizes):
        gathered = lax.all_gather(after(packed[n], cross), leaf_bits[bits - 1 - n :] + ("front",), axis=0, tiled=False)
        if size < 8:
            rows = gathered[:, :size].reshape(WIDTH // 8, 8, 2 * KC)
            diag = gathered[:, size].reshape(WIDTH // 8, 8 // size, 2 * KC).sum(1, keepdims=True)
            gathered = jnp.concatenate([rows, jnp.pad(diag, ((0, 0), (0, 7), (0, 0)))], axis=1)
        lists.append(gathered)

    fac, inv, logs = call(
        functools.partial(head_kernel, n_front),
        (shape(SEP, SEP), shape(SEP, T), shape(8, T)), 1 + n_front, 1, [row_scratch()], 300, "head_factor",
    )(pos, *panels)
    pieces3 = hypercube(strip3, inner) + hypercube(after(cross3, inv), inner)
    piece, below = call(
        functools.partial(below_kernel, n_front),
        (shape(strip_rows, SEP), shape(BND, SEP)), 3 + n_front, 1, [pltpu.VMEM((WIDTH, SEP), F32)],
        4, "leaf_below",
    )(pos, fac, inv, *panels)
    pk = call(
        functools.partial(update_kernel, n_front), shape(NPACK, T, T), 3 + n_front, 1,
        [pltpu.VMEM((BND, BND), F32)], 3, "leaf_update",
    )(pos, below, logs, *pieces3)
    pieces = [piece]
    for level in range(1, bits + 1):
        size = sizes[level - 1]
        last = level == bits
        axis = leaf_bits[bits - level]
        if level < 3:
            sibs = [lax.ppermute(pk, axis, [(0, 1), (1, 0)])]
        else:
            part = lax.dynamic_slice_in_dim(pk, (front & 1) * (NPACK // 2), NPACK // 2, 0)
            sibs = [lax.ppermute(part, axis, [(0, 1), (1, 0)])]
        bounds = piece_bounds(last)
        ranks = T // (lists[level - 1].shape[1] - 8)
        mine = pl.pallas_call(
            functools.partial(coupling_kernel, last),
            out_shape=tuple(shape(end - first, T, T) for first, end in zip(bounds, bounds[1:])),
            in_specs=[smem(), pl.BlockSpec(memory_space=pltpu.HBM)],
            out_specs=(vmem(),) * PIECES,
            scratch_shapes=[
                pltpu.VMEM((NB * WIDTH, T), F32),
                pltpu.VMEM((NB, ranks) + lists[level - 1].shape[1:], F32),
                pltpu.SemaphoreType.DMA((NB,)),
            ],
            compiler_params=params(6),
            cost_estimate=cost(0.2),
            name="coupling",
        )(pos, after(lists[level - 1], pk))
        theirs = [swap_front(block, 1) for block in mine]
        base = call(
            functools.partial(own_kernel, level, n_leaf, last), shape(pack_index(WIDTH // TILE, 0), TILE, TILE), 3, 1, extend_scratch(), 0.2, "own_child",
        )(pos, pk, child_maps)
        if level >= 3:
            sibs.append(swap_front(after(sibs[0], base), 1))
        gathered = [pltpu.VMEM((NPACK, T, T), F32)] if len(sibs) == 2 else []
        piece, pk = call(
            functools.partial(level_kernel, level, n_leaf, n_front, last, len(sibs)),
            (shape(size, SEP), shape(8, T) if last else shape(NPACK, T, T)), 4 + 2 * PIECES + len(sibs), 1,
            [pltpu.VMEM((WIDTH, WIDTH), F32), pltpu.VMEM((SEP, T), F32), pltpu.VMEM((8, T), F32), row_scratch()]
            + extend_scratch() + gathered,
            300, "level_front", 14,
        )(pos, base, pk, child_maps, *mine, *theirs, *sibs)
        pieces.append(piece)
    return jnp.concatenate(pieces, axis=0)[None, None], pk[0, 0]


def solution(mesh):
    bits = mesh.shape["leaf"].bit_length() - 1
    leaf_bits = tuple(f"leaf{b}" for b in reversed(range(bits)))
    fine = Mesh(mesh.devices.reshape((2,) * bits + (mesh.shape["front"],)), leaf_bits + ("front",))
    placed = (
        P(leaf_bits, "front", None),
        P(leaf_bits, "front", None, None),
        P(leaf_bits, "front", None, None),
        P(leaf_bits, "front", None),
        P(),
    )
    return jax.shard_map(
        functools.partial(body, leaf_bits),
        mesh=fine,
        in_specs=placed,
        out_specs=(P(leaf_bits, "front", None, None), P()),
        check_vma=False,
    )
```

```python
import functools

import jax
import jax.numpy as jnp
from jax import lax
from jax.experimental import pallas as pl
from jax.experimental.pallas import tpu as pltpu
from jax.sharding import Mesh, PartitionSpec as P

SEP = 512
BND = 512
WIDTH = SEP + BND
KC = 128
T = 128
NB = SEP // T
PANEL = 32
PIECES = 2
STEP = 64
TILE = 256
NPACK = NB * (NB + 1) // 2
F32 = jnp.float32
BF16 = jnp.bfloat16
MIB = 1024 * 1024


def pack_index(i, j):
    return i * (i + 1) // 2 + j


def split(x):
    hi = x.astype(BF16)
    return hi, (x - hi.astype(F32)).astype(BF16)


def dot_nt(a, b):
    return lax.dot_general(a, b, (((1,), (1,)), ((), ())), preferred_element_type=F32)


def dot_nn(a, b):
    return lax.dot_general(a, b, (((1,), (0,)), ((), ())), preferred_element_type=F32)


def mm_nt(a, b):
    a_hi, a_lo = split(a)
    b_hi, b_lo = split(b)
    return dot_nt(a_hi, b_hi) + (dot_nt(a_hi, b_lo) + dot_nt(a_lo, b_hi))


def iota2(shape, dim):
    return lax.broadcasted_iota(jnp.int32, shape, dim)


def tri_sym(block):
    n = block.shape[0]
    rows, cols = iota2((n, n), 0), iota2((n, n), 1)
    low = jnp.where(cols <= rows, block, 0.0)
    strict = jnp.where(cols < rows, block, 0.0)
    return low + strict.T


def row_of(x, k):
    return jnp.broadcast_to(x[k : k + 1], (8, T))


def lane_of(x, k):
    return jnp.broadcast_to(x[:, k : k + 1], (8, T))


def tree_sum(terms):
    while len(terms) > 1:
        terms = [sum(terms[i : i + 2][1:], terms[i]) for i in range(0, len(terms), 2)]
    return terms[0]


def reciprocal(x):
    return pl.reciprocal(x, approx=True)


def eliminate_eight(groups, s, c, keep, lane, sub, tmp_ref):
    panel = groups[s]
    inside = (lane >= c) & (lane < c + 8)
    base = c * 9
    for m in range(8):
        tmp_ref[base + 8 * m : base + 8 * m + 8, :] = lane_of(panel, c + m)
    tmp_ref[base + 64 : base + 72, :] = jnp.where(inside, jnp.where(lane - c == sub, 1.0, 0.0), panel)

    def row(n):
        return jnp.broadcast_to(tmp_ref[base + n : base + n + 1, :], (8, T))

    d = {(i, m): row(8 * m + i) for m in range(8) for i in range(m + 1)}
    rows = [row(64 + k) for k in range(8)]
    upper_acc = jnp.zeros((8, T), F32)
    inv_acc = jnp.zeros((8, T), F32)
    to_p, to_q, first = {}, {}, {}
    if s + 1 < keep:
        near = [lane_of(groups[s + 1], c + k) for k in range(8)]
        following = jnp.where(inside, 0.0, groups[s + 1])

    def emit(k, line, entries, root):
        inv_row = line * root
        for m in range(k, 8):
            line = jnp.where(lane == c + m, entries[m], line)
        return jnp.where(sub == k, line * root, upper_acc), jnp.where(sub == k, inv_row, inv_acc)

    for p in range(0, 8, 2):
        q = p + 1
        a, b, e = d[p, p], d[p, q], d[q, q]
        det = a * e - b * b
        recip = reciprocal(det)
        rest = range(q + 1, 8)
        w = {i: e * d[p, i] - b * d[q, i] for i in rest}
        z = {i: a * d[q, i] - b * d[p, i] for i in rest}
        root_p = lax.rsqrt(a)
        inv_a = root_p * root_p
        ratio = b * inv_a
        schur = det * inv_a
        upper_acc, inv_acc = emit(p, rows[p], {m: d[p, m] for m in range(p, 8)}, root_p)
        line_q = {m: d[q, m] - ratio * d[p, m] for m in rest}
        line_q[q] = schur
        upper_acc, inv_acc = emit(q, rows[q] - ratio * rows[p], line_q, lax.rsqrt(schur))
        for i in rest:
            for m in range(i, 8):
                d[i, m] = d[i, m] - (w[i] * d[p, m] + z[i] * d[q, m]) * recip
        for i in rest:
            to_p[p, i], to_q[p, i] = w[i] * recip, z[i] * recip
            rows[i] = rows[i] - (to_p[p, i] * rows[p] + to_q[p, i] * rows[q])
        if s + 1 < keep:
            near_p, near_q = (e * near[p] - b * near[q]) * recip, (a * near[q] - b * near[p]) * recip
            following = following - (near_p * rows[p] + near_q * rows[q])
            for m in rest:
                near[m] = near[m] - (near_p * d[p, m] + near_q * d[q, m])
        first[p] = (e * rows[p] - b * rows[q]) * recip
        first[q] = (a * rows[q] - b * rows[p]) * recip
    if s + 1 < keep:
        groups[s + 1] = following
    if s + 2 < keep:
        sol = [None] * 8
        for p in (6, 4, 2, 0):
            rest = range(p + 2, 8)
            sol[p], sol[p + 1] = first[p], first[p + 1]
            if p < 6:
                sol[p] = sol[p] - tree_sum([to_p[p, m] * sol[m] for m in rest])
                sol[p + 1] = sol[p + 1] - tree_sum([to_q[p, m] * sol[m] for m in rest])
        for g in range(s + 2, keep):
            old = groups[g]
            groups[g] = jnp.where(inside, 0.0, old) - tree_sum([lane_of(old, c + k) * sol[k] for k in range(8)])
    return jnp.where(lane >= c + sub, upper_acc, 0.0), jnp.where(lane <= c + sub, inv_acc, 0.0)


def chol_and_inverse(sym, tmp_ref):
    lane, sub = iota2((8, T), 1), iota2((8, T), 0)
    per = PANEL // 8
    diag = jnp.sum(jnp.where(iota2((T, T), 0) == iota2((T, T), 1), sym, 0.0), axis=0, keepdims=True)
    scale = jnp.broadcast_to(lax.rsqrt(diag), (T, T))
    sym = (sym * scale) * scale.T
    groups = [sym[8 * g : 8 * g + 8] for g in range(T // 8)]
    upper_rows, inv_rows = [], []
    for p in range(T // PANEL):
        for s in range(p * per, (p + 1) * per):
            upper, inv = eliminate_eight(groups, s, 8 * s, (p + 1) * per, lane, sub, tmp_ref)
            upper_rows.append(upper)
            inv_rows.append(inv)
        end = (p + 1) * PANEL
        if end < T:
            both = jnp.concatenate(
                [jnp.where(lane < end, inv_rows[s], upper_rows[s]) for s in range(p * per, (p + 1) * per)], axis=0
            )
            hi, lo = split(both)
            product = lax.dot_general(
                jnp.concatenate([hi, lo, hi], axis=0), jnp.concatenate([hi, hi, lo], axis=0),
                (((0,), (0,)), ((), ())), preferred_element_type=F32,
            )
            done = (lane >= p * PANEL) & (lane < end)
            for g in range((p + 1) * per, T // 8):
                groups[g] = jnp.where(done, 0.0, groups[g]) - product[8 * g : 8 * g + 8]
    return jnp.concatenate(upper_rows, axis=0) * (diag * scale[0:1]), jnp.concatenate(inv_rows, axis=0) * scale


def factor_panel(f_ref, x_ref, log_ref, tmp_ref, rows, blocks):
    width = blocks * T
    log_ref[...] = jnp.zeros_like(log_ref)

    @pl.loop(0, blocks)
    def _(j):
        at = pl.multiple_of(j * T, T)
        upper, inv = chol_and_inverse(tri_sym(f_ref[pl.ds(at, T), pl.ds(at, T)]), tmp_ref)
        f_ref[pl.ds(at, T), pl.ds(at, T)] = upper.T
        x_ref[pl.ds(at, T), :] = inv
        eye = iota2((T, T), 0) == iota2((T, T), 1)
        diag = jnp.sum(jnp.where(eye, upper, 0.0), axis=0, keepdims=True)
        log_ref[0:1, :] += jnp.log(diag)
        for k in range(blocks):
            first = (k + 1) * T
            if first >= rows:
                continue

            @pl.when(j == k)
            def _():
                below = mm_nt(f_ref[first:rows, k * T : first], inv)
                f_ref[first:rows, k * T : first] = below
                if first < width:
                    f_ref[first:rows, first:width] -= mm_nt(below, below[: width - first])


def zero_above(f_ref, blocks):
    for i in range(blocks - 1):
        f_ref[i * T : (i + 1) * T, (i + 1) * T : blocks * T] = jnp.zeros((T, (blocks - 1 - i) * T), F32)


def log_total(log_ref):
    return 2.0 * jnp.sum(log_ref[0:1, :], axis=1, keepdims=True)


def write_own(out_ref, f_ref, start):
    size = out_ref.shape[0]
    if size % 8 == 0:
        out_ref[...] = f_ref[pl.ds(pl.multiple_of(start, 8), size), 0:SEP]
    else:
        base = pl.multiple_of(start // 8 * 8, 8)
        block = f_ref[pl.ds(base, 8), 0:SEP]
        offset = start - base
        piece = block[0:size]
        for shift in range(size, 8, size):
            piece = jnp.where(offset == shift, block[shift : shift + size], piece)
        out_ref[...] = piece


def write_update(pk_ref, below, tail_of, log_value):
    hi, lo = split(below)
    rows, cols = iota2((T, T), 0), iota2((T, T), 1)
    for i in range(NB):
        here = slice(i * T, (i + 1) * T)
        upto = slice(0, (i + 1) * T)
        prod = dot_nt(hi[here], hi[upto]) + (dot_nt(hi[here], lo[upto]) + dot_nt(lo[here], hi[upto]))
        for j in range(i + 1):
            block = tail_of(i, j) - prod[:, j * T : (j + 1) * T]
            if i == 0:
                block = jnp.where((rows == 0) & (cols == T - 1), log_value, block)
            pk_ref[pack_index(i, j)] = block


def place(pieces, work, front, want_tail):
    count = len(pieces)
    half = count // 2
    size = pieces[0].shape[0]
    for m, piece in enumerate(pieces):
        source = front ^ m

        @pl.when((source >= half) == want_tail)
        def _():
            at = pl.multiple_of((source & (half - 1)) * size, 8)
            work[pl.ds(at, size), :] = piece[...]


def head_kernel(n, pos_ref, *refs):
    pieces, (fac_ref, x_ref, log_ref, tmp_ref) = refs[:n], refs[n:]
    place(pieces, fac_ref, pos_ref[1], False)
    factor_panel(fac_ref, x_ref, log_ref, tmp_ref, SEP, NB)
    zero_above(fac_ref, NB)


def below_kernel(n, pos_ref, fac, inv, *refs):
    pieces, (own_ref, below_ref, stack) = refs[:n], refs[n:]
    front = pos_ref[1]
    place(pieces, below_ref, front, True)
    for j in range(NB):
        here = slice(j * T, (j + 1) * T)
        solved = mm_nt(below_ref[:, here], inv[here, :])
        below_ref[:, here] = solved
        if j + 1 < NB:
            rest = slice((j + 1) * T, SEP)
            below_ref[:, rest] -= mm_nt(solved, fac[rest, here])
    stack[0:SEP, :] = fac[...]
    stack[SEP:, :] = below_ref[...]
    write_own(own_ref, stack, front * own_ref.shape[0])


def update_kernel(n, pos_ref, below_ref, log_ref, *refs):
    pieces, (pk_ref, tail_ref) = refs[:n], refs[n:]
    place(pieces, tail_ref, pos_ref[1], True)

    def tail_of(i, j):
        return tail_ref[i * T : (i + 1) * T, j * T : (j + 1) * T]

    write_update(pk_ref, below_ref[...], tail_of, log_total(log_ref))


def expand(pk_ref, u_hi, u_lo):
    rows, cols = iota2((T, T), 0), iota2((T, T), 1)
    for i in range(NB):
        for j in range(i + 1):
            block = pk_ref[pack_index(i, j)]
            if i == j:
                low = jnp.where(cols <= rows, block, 0.0)
                block = low + jnp.where(cols < rows, block, 0.0).T
            hi, lo = split(block)
            u_hi[i * T : (i + 1) * T, j * T : (j + 1) * T] = hi
            u_lo[i * T : (i + 1) * T, j * T : (j + 1) * T] = lo
            if i != j:
                hi, lo = split(block.T)
                u_hi[j * T : (j + 1) * T, i * T : (i + 1) * T] = hi
                u_lo[j * T : (j + 1) * T, i * T : (i + 1) * T] = lo


def extend_add(pk_ref, index_row, emit, last, u_hi, u_lo, hot, y_hi, y_lo):
    expand(pk_ref, u_hi, u_lo)

    @pl.loop(0, WIDTH // TILE)
    def _(tile):
        at = pl.multiple_of(tile * TILE, TILE)
        ids = iota2((TILE, BND), 0) + at
        match = jnp.where(ids == index_row, 1.0, 0.0).astype(BF16)
        hot[pl.ds(at, TILE), :] = match
        y_hi[pl.ds(at, TILE), :] = dot_nn(match, u_hi[...]).astype(BF16)
        y_lo[pl.ds(at, TILE), :] = dot_nn(match, u_lo[...]).astype(BF16)

    for a in range(WIDTH // TILE):
        here = slice(a * TILE, (a + 1) * TILE)
        for b in range(a + 1):
            if last and b * TILE >= SEP:
                continue
            there = slice(b * TILE, (b + 1) * TILE)
            part = dot_nt(y_hi[here, :], hot[there, :]) + dot_nt(y_lo[here, :], hot[there, :])
            emit(a, b, part)


def map_row(level, n_leaf, pos_ref, maps_ref, sibling):
    base = 2 * n_leaf - 2 * (n_leaf >> (level - 1))
    own = pos_ref[0] >> (level - 1)
    number = base + (own ^ 1 if sibling else own)
    return maps_ref[pl.ds(number, 1), :]


def owned_blocks(core, last):
    rows = [2 * turn + (turn + core) % 2 for turn in range(WIDTH // T // 2)]
    return [(i, j) for i in rows for j in range(min(i + 1, NB if last else 2 * NB))]


def piece_bounds(last):
    total = len(owned_blocks(0, last))
    return [total * n // PIECES for n in range(PIECES + 1)]


def coupling_kernel(last, pos_ref, lists_ref, *refs):
    out_refs, (dense, held_ref, sems) = refs[:-3], refs[-3:]
    bounds = piece_bounds(last)
    core = pos_ref[1] & 1
    size = lists_ref.shape[1] - 8
    ranks = T // size
    eye = iota2((T, T), 0) == iota2((T, T), 1)
    def fetch(turn):
        i = 2 * turn + ((turn + core) & 1)
        return pltpu.make_async_copy(lists_ref.at[pl.ds(i * ranks, ranks)], held_ref.at[turn], sems.at[turn])

    for turn in range(NB):
        fetch(turn).start()

    @pl.loop(0, NB * T // STEP)
    def _(step):
        turn = step // (T // STEP)

        @pl.when(step % (T // STEP) == 0)
        def _():
            fetch(turn).wait()

        spread_rows(held_ref, dense, turn, step % (T // STEP) * STEP)

    for owner in range(2):

        @pl.when(core == owner)
        def _():
            for n, (i, j) in enumerate(owned_blocks(owner, last)):
                turn = i // 2
                block = dense[turn * WIDTH + j * T : turn * WIDTH + (j + 1) * T, :]
                if i == j:
                    diag = held_ref[turn, 0, size : size + 1, 0:T]
                    for m in range(1, ranks):
                        diag = diag + held_ref[turn, m, size : size + 1, 0:T]
                    block = block + jnp.where(eye, diag, 0.0)
                p = max(m for m in range(PIECES) if bounds[m] <= n)
                out_refs[p][n - bounds[p]] = block


def own_kernel(level, n_leaf, last, pos_ref, pk_ref, maps_ref, f_ref, u_hi, u_lo, hot, y_hi, y_lo):
    index_row = map_row(level, n_leaf, pos_ref, maps_ref, False)

    def emit(a, b, part):
        f_ref[pack_index(a, b)] = part

    extend_add(pk_ref, index_row, emit, last, u_hi, u_lo, hot, y_hi, y_lo)


def level_kernel(
    level, n_leaf, n_front, last, n_sib,
    pos_ref, base_ref, own_pk, maps_ref, *refs,
):
    mine_refs, theirs_refs, refs = refs[:PIECES], refs[PIECES : 2 * PIECES], refs[2 * PIECES :]
    sibs, (own_ref, next_ref, f_ref, x_ref, log_ref, tmp_ref, u_hi, u_lo, hot, y_hi, y_lo, *gathered) = (
        refs[:n_sib], refs[n_sib:],
    )
    core = pos_ref[1] & 1
    if n_sib == 1:
        sib_pk = sibs[0]
    else:
        sib_pk = gathered[0]
        sib_pk[pl.ds(core * (NPACK // 2), NPACK // 2)] = sibs[0][...]
        sib_pk[pl.ds((1 - core) * (NPACK // 2), NPACK // 2)] = sibs[1][...]
    index_row = map_row(level, n_leaf, pos_ref, maps_ref, True)
    where_is = {}
    bounds = piece_bounds(last)
    for owner in range(2):
        for n, block in enumerate(owned_blocks(owner, last)):
            p = max(m for m in range(PIECES) if bounds[m] <= n)
            where_is[block] = owner, p, n - bounds[p]

    def emit(a, b, part):
        per = TILE // T
        for r in range(per):
            for h in range(per):
                i, j = a * per + r, b * per + h
                if j > i:
                    continue
                owner, p, n = where_is[i, j]
                here, there = slice(i * T, (i + 1) * T), slice(j * T, (j + 1) * T)
                dense = jnp.where(core == owner, mine_refs[p][n], theirs_refs[p][n])
                mine, its = slice(r * T, (r + 1) * T), slice(h * T, (h + 1) * T)
                f_ref[here, there] = (base_ref[pack_index(a, b), mine, its] + part[mine, its]) + dense

    extend_add(sib_pk, index_row, emit, last, u_hi, u_lo, hot, y_hi, y_lo)
    factor_panel(f_ref, x_ref, log_ref, tmp_ref, WIDTH, NB)
    zero_above(f_ref, NB)
    rank = (pos_ref[0] & ((1 << level) - 1)) * n_front + pos_ref[1]
    write_own(own_ref, f_ref, rank * own_ref.shape[0])
    kids_log = own_pk[0][0:1, T - 1 : T] + sib_pk[0][0:1, T - 1 : T]
    log_value = kids_log + log_total(log_ref)
    if last:
        next_ref[...] = jnp.broadcast_to(log_value, next_ref.shape)
    else:

        def tail_of(i, j):
            return f_ref[SEP + i * T : SEP + (i + 1) * T, SEP + j * T : SEP + (j + 1) * T]

        write_update(next_ref, f_ref[SEP:, 0:SEP], tail_of, log_value)


def spread_rows(lists_ref, dense, turn, first):
    block_ids = iota2((8, KC), 0).astype(F32)
    column_ids = [(iota2((16, KC), 0) + 16 * j).astype(F32).astype(BF16) for j in range(T // 16)]
    one, zero = jnp.ones((16, KC), BF16), jnp.zeros((16, KC), BF16)
    blank = jnp.zeros((8, KC), F32)
    pair_of = iota2((T, T), 1) % 64 // 16
    size = lists_ref.shape[2] - 8
    for g in range(STEP // 8):
        hots, parts = [], ([], [])
        rank = (first + g * 8) // size
        at = pl.multiple_of((first + g * 8) % size, 8)
        cols = lists_ref[turn, rank, pl.ds(at, 8), 0:KC]
        vals = lists_ref[turn, rank, pl.ds(at, 8), KC:]
        block_no = jnp.floor(cols * (1.0 / T))
        within = cols - block_no * T
        for r in range(8):
            column = row_of(within, r)
            column = jnp.concatenate([column, column], axis=0).astype(BF16)
            hots.append(jnp.concatenate([jnp.where(ids == column, one, zero) for ids in column_ids], axis=0))
            val = row_of(vals, r)
            hi = val.astype(BF16).astype(F32)
            pick = block_ids == row_of(block_no, r)
            parts[0].append(jnp.where(pick, hi, 0.0))
            parts[1].append(jnp.where(pick, val - hi, 0.0))
        held = [
            jnp.concatenate(
                [
                    jnp.concatenate([part[r], blank] if side == 0 else [blank, part[r + 1]], axis=0).astype(BF16)
                    for part in parts
                    for r in range(0, 8, 2)
                ],
                axis=0,
            )
            for side in range(2)
        ]
        held = jnp.concatenate(held, axis=1)
        total = jnp.zeros((T, T), F32)
        for pair in range(4):
            streamed = jnp.concatenate([hots[2 * pair], hots[2 * pair + 1]], axis=1)
            total = jnp.where(pair_of == pair, dot_nt(streamed, held), total)
        flipped = total.T
        both = flipped[0:64] + flipped[64:128]
        for r in range(8):
            dense[pl.ds(turn * WIDTH + first + g * 8 + r, 8, stride=T), :] = both[8 * r : 8 * r + 8]


def pack_kernel(n_front, sizes, pos_ref, cols_ref, vals_ref, diag_ref, *refs):
    out_refs, line_ref = refs[:-1], refs[-1]
    line_ref[...] = jnp.zeros_like(line_ref)
    line_ref[0:1, 0 : diag_ref.shape[1]] = diag_ref[...]
    lane = iota2((8, 2 * KC), 1)
    offset = 0
    for n, (size, out_ref) in enumerate(zip(sizes, out_refs)):
        out_ref[0:size, 0:KC] = cols_ref[offset : offset + size, :].astype(F32)
        out_ref[0:size, KC:] = vals_ref[offset : offset + size, :]
        rank = (pos_ref[0] & ((2 << n) - 1)) * n_front + pos_ref[1]
        first = rank * size % T
        line = pltpu.roll(line_ref[...], (first - offset) & (2 * KC - 1), 1)
        line = jnp.broadcast_to(jnp.where((lane >= first) & (lane < first + size), line, 0.0)[0:1], (8, 2 * KC))
        out_ref[size : size + 8, :] = line
        offset += size


def params(mib):
    return pltpu.CompilerParams(vmem_limit_bytes=mib * MIB)


def vmem():
    return pl.BlockSpec(memory_space=pltpu.VMEM)


def smem():
    return pl.BlockSpec(memory_space=pltpu.SMEM)


def shape(*dims):
    return jax.ShapeDtypeStruct(dims, F32)


def cost(us):
    return pl.CostEstimate(flops=0, bytes_accessed=int(us * 3.0e6), transcendentals=0)


def call(kernel, out_shape, n_args, n_smem, scratch, us, name, mib=10):
    outs = out_shape if isinstance(out_shape, tuple) else (out_shape,)
    return pl.pallas_call(
        kernel,
        out_shape=out_shape,
        in_specs=[smem()] * n_smem + [vmem()] * (n_args - n_smem),
        out_specs=(vmem(),) * len(outs) if isinstance(out_shape, tuple) else vmem(),
        scratch_shapes=scratch,
        compiler_params=params(mib),
        cost_estimate=cost(us),
        name=name,
    )


def row_scratch():
    return pltpu.VMEM((9 * T, T), F32)


def extend_scratch():
    return [pltpu.VMEM((BND, BND), BF16)] * 2 + [pltpu.VMEM((WIDTH, BND), BF16)] * 3


def swap_front(x, mask):
    count = lax.axis_size("front")
    return lax.ppermute(x, "front", [(f, f ^ mask) for f in range(count)])


def hypercube(strip, masks):
    pieces = {0: strip}
    for mask in masks:
        for m in sorted(pieces):
            pieces[m | mask] = swap_front(pieces[m], mask)
    return [pieces[m] for m in range(len(pieces))]


def after(x, done):
    return lax.optimization_barrier((x, done))[0]


def body(leaf_bits, leaf_fronts, coupling_cols, coupling_vals, sep_diag, child_maps):
    n_front = lax.axis_size("front")
    bits = len(leaf_bits)
    n_leaf = 1 << bits
    front = lax.axis_index("front")
    leaf = lax.axis_index(leaf_bits)
    pos = jnp.stack([leaf, front]).astype(jnp.int32)
    strip = leaf_fronts[0]
    half = n_front // 2
    inner = [1 << b for b in range(half.bit_length() - 1)]
    strip_rows = WIDTH // n_front
    panel_strip = strip[:, :SEP]
    cross = swap_front(panel_strip, half)
    sizes = [WIDTH // (n_front << level) for level in range(1, bits + 1)]
    packed = call(
        functools.partial(pack_kernel, n_front, sizes),
        tuple(shape(size + 8, 2 * KC) for size in sizes), 4, 1, [pltpu.VMEM((8, 2 * KC), F32)], 1, "pack_lists",
    )(pos, coupling_cols[0, 0], coupling_vals[0, 0], sep_diag[0])
    panels = hypercube(panel_strip, inner) + hypercube(cross, inner)
    strip3 = after(strip[:, SEP:], panels[-1])
    cross3 = lax.ppermute(strip3, "front", [(f, f - half) for f in range(half, n_front)])

    lists = []
    for n, size in enumerate(sizes):
        gathered = lax.all_gather(after(packed[n], cross), leaf_bits[bits - 1 - n :] + ("front",), axis=0, tiled=False)
        if size < 8:
            rows = gathered[:, :size].reshape(WIDTH // 8, 8, 2 * KC)
            diag = gathered[:, size].reshape(WIDTH // 8, 8 // size, 2 * KC).sum(1, keepdims=True)
            gathered = jnp.concatenate([rows, jnp.pad(diag, ((0, 0), (0, 7), (0, 0)))], axis=1)
        lists.append(gathered)

    fac, inv, logs = call(
        functools.partial(head_kernel, n_front),
        (shape(SEP, SEP), shape(SEP, T), shape(8, T)), 1 + n_front, 1, [row_scratch()], 300, "head_factor",
    )(pos, *panels)
    pieces3 = hypercube(strip3, inner) + hypercube(after(cross3, inv), inner)
    piece, below = call(
        functools.partial(below_kernel, n_front),
        (shape(strip_rows, SEP), shape(BND, SEP)), 3 + n_front, 1, [pltpu.VMEM((WIDTH, SEP), F32)],
        4, "leaf_below",
    )(pos, fac, inv, *panels)
    pk = call(
        functools.partial(update_kernel, n_front), shape(NPACK, T, T), 3 + n_front, 1,
        [pltpu.VMEM((BND, BND), F32)], 3, "leaf_update",
    )(pos, below, logs, *pieces3)
    pieces = [piece]
    for level in range(1, bits + 1):
        size = sizes[level - 1]
        last = level == bits
        axis = leaf_bits[bits - level]
        if level < 3:
            sibs = [lax.ppermute(pk, axis, [(0, 1), (1, 0)])]
        else:
            part = lax.dynamic_slice_in_dim(pk, (front & 1) * (NPACK // 2), NPACK // 2, 0)
            sibs = [lax.ppermute(part, axis, [(0, 1), (1, 0)])]
        base = call(
            functools.partial(own_kernel, level, n_leaf, last), shape(pack_index(WIDTH // TILE, 0), TILE, TILE), 3, 1, extend_scratch(), 0.2, "own_child",
        )(pos, pk, child_maps)
        bounds = piece_bounds(last)
        ranks = T // (lists[level - 1].shape[1] - 8)
        mine = pl.pallas_call(
            functools.partial(coupling_kernel, last),
            out_shape=tuple(shape(end - first, T, T) for first, end in zip(bounds, bounds[1:])),
            in_specs=[smem(), pl.BlockSpec(memory_space=pltpu.HBM)],
            out_specs=(vmem(),) * PIECES,
            scratch_shapes=[
                pltpu.VMEM((NB * WIDTH, T), F32),
                pltpu.VMEM((NB, ranks) + lists[level - 1].shape[1:], F32),
                pltpu.SemaphoreType.DMA((NB,)),
            ],
            compiler_params=params(6),
            cost_estimate=cost(0.2),
            name="coupling",
        )(pos, after(lists[level - 1], pk if level < 3 else base))
        theirs = [swap_front(block, 1) for block in mine]
        if level >= 3:
            sibs.append(swap_front(after(sibs[0], base), 1))
        gathered = [pltpu.VMEM((NPACK, T, T), F32)] if len(sibs) == 2 else []
        piece, pk = call(
            functools.partial(level_kernel, level, n_leaf, n_front, last, len(sibs)),
            (shape(size, SEP), shape(8, T) if last else shape(NPACK, T, T)), 4 + 2 * PIECES + len(sibs), 1,
            [pltpu.VMEM((WIDTH, WIDTH), F32), pltpu.VMEM((SEP, T), F32), pltpu.VMEM((8, T), F32), row_scratch()]
            + extend_scratch() + gathered,
            300, "level_front", 14,
        )(pos, base, pk, child_maps, *mine, *theirs, *sibs)
        pieces.append(piece)
    return jnp.concatenate(pieces, axis=0)[None, None], pk[0, 0]


def solution(mesh):
    bits = mesh.shape["leaf"].bit_length() - 1
    leaf_bits = tuple(f"leaf{b}" for b in reversed(range(bits)))
    fine = Mesh(mesh.devices.reshape((2,) * bits + (mesh.shape["front"],)), leaf_bits + ("front",))
    placed = (
        P(leaf_bits, "front", None),
        P(leaf_bits, "front", None, None),
        P(leaf_bits, "front", None, None),
        P(leaf_bits, "front", None),
        P(),
    )
    return jax.shard_map(
        functools.partial(body, leaf_bits),
        mesh=fine,
        in_specs=placed,
        out_specs=(P(leaf_bits, "front", None, None), P()),
        check_vma=False,
    )
```

```python
import functools

import jax
import jax.numpy as jnp
from jax import lax
from jax.experimental import pallas as pl
from jax.experimental.pallas import tpu as pltpu
from jax.sharding import Mesh, PartitionSpec as P

SEP = 512
BND = 512
WIDTH = SEP + BND
KC = 128
T = 128
NB = SEP // T
PANEL = 32
PIECES = 2
STEP = 64
TILE = 256
NPACK = NB * (NB + 1) // 2
F32 = jnp.float32
BF16 = jnp.bfloat16
MIB = 1024 * 1024


def pack_index(i, j):
    return i * (i + 1) // 2 + j


def split(x):
    hi = x.astype(BF16)
    return hi, (x - hi.astype(F32)).astype(BF16)


def dot_nt(a, b):
    return lax.dot_general(a, b, (((1,), (1,)), ((), ())), preferred_element_type=F32)


def dot_nn(a, b):
    return lax.dot_general(a, b, (((1,), (0,)), ((), ())), preferred_element_type=F32)


def mm_nt(a, b):
    a_hi, a_lo = split(a)
    b_hi, b_lo = split(b)
    return dot_nt(a_hi, b_hi) + (dot_nt(a_hi, b_lo) + dot_nt(a_lo, b_hi))


def iota2(shape, dim):
    return lax.broadcasted_iota(jnp.int32, shape, dim)


def tri_sym(block):
    n = block.shape[0]
    rows, cols = iota2((n, n), 0), iota2((n, n), 1)
    low = jnp.where(cols <= rows, block, 0.0)
    strict = jnp.where(cols < rows, block, 0.0)
    return low + strict.T


def row_of(x, k):
    return jnp.broadcast_to(x[k : k + 1], (8, T))


def lane_of(x, k):
    return jnp.broadcast_to(x[:, k : k + 1], (8, T))


def tree_sum(terms):
    while len(terms) > 1:
        terms = [sum(terms[i : i + 2][1:], terms[i]) for i in range(0, len(terms), 2)]
    return terms[0]


def reciprocal(x):
    return pl.reciprocal(x, approx=True)


def eliminate_eight(groups, s, c, keep, lane, sub, tmp_ref):
    panel = groups[s]
    inside = (lane >= c) & (lane < c + 8)
    base = c * 9
    for m in range(8):
        tmp_ref[base + 8 * m : base + 8 * m + 8, :] = lane_of(panel, c + m)
    tmp_ref[base + 64 : base + 72, :] = jnp.where(inside, jnp.where(lane - c == sub, 1.0, 0.0), panel)

    def row(n):
        return jnp.broadcast_to(tmp_ref[base + n : base + n + 1, :], (8, T))

    d = {(i, m): row(8 * m + i) for m in range(8) for i in range(m + 1)}
    rows = [row(64 + k) for k in range(8)]
    upper_acc = jnp.zeros((8, T), F32)
    inv_acc = jnp.zeros((8, T), F32)
    to_p, to_q, first = {}, {}, {}
    if s + 1 < keep:
        near = [lane_of(groups[s + 1], c + k) for k in range(8)]
        following = jnp.where(inside, 0.0, groups[s + 1])

    def emit(k, line, entries, root):
        inv_row = line * root
        for m in range(k, 8):
            line = jnp.where(lane == c + m, entries[m], line)
        return jnp.where(sub == k, line * root, upper_acc), jnp.where(sub == k, inv_row, inv_acc)

    for p in range(0, 8, 2):
        q = p + 1
        a, b, e = d[p, p], d[p, q], d[q, q]
        det = a * e - b * b
        recip = reciprocal(det)
        rest = range(q + 1, 8)
        w = {i: e * d[p, i] - b * d[q, i] for i in rest}
        z = {i: a * d[q, i] - b * d[p, i] for i in rest}
        root_p = lax.rsqrt(a)
        inv_a = root_p * root_p
        ratio = b * inv_a
        schur = det * inv_a
        upper_acc, inv_acc = emit(p, rows[p], {m: d[p, m] for m in range(p, 8)}, root_p)
        line_q = {m: d[q, m] - ratio * d[p, m] for m in rest}
        line_q[q] = schur
        upper_acc, inv_acc = emit(q, rows[q] - ratio * rows[p], line_q, lax.rsqrt(schur))
        for i in rest:
            for m in range(i, 8):
                d[i, m] = d[i, m] - (w[i] * d[p, m] + z[i] * d[q, m]) * recip
        for i in rest:
            to_p[p, i], to_q[p, i] = w[i] * recip, z[i] * recip
            rows[i] = rows[i] - (to_p[p, i] * rows[p] + to_q[p, i] * rows[q])
        if s + 1 < keep:
            near_p, near_q = (e * near[p] - b * near[q]) * recip, (a * near[q] - b * near[p]) * recip
            following = following - (near_p * rows[p] + near_q * rows[q])
            for m in rest:
                near[m] = near[m] - (near_p * d[p, m] + near_q * d[q, m])
        first[p] = (e * rows[p] - b * rows[q]) * recip
        first[q] = (a * rows[q] - b * rows[p]) * recip
    if s + 1 < keep:
        groups[s + 1] = following
    if s + 2 < keep:
        sol = [None] * 8
        for p in (6, 4, 2, 0):
            rest = range(p + 2, 8)
            sol[p], sol[p + 1] = first[p], first[p + 1]
            if p < 6:
                sol[p] = sol[p] - tree_sum([to_p[p, m] * sol[m] for m in rest])
                sol[p + 1] = sol[p + 1] - tree_sum([to_q[p, m] * sol[m] for m in rest])
        for g in range(s + 2, keep):
            old = groups[g]
            groups[g] = jnp.where(inside, 0.0, old) - tree_sum([lane_of(old, c + k) * sol[k] for k in range(8)])
    return jnp.where(lane >= c + sub, upper_acc, 0.0), jnp.where(lane <= c + sub, inv_acc, 0.0)


def chol_and_inverse(sym, tmp_ref):
    lane, sub = iota2((8, T), 1), iota2((8, T), 0)
    per = PANEL // 8
    diag = jnp.sum(jnp.where(iota2((T, T), 0) == iota2((T, T), 1), sym, 0.0), axis=0, keepdims=True)
    scale = jnp.broadcast_to(lax.rsqrt(diag), (T, T))
    sym = (sym * scale) * scale.T
    groups = [sym[8 * g : 8 * g + 8] for g in range(T // 8)]
    upper_rows, inv_rows = [], []
    for p in range(T // PANEL):
        for s in range(p * per, (p + 1) * per):
            upper, inv = eliminate_eight(groups, s, 8 * s, (p + 1) * per, lane, sub, tmp_ref)
            upper_rows.append(upper)
            inv_rows.append(inv)
        end = (p + 1) * PANEL
        if end < T:
            both = jnp.concatenate(
                [jnp.where(lane < end, inv_rows[s], upper_rows[s]) for s in range(p * per, (p + 1) * per)], axis=0
            )
            hi, lo = split(both)
            product = lax.dot_general(
                jnp.concatenate([hi, lo, hi], axis=0), jnp.concatenate([hi, hi, lo], axis=0),
                (((0,), (0,)), ((), ())), preferred_element_type=F32,
            )
            done = (lane >= p * PANEL) & (lane < end)
            for g in range((p + 1) * per, T // 8):
                groups[g] = jnp.where(done, 0.0, groups[g]) - product[8 * g : 8 * g + 8]
    return jnp.concatenate(upper_rows, axis=0) * (diag * scale[0:1]), jnp.concatenate(inv_rows, axis=0) * scale


def factor_panel(f_ref, x_ref, log_ref, tmp_ref, rows, blocks):
    width = blocks * T
    log_ref[...] = jnp.zeros_like(log_ref)

    @pl.loop(0, blocks)
    def _(j):
        at = pl.multiple_of(j * T, T)
        upper, inv = chol_and_inverse(tri_sym(f_ref[pl.ds(at, T), pl.ds(at, T)]), tmp_ref)
        f_ref[pl.ds(at, T), pl.ds(at, T)] = upper.T
        x_ref[pl.ds(at, T), :] = inv
        eye = iota2((T, T), 0) == iota2((T, T), 1)
        diag = jnp.sum(jnp.where(eye, upper, 0.0), axis=0, keepdims=True)
        log_ref[0:1, :] += jnp.log(diag)
        for k in range(blocks):
            first = (k + 1) * T
            if first >= rows:
                continue

            @pl.when(j == k)
            def _():
                below = mm_nt(f_ref[first:rows, k * T : first], inv)
                f_ref[first:rows, k * T : first] = below
                if first < width:
                    f_ref[first:rows, first:width] -= mm_nt(below, below[: width - first])


def zero_above(f_ref, blocks):
    for i in range(blocks - 1):
        f_ref[i * T : (i + 1) * T, (i + 1) * T : blocks * T] = jnp.zeros((T, (blocks - 1 - i) * T), F32)


def log_total(log_ref):
    return 2.0 * jnp.sum(log_ref[0:1, :], axis=1, keepdims=True)


def write_own(out_ref, f_ref, start):
    size = out_ref.shape[0]
    if size % 8 == 0:
        out_ref[...] = f_ref[pl.ds(pl.multiple_of(start, 8), size), 0:SEP]
    else:
        base = pl.multiple_of(start // 8 * 8, 8)
        block = f_ref[pl.ds(base, 8), 0:SEP]
        offset = start - base
        piece = block[0:size]
        for shift in range(size, 8, size):
            piece = jnp.where(offset == shift, block[shift : shift + size], piece)
        out_ref[...] = piece


def write_update(pk_ref, below, tail_of, log_value):
    hi, lo = split(below)
    rows, cols = iota2((T, T), 0), iota2((T, T), 1)
    for i in range(NB):
        here = slice(i * T, (i + 1) * T)
        upto = slice(0, (i + 1) * T)
        prod = dot_nt(hi[here], hi[upto]) + (dot_nt(hi[here], lo[upto]) + dot_nt(lo[here], hi[upto]))
        for j in range(i + 1):
            block = tail_of(i, j) - prod[:, j * T : (j + 1) * T]
            if i == 0:
                block = jnp.where((rows == 0) & (cols == T - 1), log_value, block)
            pk_ref[pack_index(i, j)] = block


def place(pieces, work, front, want_tail):
    count = len(pieces)
    half = count // 2
    size = pieces[0].shape[0]
    for m, piece in enumerate(pieces):
        source = front ^ m

        @pl.when((source >= half) == want_tail)
        def _():
            at = pl.multiple_of((source & (half - 1)) * size, 8)
            work[pl.ds(at, size), :] = piece[...]


def head_kernel(n, pos_ref, *refs):
    pieces, (fac_ref, x_ref, log_ref, tmp_ref) = refs[:n], refs[n:]
    place(pieces, fac_ref, pos_ref[1], False)
    factor_panel(fac_ref, x_ref, log_ref, tmp_ref, SEP, NB)
    zero_above(fac_ref, NB)


def below_kernel(n, pos_ref, fac, inv, *refs):
    pieces, (own_ref, below_ref, stack) = refs[:n], refs[n:]
    front = pos_ref[1]
    place(pieces, below_ref, front, True)
    for j in range(NB):
        here = slice(j * T, (j + 1) * T)
        solved = mm_nt(below_ref[:, here], inv[here, :])
        below_ref[:, here] = solved
        if j + 1 < NB:
            rest = slice((j + 1) * T, SEP)
            below_ref[:, rest] -= mm_nt(solved, fac[rest, here])
    stack[0:SEP, :] = fac[...]
    stack[SEP:, :] = below_ref[...]
    write_own(own_ref, stack, front * own_ref.shape[0])


def update_kernel(n, pos_ref, below_ref, log_ref, *refs):
    pieces, (pk_ref, tail_ref) = refs[:n], refs[n:]
    place(pieces, tail_ref, pos_ref[1], True)

    def tail_of(i, j):
        return tail_ref[i * T : (i + 1) * T, j * T : (j + 1) * T]

    write_update(pk_ref, below_ref[...], tail_of, log_total(log_ref))


def expand(pk_ref, u_hi, u_lo):
    rows, cols = iota2((T, T), 0), iota2((T, T), 1)
    for i in range(NB):
        for j in range(i + 1):
            block = pk_ref[pack_index(i, j)]
            if i == j:
                low = jnp.where(cols <= rows, block, 0.0)
                block = low + jnp.where(cols < rows, block, 0.0).T
            hi, lo = split(block)
            u_hi[i * T : (i + 1) * T, j * T : (j + 1) * T] = hi
            u_lo[i * T : (i + 1) * T, j * T : (j + 1) * T] = lo
            if i != j:
                hi, lo = split(block.T)
                u_hi[j * T : (j + 1) * T, i * T : (i + 1) * T] = hi
                u_lo[j * T : (j + 1) * T, i * T : (i + 1) * T] = lo


def extend_add(pk_ref, index_row, emit, last, u_hi, u_lo, hot, y_hi, y_lo):
    expand(pk_ref, u_hi, u_lo)

    @pl.loop(0, WIDTH // TILE)
    def _(tile):
        at = pl.multiple_of(tile * TILE, TILE)
        ids = iota2((TILE, BND), 0) + at
        match = jnp.where(ids == index_row, 1.0, 0.0).astype(BF16)
        hot[pl.ds(at, TILE), :] = match
        y_hi[pl.ds(at, TILE), :] = dot_nn(match, u_hi[...]).astype(BF16)
        y_lo[pl.ds(at, TILE), :] = dot_nn(match, u_lo[...]).astype(BF16)

    for a in range(WIDTH // TILE):
        here = slice(a * TILE, (a + 1) * TILE)
        for b in range(a + 1):
            if last and b * TILE >= SEP:
                continue
            there = slice(b * TILE, (b + 1) * TILE)
            part = dot_nt(y_hi[here, :], hot[there, :]) + dot_nt(y_lo[here, :], hot[there, :])
            emit(a, b, part)


def map_row(level, n_leaf, pos_ref, maps_ref, sibling):
    base = 2 * n_leaf - 2 * (n_leaf >> (level - 1))
    own = pos_ref[0] >> (level - 1)
    number = base + (own ^ 1 if sibling else own)
    return maps_ref[pl.ds(number, 1), :]


def owned_blocks(core, last):
    rows = [2 * turn + (turn + core) % 2 for turn in range(WIDTH // T // 2)]
    return [(i, j) for i in rows for j in range(min(i + 1, NB if last else 2 * NB))]


def piece_bounds(last):
    total = len(owned_blocks(0, last))
    return [total * n // PIECES for n in range(PIECES + 1)]


def coupling_kernel(last, pos_ref, lists_ref, *refs):
    out_refs, (dense, held_ref, sems) = refs[:-3], refs[-3:]
    bounds = piece_bounds(last)
    core = pos_ref[1] & 1
    size = lists_ref.shape[1] - 8
    ranks = T // size
    eye = iota2((T, T), 0) == iota2((T, T), 1)
    def fetch(turn):
        i = 2 * turn + ((turn + core) & 1)
        return pltpu.make_async_copy(lists_ref.at[pl.ds(i * ranks, ranks)], held_ref.at[turn], sems.at[turn])

    for turn in range(NB):
        fetch(turn).start()

    @pl.loop(0, NB * T // STEP)
    def _(step):
        turn = step // (T // STEP)

        @pl.when(step % (T // STEP) == 0)
        def _():
            fetch(turn).wait()

        spread_rows(held_ref, dense, turn, step % (T // STEP) * STEP)

    for owner in range(2):

        @pl.when(core == owner)
        def _():
            for n, (i, j) in enumerate(owned_blocks(owner, last)):
                turn = i // 2
                block = dense[turn * WIDTH + j * T : turn * WIDTH + (j + 1) * T, :]
                if i == j:
                    diag = held_ref[turn, 0, size : size + 1, 0:T]
                    for m in range(1, ranks):
                        diag = diag + held_ref[turn, m, size : size + 1, 0:T]
                    block = block + jnp.where(eye, diag, 0.0)
                p = max(m for m in range(PIECES) if bounds[m] <= n)
                out_refs[p][n - bounds[p]] = block


def own_kernel(level, n_leaf, last, pos_ref, pk_ref, maps_ref, f_ref, u_hi, u_lo, hot, y_hi, y_lo):
    index_row = map_row(level, n_leaf, pos_ref, maps_ref, False)

    def emit(a, b, part):
        f_ref[pack_index(a, b)] = part

    extend_add(pk_ref, index_row, emit, last, u_hi, u_lo, hot, y_hi, y_lo)


def level_kernel(
    level, n_leaf, n_front, last, n_sib,
    pos_ref, base_ref, own_pk, maps_ref, *refs,
):
    mine_refs, theirs_refs, refs = refs[:PIECES], refs[PIECES : 2 * PIECES], refs[2 * PIECES :]
    sibs, (own_ref, next_ref, f_ref, x_ref, log_ref, tmp_ref, u_hi, u_lo, hot, y_hi, y_lo, *gathered) = (
        refs[:n_sib], refs[n_sib:],
    )
    core = pos_ref[1] & 1
    if n_sib == 1:
        sib_pk = sibs[0]
    else:
        sib_pk = gathered[0]
        sib_pk[pl.ds(core * (NPACK // 2), NPACK // 2)] = sibs[0][...]
        sib_pk[pl.ds((1 - core) * (NPACK // 2), NPACK // 2)] = sibs[1][...]
    index_row = map_row(level, n_leaf, pos_ref, maps_ref, True)
    where_is = {}
    bounds = piece_bounds(last)
    for owner in range(2):
        for n, block in enumerate(owned_blocks(owner, last)):
            p = max(m for m in range(PIECES) if bounds[m] <= n)
            where_is[block] = owner, p, n - bounds[p]

    def emit(a, b, part):
        per = TILE // T
        for r in range(per):
            for h in range(per):
                i, j = a * per + r, b * per + h
                if j > i:
                    continue
                owner, p, n = where_is[i, j]
                here, there = slice(i * T, (i + 1) * T), slice(j * T, (j + 1) * T)
                dense = jnp.where(core == owner, mine_refs[p][n], theirs_refs[p][n])
                mine, its = slice(r * T, (r + 1) * T), slice(h * T, (h + 1) * T)
                f_ref[here, there] = (base_ref[pack_index(a, b), mine, its] + part[mine, its]) + dense

    extend_add(sib_pk, index_row, emit, last, u_hi, u_lo, hot, y_hi, y_lo)
    factor_panel(f_ref, x_ref, log_ref, tmp_ref, WIDTH, NB)
    zero_above(f_ref, NB)
    rank = (pos_ref[0] & ((1 << level) - 1)) * n_front + pos_ref[1]
    write_own(own_ref, f_ref, rank * own_ref.shape[0])
    kids_log = own_pk[0][0:1, T - 1 : T] + sib_pk[0][0:1, T - 1 : T]
    log_value = kids_log + log_total(log_ref)
    if last:
        next_ref[...] = jnp.broadcast_to(log_value, next_ref.shape)
    else:

        def tail_of(i, j):
            return f_ref[SEP + i * T : SEP + (i + 1) * T, SEP + j * T : SEP + (j + 1) * T]

        write_update(next_ref, f_ref[SEP:, 0:SEP], tail_of, log_value)


def spread_rows(lists_ref, dense, turn, first):
    block_ids = iota2((8, KC), 0).astype(F32)
    column_ids = [(iota2((16, KC), 0) + 16 * j).astype(F32).astype(BF16) for j in range(T // 16)]
    one, zero = jnp.ones((16, KC), BF16), jnp.zeros((16, KC), BF16)
    blank = jnp.zeros((8, KC), F32)
    pair_of = iota2((T, T), 1) % 64 // 16
    size = lists_ref.shape[2] - 8
    for g in range(STEP // 8):
        hots, parts = [], ([], [])
        rank = (first + g * 8) // size
        at = pl.multiple_of((first + g * 8) % size, 8)
        cols = lists_ref[turn, rank, pl.ds(at, 8), 0:KC]
        vals = lists_ref[turn, rank, pl.ds(at, 8), KC:]
        block_no = jnp.floor(cols * (1.0 / T))
        within = cols - block_no * T
        for r in range(8):
            column = row_of(within, r)
            column = jnp.concatenate([column, column], axis=0).astype(BF16)
            hots.append(jnp.concatenate([jnp.where(ids == column, one, zero) for ids in column_ids], axis=0))
            val = row_of(vals, r)
            hi = val.astype(BF16).astype(F32)
            pick = block_ids == row_of(block_no, r)
            parts[0].append(jnp.where(pick, hi, 0.0))
            parts[1].append(jnp.where(pick, val - hi, 0.0))
        held = [
            jnp.concatenate(
                [
                    jnp.concatenate([part[r], blank] if side == 0 else [blank, part[r + 1]], axis=0).astype(BF16)
                    for part in parts
                    for r in range(0, 8, 2)
                ],
                axis=0,
            )
            for side in range(2)
        ]
        held = jnp.concatenate(held, axis=1)
        total = jnp.zeros((T, T), F32)
        for pair in range(4):
            streamed = jnp.concatenate([hots[2 * pair], hots[2 * pair + 1]], axis=1)
            total = jnp.where(pair_of == pair, dot_nt(streamed, held), total)
        flipped = total.T
        both = flipped[0:64] + flipped[64:128]
        for r in range(8):
            dense[pl.ds(turn * WIDTH + first + g * 8 + r, 8, stride=T), :] = both[8 * r : 8 * r + 8]


def pack_kernel(n_front, sizes, pos_ref, cols_ref, vals_ref, diag_ref, *refs):
    out_refs, line_ref = refs[:-1], refs[-1]
    line_ref[...] = jnp.zeros_like(line_ref)
    line_ref[0:1, 0 : diag_ref.shape[1]] = diag_ref[...]
    lane = iota2((8, 2 * KC), 1)
    offset = 0
    for n, (size, out_ref) in enumerate(zip(sizes, out_refs)):
        out_ref[0:size, 0:KC] = cols_ref[offset : offset + size, :].astype(F32)
        out_ref[0:size, KC:] = vals_ref[offset : offset + size, :]
        rank = (pos_ref[0] & ((2 << n) - 1)) * n_front + pos_ref[1]
        first = rank * size % T
        line = pltpu.roll(line_ref[...], (first - offset) & (2 * KC - 1), 1)
        line = jnp.broadcast_to(jnp.where((lane >= first) & (lane < first + size), line, 0.0)[0:1], (8, 2 * KC))
        out_ref[size : size + 8, :] = line
        offset += size


def params(mib):
    return pltpu.CompilerParams(vmem_limit_bytes=mib * MIB)


def vmem():
    return pl.BlockSpec(memory_space=pltpu.VMEM)


def smem():
    return pl.BlockSpec(memory_space=pltpu.SMEM)


def shape(*dims):
    return jax.ShapeDtypeStruct(dims, F32)


def cost(us):
    return pl.CostEstimate(flops=0, bytes_accessed=int(us * 3.0e6), transcendentals=0)


def call(kernel, out_shape, n_args, n_smem, scratch, us, name, mib=10):
    outs = out_shape if isinstance(out_shape, tuple) else (out_shape,)
    return pl.pallas_call(
        kernel,
        out_shape=out_shape,
        in_specs=[smem()] * n_smem + [vmem()] * (n_args - n_smem),
        out_specs=(vmem(),) * len(outs) if isinstance(out_shape, tuple) else vmem(),
        scratch_shapes=scratch,
        compiler_params=params(mib),
        cost_estimate=cost(us),
        name=name,
    )


def row_scratch():
    return pltpu.VMEM((9 * T, T), F32)


def extend_scratch():
    return [pltpu.VMEM((BND, BND), BF16)] * 2 + [pltpu.VMEM((WIDTH, BND), BF16)] * 3


def swap_front(x, mask):
    count = lax.axis_size("front")
    return lax.ppermute(x, "front", [(f, f ^ mask) for f in range(count)])


def hypercube(strip, masks):
    pieces = {0: strip}
    for mask in masks:
        for m in sorted(pieces):
            pieces[m | mask] = swap_front(pieces[m], mask)
    return [pieces[m] for m in range(len(pieces))]


def after(x, done):
    return lax.optimization_barrier((x, done))[0]


def body(leaf_bits, leaf_fronts, coupling_cols, coupling_vals, sep_diag, child_maps):
    n_front = lax.axis_size("front")
    bits = len(leaf_bits)
    n_leaf = 1 << bits
    front = lax.axis_index("front")
    leaf = lax.axis_index(leaf_bits)
    pos = jnp.stack([leaf, front]).astype(jnp.int32)
    strip = leaf_fronts[0]
    half = n_front // 2
    inner = [1 << b for b in range(half.bit_length() - 1)]
    strip_rows = WIDTH // n_front
    panel_strip = strip[:, :SEP]
    cross = swap_front(panel_strip, half)
    sizes = [WIDTH // (n_front << level) for level in range(1, bits + 1)]
    packed = call(
        functools.partial(pack_kernel, n_front, sizes),
        tuple(shape(size + 8, 2 * KC) for size in sizes), 4, 1, [pltpu.VMEM((8, 2 * KC), F32)], 1, "pack_lists",
    )(pos, coupling_cols[0, 0], coupling_vals[0, 0], sep_diag[0])
    panels = hypercube(panel_strip, inner) + hypercube(after(cross, packed[0]), inner)
    strip3 = after(strip[:, SEP:], panels[-1])
    cross3 = lax.ppermute(strip3, "front", [(f, f - half) for f in range(half, n_front)])

    lists = []
    for n, size in enumerate(sizes):
        gathered = lax.all_gather(packed[n], leaf_bits[bits - 1 - n :] + ("front",), axis=0, tiled=False)
        if size < 8:
            rows = gathered[:, :size].reshape(WIDTH // 8, 8, 2 * KC)
            diag = gathered[:, size].reshape(WIDTH // 8, 8 // size, 2 * KC).sum(1, keepdims=True)
            gathered = jnp.concatenate([rows, jnp.pad(diag, ((0, 0), (0, 7), (0, 0)))], axis=1)
        lists.append(gathered)

    fac, inv, logs = call(
        functools.partial(head_kernel, n_front),
        (shape(SEP, SEP), shape(SEP, T), shape(8, T)), 1 + n_front, 1, [row_scratch()], 300, "head_factor",
    )(pos, *panels)
    pieces3 = hypercube(strip3, inner) + hypercube(after(cross3, inv), inner)
    piece, below = call(
        functools.partial(below_kernel, n_front),
        (shape(strip_rows, SEP), shape(BND, SEP)), 3 + n_front, 1, [pltpu.VMEM((WIDTH, SEP), F32)],
        4, "leaf_below",
    )(pos, fac, inv, *panels)
    pk = call(
        functools.partial(update_kernel, n_front), shape(NPACK, T, T), 3 + n_front, 1,
        [pltpu.VMEM((BND, BND), F32)], 3, "leaf_update",
    )(pos, below, logs, *pieces3)
    pieces = [piece]
    for level in range(1, bits + 1):
        size = sizes[level - 1]
        last = level == bits
        axis = leaf_bits[bits - level]
        if level < 3:
            sibs = [lax.ppermute(pk, axis, [(0, 1), (1, 0)])]
        else:
            part = lax.dynamic_slice_in_dim(pk, (front & 1) * (NPACK // 2), NPACK // 2, 0)
            sibs = [lax.ppermute(part, axis, [(0, 1), (1, 0)])]
        base = call(
            functools.partial(own_kernel, level, n_leaf, last), shape(pack_index(WIDTH // TILE, 0), TILE, TILE), 3, 1, extend_scratch(), 0.2, "own_child",
        )(pos, pk, child_maps)
        bounds = piece_bounds(last)
        ranks = T // (lists[level - 1].shape[1] - 8)
        mine = pl.pallas_call(
            functools.partial(coupling_kernel, last),
            out_shape=tuple(shape(end - first, T, T) for first, end in zip(bounds, bounds[1:])),
            in_specs=[smem(), pl.BlockSpec(memory_space=pltpu.HBM)],
            out_specs=(vmem(),) * PIECES,
            scratch_shapes=[
                pltpu.VMEM((NB * WIDTH, T), F32),
                pltpu.VMEM((NB, ranks) + lists[level - 1].shape[1:], F32),
                pltpu.SemaphoreType.DMA((NB,)),
            ],
            compiler_params=params(6),
            cost_estimate=cost(0.2),
            name="coupling",
        )(pos, after(lists[level - 1], pk if level < 3 else base))
        theirs = [swap_front(block, 1) for block in mine]
        if level >= 3:
            sibs.append(swap_front(after(sibs[0], base), 1))
        gathered = [pltpu.VMEM((NPACK, T, T), F32)] if len(sibs) == 2 else []
        piece, pk = call(
            functools.partial(level_kernel, level, n_leaf, n_front, last, len(sibs)),
            (shape(size, SEP), shape(8, T) if last else shape(NPACK, T, T)), 4 + 2 * PIECES + len(sibs), 1,
            [pltpu.VMEM((WIDTH, WIDTH), F32), pltpu.VMEM((SEP, T), F32), pltpu.VMEM((8, T), F32), row_scratch()]
            + extend_scratch() + gathered,
            300, "level_front", 14,
        )(pos, base, pk, child_maps, *mine, *theirs, *sibs)
        pieces.append(piece)
    return jnp.concatenate(pieces, axis=0)[None, None], pk[0, 0]


def solution(mesh):
    bits = mesh.shape["leaf"].bit_length() - 1
    leaf_bits = tuple(f"leaf{b}" for b in reversed(range(bits)))
    fine = Mesh(mesh.devices.reshape((2,) * bits + (mesh.shape["front"],)), leaf_bits + ("front",))
    placed = (
        P(leaf_bits, "front", None),
        P(leaf_bits, "front", None, None),
        P(leaf_bits, "front", None, None),
        P(leaf_bits, "front", None),
        P(),
    )
    return jax.shard_map(
        functools.partial(body, leaf_bits),
        mesh=fine,
        in_specs=placed,
        out_specs=(P(leaf_bits, "front", None, None), P()),
        check_vma=False,
    )
```
